256 devices in a mesh: gz: 8 (over x, core), tile: 32 (over z, y).
Axes of the slice: x: 4, y: 4, z: 8, core: 2. Of those that a mesh axis runs over, the one named last changes fastest.
Arguments:
- patches: bfloat16 [8, 512, 25600], P('gz', 'tile'), may hold values from -450 to 450, as said below
- prior_patches: bfloat16 [512, 25600], P('tile'), may hold values from -450 to 450, as said below
- blocks: bfloat16 [8, 1024, 25600], P('gz', 'tile'), may hold values from -450 to 450, as said below
- dest: int32 [8, 1024, 1], P('gz', 'tile'), may hold values from 0 to 31; in each aligned block of 32 rows (0 to 31, 32 to 63, ..., all dimensions but the last counted through in order) at most 2 rows name the same one
- target: int32 [8, 1024], P('gz', 'tile'), may hold values from 0 to 15
- flows: float32 [8, 2, 256, 256], P('gz', None, 'tile'), may hold values from -8 to 8
- valid: int32 [8, 256, 256], P('gz', 'tile'), may hold values 0 or 1
- stiffness: float32 [8, 256, 256], P('gz', 'tile'), may hold values from 0.2 to 1
Outputs:
- corr_maps: bfloat16 [8, 1024, 25600], P('gz', 'tile')
- mesh_nodes: float32 [8, 2, 256, 256], P('gz', None, 'tile')
The draws below stay inside these ranges and needn't reach their ends.
Inputs may be any that keep to these rules, and one draw needn't show every extreme that they name: `patches`: pixel intensities. `prior_patches`: pixel intensities. `blocks`: pixel intensities. `dest`: among the 32 blocks of one device, at most 2 name the same tile, and on every device some tile is named by exactly 2 of them.
All inputs are finite; a program needn't handle non-finite values. No bound on the sum of `valid` on one device may be relied on, other than what follows from the above.
Results may differ from the reference program's by a relative error of at most 0.015.
Values may be sent and summed in bfloat16 or wider, within the bound.
A program may use at most 128 MiB of HBM per device.

```python
import math
import jax
import jax.numpy as jnp
import numpy as np
from jax import lax

P_SIZE = 160
PIX = 25600
NP = 16
CAP = 2
NB = 32
RX = 8
RY = 256
ITERS = 64
SECTIONS = 8
PATCHES = 512
BLOCKS = 1024
ROWS = 256
N_TILE = 32


def image_rows(key, count, log_top):
    subkeys = jax.random.split(key, 5)
    normal_part = jnp.clip(jax.random.normal(subkeys[0], (count, P_SIZE, P_SIZE), jnp.float32), -4.0, 4.0)
    base_draw = normal_part
    row_scale = jnp.exp(jax.random.uniform(subkeys[2], (count, P_SIZE, 1), jnp.float32, 0.0, log_top))
    col_scale = jnp.exp(jax.random.uniform(subkeys[3], (count, 1, P_SIZE), jnp.float32, 0.0, log_top))
    offset = jax.random.uniform(subkeys[4], (count, 1, 1), jnp.float32, -50.0, 50.0)
    values = base_draw * row_scale * col_scale + offset
    return jnp.clip(values, -450.0, 450.0).reshape(count, P_SIZE * P_SIZE)


def draw_patches(key, part):
    key = jax.random.fold_in(key, 11)
    values = image_rows(key, SECTIONS * PATCHES, 2.3)
    return values.reshape(SECTIONS, PATCHES, PIX).astype(jnp.bfloat16)


def draw_prior_patches(key, part):
    key = jax.random.fold_in(key, 23)
    values = image_rows(key, PATCHES, 2.3)
    return values.astype(jnp.bfloat16)


def draw_blocks(key, part):
    key = jax.random.fold_in(key, 37)
    values = image_rows(key, SECTIONS * BLOCKS, 2.3)
    return values.reshape(SECTIONS, BLOCKS, PIX).astype(jnp.bfloat16)


def place_ends(entries, stream_key, least, top_value):
    index_at = [jax.random.randint(jax.random.fold_in(stream_key, axis), (), 0, length) for axis, length in enumerate(entries.shape)]
    longest = entries.shape.index(max(entries.shape))
    next_to = index_at[:longest] + [(index_at[longest] + 1) % entries.shape[longest]] + index_at[longest + 1:]
    return entries.at[tuple(index_at)].set(least).at[tuple(next_to)].set(top_value)


def steps_of(own_key, shape, shards, smallest, high):
    loudness, own = 1.0, jax.random.fold_in(own_key, 6)
    for dim, shards_of in shards:
        steps = jnp.exp(jax.random.uniform(jax.random.fold_in(own, dim), (shards_of,), jnp.float32, smallest / len(shards), high / len(shards)))
        loudness = loudness * jnp.repeat(steps, shape[dim] // shards_of).reshape([-1 if axis == dim else 1 for axis in range(len(shape))])
    return loudness


def shared_out(stream_key, own, number, rows, number_of, top, most, slope):
    order = jax.random.permutation(stream_key, number_of)
    crowded, common = portions_of(number_of, rows * top, most, slope, True), portions_of(number_of, rows * top, most, slope, False)
    places = jnp.arange(number_of)

    def named(sizes, rotation):
        used = int((sizes > 0).sum())
        fixed = max(1, used // 4)
        shifted = fixed + (places - fixed + rotation * (used - fixed)) % max(1, number_of - fixed)
        return jnp.zeros((number_of,), jnp.int32).at[order[jnp.where(places < fixed, places, shifted)]].set(jnp.asarray(sizes, jnp.int32))

    sizes = jnp.where(number % 4 == 0, named(crowded, number // 4), named(common, number - number // 4 - 1))
    mixed = jax.random.permutation(jax.random.fold_in(own, 3), number_of)
    giver, sink = mixed[0:number_of // 2 * 2:2], mixed[1:number_of // 2 * 2:2]
    margin = jnp.minimum(sizes[giver] - 1, most - sizes[sink]) // 2
    margin = jnp.where((giver == order[0]) | (sink == order[0]) | (sizes[sink] == 0), 0, jnp.maximum(margin, 0))
    shifted = jax.random.randint(jax.random.fold_in(own, 4), (number_of // 2,), 0, 1 << 20) % (margin + 1)
    sizes = sizes.at[giver].add(-shifted).at[sink].add(shifted)
    labels = jnp.searchsorted(jnp.cumsum(sizes), jnp.arange(rows * top), side="right").astype(jnp.int32)
    grid = labels.reshape(top, rows).T
    grid = grid[jax.random.permutation(jax.random.fold_in(own, 1), rows)]
    rotation = jax.random.randint(jax.random.fold_in(own, 2), (rows, 1), 0, top)
    return jnp.take_along_axis(grid, (jnp.arange(top)[None, :] + rotation) % top, axis=1)


def portions_of(amount, total, reach, slope, full):
    portions = [(1 << 20) // math.isqrt(grade ** slope) + 1 for grade in range(1, amount + 1)]
    largest = reach if full else min(reach, max(-(-total // amount), total * portions[0] // sum(portions)))
    least = 1 if total - largest >= amount - 1 else 0
    counts, surplus = [largest] + [least] * (amount - 1), total - largest - least * (amount - 1)
    while surplus > 0:
        candidates = [i for i in range(1, amount) if counts[i] < largest] or [i for i in range(1, amount) if counts[i] < reach]
        pool, budget = sum([portions[i] for i in candidates]), surplus
        for i in candidates:
            extra = min(reach - counts[i], max(1, budget * portions[i] // pool), surplus)
            counts[i] = counts[i] + extra
            surplus = surplus - extra
    return np.array(counts)


def noise(key, dims, width, reach, shards=(), kind=jnp.bfloat16):
    entries = width * jax.random.normal(key, dims, jnp.float32)
    if shards:
        entries = entries * steps_of(key, dims, shards, -0.22, 0.18)
    return jnp.clip(entries, -reach, reach).astype(kind)


def setup_inputs(seed: int = 0) -> dict:
    key_list = jax.random.split(jax.random.key(seed), 9)
    patches = draw_patches(jax.random.fold_in(key_list[8], 71), 0)
    prior_patches = draw_prior_patches(jax.random.fold_in(key_list[8], 71), 0)
    blocks = draw_blocks(jax.random.fold_in(key_list[8], 71), 0)
    dest_keys = jax.random.split(jax.random.fold_in(key_list[3], 1), SECTIONS * BLOCKS // NB)
    dest_turns = jax.random.permutation(jax.random.fold_in(key_list[3], 3), SECTIONS * BLOCKS // NB)
    dest = jax.vmap(lambda own, number: shared_out(jax.random.fold_in(key_list[3], 2), own, number, NB, N_TILE, 1, CAP, 2))(dest_keys, dest_turns).reshape((SECTIONS, BLOCKS, 1))
    target = place_ends(jax.random.randint(key_list[4], (SECTIONS, BLOCKS), 0, NP), jax.random.fold_in(key_list[4], 1), 0, NP - 1).astype(jnp.int32)
    flows = noise(key_list[5], (SECTIONS, 2, ROWS, RY), 2.0, 8.0, ((0, 8), (2, 32)), jnp.float32)
    valid = place_ends((jax.random.randint(key_list[6], (SECTIONS, ROWS, RY), 0, 4) < 3).astype(jnp.int32), jax.random.fold_in(key_list[6], 1), 0, 1)
    stiffness = jnp.clip(jnp.exp(math.log(1.0) - 1.609438 * jax.random.uniform(key_list[7], (SECTIONS, ROWS, RY), jnp.float32) ** steps_of(key_list[7], (SECTIONS, ROWS, RY), ((0, 8), (1, 32)), -0.2, 0.2)), 0.2, 1.0)
    return dict(patches=patches, prior_patches=prior_patches, blocks=blocks, dest=dest, target=target, flows=flows, valid=valid, stiffness=stiffness)


def dft_tables(edge_len):
    positions = jnp.arange(edge_len, dtype=jnp.int32)
    phase_idx = positions[:, None] * positions[None, :] % edge_len
    angles = phase_idx.astype(jnp.float32) * (2.0 * jnp.pi / edge_len)
    return (jnp.cos(angles).astype(jnp.bfloat16), jnp.sin(angles).astype(jnp.bfloat16))

def right_mul(pixels, matrix_t):
    return jnp.einsum('npq,qk->npk', pixels.astype(jnp.float32), matrix_t.astype(jnp.float32))

def left_mul(matrix_t, pixels):
    return jnp.einsum('jp,npk->njk', matrix_t.astype(jnp.float32), pixels.astype(jnp.float32))

def normalized(pixel_rows):
    values = pixel_rows.astype(jnp.float32)
    centred = values - lax.optimization_barrier(jnp.mean(values, axis=-1, keepdims=True))
    spread = lax.optimization_barrier(jnp.mean(centred * centred, axis=-1, keepdims=True))
    return (centred * lax.rsqrt(spread + 1e-05)).astype(jnp.bfloat16)

def spectrum(pixel_rows, cos_t, sin_t):
    edge_len = cos_t.shape[0]
    pixels = normalized(pixel_rows).reshape(pixel_rows.shape[0], edge_len, edge_len)
    first_re = right_mul(pixels, cos_t).astype(jnp.bfloat16)
    first_im = right_mul(pixels, sin_t).astype(jnp.bfloat16)
    spec_re = (left_mul(cos_t, first_re) - left_mul(sin_t, first_im)).astype(jnp.bfloat16)
    spec_im = (left_mul(sin_t, first_re) + left_mul(cos_t, first_im)).astype(jnp.bfloat16)
    return (spec_re, spec_im)

def correlate(spec_a, spec_b, cos_t, sin_t):
    edge_len = cos_t.shape[0]
    a_re = spec_a[0].astype(jnp.float32)
    a_im = spec_a[1].astype(jnp.float32)
    b_re = spec_b[0].astype(jnp.float32)
    b_im = spec_b[1].astype(jnp.float32)
    cross_re = (a_re * b_re + a_im * b_im).astype(jnp.bfloat16)
    cross_im = (a_im * b_re - a_re * b_im).astype(jnp.bfloat16)
    back_re = (right_mul(cross_re, cos_t) - right_mul(cross_im, sin_t)).astype(jnp.bfloat16)
    back_im = (right_mul(cross_re, sin_t) + right_mul(cross_im, cos_t)).astype(jnp.bfloat16)
    field_out = (left_mul(cos_t, back_re) - left_mul(sin_t, back_im)) * (1.0 / float(edge_len) ** 3)
    return field_out.astype(jnp.bfloat16).reshape(cross_re.shape[0], edge_len * edge_len)

def relax_step(nodes, weight, weight_next, flows, flow_next):
    padded = jnp.pad(nodes, ((1, 1), (0, 0), (1, 1), (1, 1)))
    middle = padded[1:-1]
    laplace = middle[:, :, 2:, 1:-1] + middle[:, :, :-2, 1:-1] + middle[:, :, 1:-1, 2:] + middle[:, :, 1:-1, :-2] - 4.0 * nodes
    lower_nbr = padded[:-2, :, 1:-1, 1:-1]
    upper_nbr = padded[2:, :, 1:-1, 1:-1]
    pull_total = laplace + weight[:, None] * (lower_nbr + flows - nodes) + weight_next[:, None] * (upper_nbr - flow_next - nodes)
    return nodes + 0.15 * pull_total

def reference(patches, prior_patches, blocks, dest, target, flows, valid, stiffness):
    cos_t, sin_t = dft_tables(P_SIZE)
    earlier = jnp.concatenate([prior_patches[None], patches[:-1]], axis=0)

    def one_section(section_args):
        owners, own_blocks, owner_dest, owner_index = section_args
        row_index = (owner_dest[:, 0] * NP + owner_index).astype(jnp.int32)
        chosen = jnp.take(owners, row_index, axis=0)
        return correlate(spectrum(chosen, cos_t, sin_t), spectrum(own_blocks, cos_t, sin_t), cos_t, sin_t)
    corr_maps = lax.map(one_section, (earlier, blocks, dest, target))
    sections = flows.shape[0]
    peak = lax.optimization_barrier(jnp.max(corr_maps.astype(jnp.float32), axis=-1))
    confidence = peak / (1.0 + peak)
    per_tile = confidence.reshape(sections, N_TILE, NB)
    per_column = jnp.repeat(per_tile, RY // NB, axis=2)
    conf_node = jnp.broadcast_to(per_column[:, :, None, :], (sections, N_TILE, RX, RY)).reshape(sections, N_TILE * RX, RY)
    has_prior = (jnp.arange(sections) > 0).astype(jnp.float32)
    weight = stiffness * valid.astype(jnp.float32) * conf_node * has_prior[:, None, None]
    weight_next = jnp.concatenate([weight[1:], jnp.zeros_like(weight[:1])], axis=0)
    flow_next = jnp.concatenate([flows[1:], jnp.zeros_like(flows[:1])], axis=0)

    def iteration(counter, nodes):
        return relax_step(nodes, weight, weight_next, flows, flow_next)
    mesh_nodes = lax.fori_loop(0, ITERS, iteration, jnp.zeros_like(flows))
    return (corr_maps, mesh_nodes)
```

```python
import functools

import jax
import jax.numpy as jnp
from jax import lax
from jax.experimental import pallas as pl
from jax.experimental.pallas import tpu as pltpu
from jax.sharding import PartitionSpec as P

P_SIZE = 160
PIX = 25600
CAP = 2
ITERS = 64
GROUP = 8


def from_behind(value, axis, steps):
    count = lax.axis_size(axis)
    first, last = (max(0, -steps), min(count, count - steps))
    return lax.ppermute(value, axis, [(source, source + steps) for source in range(first, last)])


def dft_tables(edge_len):
    positions = jnp.arange(edge_len, dtype=jnp.int32)
    phase_idx = positions[:, None] * positions[None, :] % edge_len
    angles = phase_idx.astype(jnp.float32) * (2.0 * jnp.pi / edge_len)
    return (jnp.cos(angles).astype(jnp.bfloat16), jnp.sin(angles).astype(jnp.bfloat16))


def right_mul(pixels, matrix_t):
    return jnp.einsum("npq,qk->npk", pixels, matrix_t, preferred_element_type=jnp.float32)


def left_mul(matrix_t, pixels):
    return jnp.einsum("jp,npk->njk", matrix_t, pixels, preferred_element_type=jnp.float32)


def normalized(pixel_rows):
    values = pixel_rows.astype(jnp.float32)
    centred = values - jnp.mean(values, axis=-1, keepdims=True)
    spread = jnp.mean(centred * centred, axis=-1, keepdims=True)
    return (centred * lax.rsqrt(spread + 1e-05)).astype(jnp.bfloat16)


def spectrum(pixel_rows, cos_t, sin_t):
    edge_len = cos_t.shape[0]
    pixels = normalized(pixel_rows).reshape(pixel_rows.shape[0], edge_len, edge_len)
    first_re = right_mul(pixels, cos_t).astype(jnp.bfloat16)
    first_im = right_mul(pixels, sin_t).astype(jnp.bfloat16)
    spec_re = (left_mul(cos_t, first_re) - left_mul(sin_t, first_im)).astype(jnp.bfloat16)
    spec_im = (left_mul(sin_t, first_re) + left_mul(cos_t, first_im)).astype(jnp.bfloat16)
    return (spec_re, spec_im)


def correlate(spec_a, spec_b, cos_t, sin_t):
    edge_len = cos_t.shape[0]
    a_re = spec_a[0].astype(jnp.float32)
    a_im = spec_a[1].astype(jnp.float32)
    b_re = spec_b[0].astype(jnp.float32)
    b_im = spec_b[1].astype(jnp.float32)
    cross_re = (a_re * b_re + a_im * b_im).astype(jnp.bfloat16)
    cross_im = (a_im * b_re - a_re * b_im).astype(jnp.bfloat16)
    back_re = (right_mul(cross_re, cos_t) - right_mul(cross_im, sin_t)).astype(jnp.bfloat16)
    back_im = (right_mul(cross_re, sin_t) + right_mul(cross_im, cos_t)).astype(jnp.bfloat16)
    field_out = (left_mul(cos_t, back_re) - left_mul(sin_t, back_im)) * (1.0 / float(edge_len) ** 3)
    return field_out.astype(jnp.bfloat16).reshape(cross_re.shape[0], edge_len * edge_len)


def relax_kernel(start_ref, spring_ref, flow_ref, conf_ref, out_ref, a_buf, w_buf, n_buf, c_buf, u_buf):
    start = start_ref[0]
    rows = a_buf.shape[0]
    total = spring_ref.shape[0]
    lane = lax.broadcasted_iota(jnp.int32, (1, 8, 128), 2)
    first_col, last_col = lane == 0, lane == 127
    section = lax.broadcasted_iota(jnp.int32, (8, 256), 0)
    u_buf[...] = jnp.zeros_like(u_buf)

    def prepare(i, carry):
        r = start + i
        inside = (r >= 0) & (r < total)

        @pl.when(inside)
        def _():
            conf = conf_ref[r // 8]
            w = 0.15 * spring_ref[r].astype(jnp.float32) * conf
            w = jnp.where(section == 0, 0.0, w)
            f = flow_ref[0, r].astype(jnp.float32)
            wf = w * f
            wn = pltpu.roll(w, 7, 0)
            c = wf - pltpu.roll(wf, 7, 0)
            w_buf[i] = w
            n_buf[i] = wn
            a_buf[i] = 0.4 - w - wn
            c_buf[i] = c
            u_buf[0, i + GROUP] = c

        @pl.when(jnp.logical_not(inside))
        def _():
            zero = jnp.zeros((8, 256), jnp.float32)
            w_buf[i] = zero
            n_buf[i] = zero
            a_buf[i] = zero
            c_buf[i] = zero

        return carry

    lax.fori_loop(0, rows, prepare, 0)

    def step(source, target, s):
        low = (s - 1) // GROUP
        high = (129 - s + GROUP - 1) // GROUP

        def group(g, carry):
            i = g * GROUP
            x = [u_buf[source, pl.ds(i + GROUP - 1, GROUP + 2), :, 128 * h : 128 * h + 128] for h in range(2)]
            mid = [v[1:-1] for v in x]
            rot_up = [pltpu.roll(v, 1, 2) for v in mid]
            rot_down = [pltpu.roll(v, 127, 2) for v in mid]
            left = [jnp.where(first_col, 0.0, rot_up[0]), jnp.where(first_col, rot_up[0], rot_up[1])]
            right = [jnp.where(last_col, rot_down[1], rot_down[0]), jnp.where(last_col, 0.0, rot_down[1])]
            for h in range(2):
                at = (pl.ds(i, GROUP), slice(None), slice(128 * h, 128 * h + 128))
                around = x[h][:-2] + x[h][2:] + left[h] + right[h]
                r = start + i
                row = lax.broadcasted_iota(jnp.int32, (GROUP, 1, 1), 0) + r
                share = jnp.where((row >= 0) & (row < total), 0.15, 0.0)
                new = a_buf[at] * mid[h] + c_buf[at] + share * around
                new = new + w_buf[at] * pltpu.roll(mid[h], 1, 1) + n_buf[at] * pltpu.roll(mid[h], 7, 1)
                u_buf[target, pl.ds(i + GROUP, GROUP), :, 128 * h : 128 * h + 128] = new
            return carry

        lax.fori_loop(low, high, group, 0)

    def pair(k, carry):
        step(0, 1, 2 * k + 2)
        step(1, 0, 2 * k + 3)
        return carry

    lax.fori_loop(0, (ITERS - 2) // 2, pair, 0)
    step(0, 1, ITERS)
    out_ref[...] = u_buf[1, pl.ds(63 + GROUP, 2)]


def relax(start, component, spring, flow, conf):
    rows = 2 * ITERS
    return pl.pallas_call(
        relax_kernel,
        out_shape=jax.ShapeDtypeStruct((2, 8, 256), jnp.float32),
        grid_spec=pltpu.PrefetchScalarGridSpec(
            num_scalar_prefetch=1,
            grid=(1,),
            in_specs=[
                pl.BlockSpec(spring.shape, lambda i, s: (0, 0, 0)),
                pl.BlockSpec((1,) + flow.shape[1:], lambda i, s: (s[1], 0, 0, 0)),
                pl.BlockSpec(conf.shape, lambda i, s: (0, 0, 0)),
            ],
            out_specs=pl.BlockSpec((2, 8, 256), lambda i, s: (0, 0, 0)),
            scratch_shapes=[pltpu.VMEM((rows, 8, 256), jnp.float32)] * 4
            + [pltpu.VMEM((2, rows + 2 * GROUP, 8, 256), jnp.float32)],
        ),
        compiler_params=pltpu.CompilerParams(vmem_limit_bytes=40 * 1024 * 1024),
    )(jnp.stack([start, component]).astype(jnp.int32), spring, flow, conf)


def on_device(patches, prior_patches, blocks, dest, target, flows, valid, stiffness):
    cos_t, sin_t = dft_tables(P_SIZE)
    tile_count = lax.axis_size("tile")
    gz_index = lax.axis_index("gz")
    tile_index = lax.axis_index("tile")

    spring = (stiffness * valid.astype(jnp.float32))[0].astype(jnp.bfloat16)
    both = jnp.stack([spring, flows[0, 0].astype(jnp.bfloat16), flows[0, 1].astype(jnp.bfloat16)])
    everywhere = lax.all_gather(both, ("tile", "gz"))
    node_rows = flows.shape[2]
    everywhere = everywhere.reshape(tile_count, 8, 3, node_rows, -1).transpose(2, 0, 3, 1, 4)
    everywhere = everywhere.reshape(3, tile_count * node_rows, 8, -1)

    shifted = from_behind(patches, "gz", 1)
    earlier = jnp.where(gz_index == 0, prior_patches[None], shifted)[0]
    owner_tile = dest[0, :, 0]
    wanted = target[0]
    own_blocks = blocks[0]
    block_count = own_blocks.shape[0]
    tile_ids = jnp.arange(tile_count, dtype=jnp.int32)
    slot_ids = jnp.arange(tile_count * CAP, dtype=jnp.int32)
    tile_hits = (owner_tile[:, None] == tile_ids[None, :]).astype(jnp.int32)
    slot_rank = jnp.sum((jnp.cumsum(tile_hits, axis=0) - tile_hits) * tile_hits, axis=1)
    slot_index = owner_tile * CAP + slot_rank
    slot_picks = slot_index[:, None] == slot_ids[None, :]
    requested = jnp.sum(jnp.where(slot_picks, wanted[:, None], 0), axis=0).reshape(tile_count, CAP)
    asked_rows = lax.all_to_all(requested, "tile", split_axis=0, concat_axis=0, tiled=True)
    outgoing = jnp.take(earlier, asked_rows.reshape(-1), axis=0).reshape(tile_count, CAP, PIX)
    arrived = lax.all_to_all(outgoing, "tile", split_axis=0, concat_axis=0, tiled=True)
    spec_b = spectrum(own_blocks, cos_t, sin_t)
    chosen = jnp.take(arrived.reshape(tile_count * CAP, PIX), slot_index, axis=0)
    spec_a = spectrum(chosen, cos_t, sin_t)
    corr_maps = correlate(spec_a, spec_b, cos_t, sin_t)
    peak = jnp.max(corr_maps.astype(jnp.float32), axis=-1)
    confidence = peak / (1.0 + peak)

    all_conf = lax.all_gather(confidence, ("tile", "gz")).reshape(tile_count, 8, block_count)
    node_cols = flows.shape[3]
    conf_cols = jnp.repeat(all_conf, node_cols // block_count, axis=2)
    start = tile_index * node_rows + 2 * (gz_index // 2) - (ITERS - 1)
    mine = relax(start, gz_index % 2, everywhere[0], everywhere[1:], conf_cols)
    swapped = lax.all_to_all(mine.transpose(1, 0, 2), "gz", split_axis=0, concat_axis=0, tiled=True)
    mesh_nodes = swapped.reshape(4, 2, 2, node_cols).transpose(1, 0, 2, 3).reshape(1, 2, node_rows, node_cols)
    return (corr_maps[None], mesh_nodes)


def solution(mesh):
    return jax.shard_map(
        on_device,
        mesh=mesh,
        in_specs=(
            P("gz", "tile", None),
            P("tile", None),
            P("gz", "tile", None),
            P("gz", "tile", None),
            P("gz", "tile"),
            P("gz", None, "tile", None),
            P("gz", "tile", None),
            P("gz", "tile", None),
        ),
        out_specs=(P("gz", "tile", None), P("gz", None, "tile", None)),
        check_vma=False,
    )
```

```python
import functools

import jax
import jax.numpy as jnp
from jax import lax
from jax.experimental import pallas as pl
from jax.experimental.pallas import tpu as pltpu
from jax.sharding import PartitionSpec as P

P_SIZE = 160
PIX = 25600
CAP = 2
ITERS = 64
GROUP = 8


def from_behind(value, axis, steps):
    count = lax.axis_size(axis)
    first, last = (max(0, -steps), min(count, count - steps))
    return lax.ppermute(value, axis, [(source, source + steps) for source in range(first, last)])


def dft_tables(edge_len):
    positions = jnp.arange(edge_len, dtype=jnp.int32)
    phase_idx = positions[:, None] * positions[None, :] % edge_len
    angles = phase_idx.astype(jnp.float32) * (2.0 * jnp.pi / edge_len)
    return (jnp.cos(angles).astype(jnp.bfloat16), jnp.sin(angles).astype(jnp.bfloat16))


def right_mul(pixels, matrix_t):
    return jnp.einsum("npq,qk->npk", pixels, matrix_t, preferred_element_type=jnp.float32)


def left_mul(matrix_t, pixels):
    return jnp.einsum("jp,npk->njk", matrix_t, pixels, preferred_element_type=jnp.float32)


def normalized(pixel_rows):
    values = pixel_rows.astype(jnp.float32)
    centred = values - jnp.mean(values, axis=-1, keepdims=True)
    spread = jnp.mean(centred * centred, axis=-1, keepdims=True)
    return (centred * lax.rsqrt(spread + 1e-05)).astype(jnp.bfloat16)


def spectrum(pixel_rows, cos_t, sin_t):
    edge_len = cos_t.shape[0]
    pixels = normalized(pixel_rows).reshape(pixel_rows.shape[0], edge_len, edge_len)
    first_re = right_mul(pixels, cos_t).astype(jnp.bfloat16)
    first_im = right_mul(pixels, sin_t).astype(jnp.bfloat16)
    spec_re = (left_mul(cos_t, first_re) - left_mul(sin_t, first_im)).astype(jnp.bfloat16)
    spec_im = (left_mul(sin_t, first_re) + left_mul(cos_t, first_im)).astype(jnp.bfloat16)
    return (spec_re, spec_im)


def correlate(spec_a, spec_b, cos_t, sin_t):
    edge_len = cos_t.shape[0]
    a_re = spec_a[0].astype(jnp.float32)
    a_im = spec_a[1].astype(jnp.float32)
    b_re = spec_b[0].astype(jnp.float32)
    b_im = spec_b[1].astype(jnp.float32)
    cross_re = (a_re * b_re + a_im * b_im).astype(jnp.bfloat16)
    cross_im = (a_im * b_re - a_re * b_im).astype(jnp.bfloat16)
    back_re = (right_mul(cross_re, cos_t) - right_mul(cross_im, sin_t)).astype(jnp.bfloat16)
    back_im = (right_mul(cross_re, sin_t) + right_mul(cross_im, cos_t)).astype(jnp.bfloat16)
    field_out = (left_mul(cos_t, back_re) - left_mul(sin_t, back_im)) * (1.0 / float(edge_len) ** 3)
    return field_out.astype(jnp.bfloat16).reshape(cross_re.shape[0], edge_len * edge_len)


MESH = pl.DeviceIdType.MESH
GZ = 8
REACH = 8


def group_barrier(peers):
    barrier = pltpu.get_barrier_semaphore()
    for peer in peers:
        pl.semaphore_signal(barrier, inc=1, device_id=peer, device_id_type=MESH)
    pl.semaphore_wait(barrier, len(peers))


def gz_peers():
    gz, tile = lax.axis_index("gz"), lax.axis_index("tile")
    return [(lax.rem(gz + d, GZ), tile) for d in range(1, GZ)]


def tile_peers(tile_count):
    gz, tile = lax.axis_index("gz"), lax.axis_index("tile")
    offsets = [e for k in range(1, REACH + 1) for e in (k, -k)]
    return offsets, [(gz, lax.rem(tile + e + tile_count, tile_count)) for e in offsets]


def exchange_gz(source_of, held, send, recv):
    gz = lax.axis_index("gz")
    copies = []
    for d, peer in enumerate(gz_peers()):
        copies.append(
            pltpu.make_async_remote_copy(
                src_ref=source_of(peer[0]), dst_ref=held.at[gz], send_sem=send.at[d], recv_sem=recv.at[d],
                device_id=peer, device_id_type=MESH,
            )
        )
    for copy in copies:
        copy.start()
    return copies


def exchange_tiles(tile_count, source, window, send, recv):
    offsets, peers = tile_peers(tile_count)
    copies = []
    for n, (e, peer) in enumerate(zip(offsets, peers)):
        copies.append(
            pltpu.make_async_remote_copy(
                src_ref=source, dst_ref=window.at[REACH - e], send_sem=send.at[n], recv_sem=recv.at[n],
                device_id=peer, device_id_type=MESH,
            )
        )
    for copy in copies:
        copy.start()
    return copies


def gather_kernel(tile_count, own_ref, window_ref, held, local, send_a, recv_a, send_b, recv_b):
    gz = lax.axis_index("gz")
    group_barrier(gz_peers() + tile_peers(tile_count)[1])
    copies = exchange_gz(lambda peer: own_ref.at[lax.rem(peer, 2)], held, send_a, recv_a)
    mine = pltpu.make_async_copy(own_ref.at[lax.rem(gz, 2)], held.at[gz], local.at[0])
    mine.start()
    mine.wait()
    for copy in copies:
        copy.wait()
    copies = exchange_tiles(tile_count, held, window_ref, send_b, recv_b)
    mine = pltpu.make_async_copy(held, window_ref.at[REACH], local.at[1])
    mine.start()
    mine.wait()
    for copy in copies:
        copy.wait()


def gather_springs(tile_count, own):
    return pl.pallas_call(
        functools.partial(gather_kernel, tile_count),
        out_shape=jax.ShapeDtypeStruct((2 * REACH + 1, GZ) + own.shape[1:], own.dtype),
        in_specs=[pl.BlockSpec(memory_space=pltpu.VMEM)],
        out_specs=pl.BlockSpec(memory_space=pl.ANY),
        scratch_shapes=[
            pltpu.VMEM((GZ,) + own.shape[1:], own.dtype),
            pltpu.SemaphoreType.DMA((2,)),
            pltpu.SemaphoreType.DMA((GZ - 1,)),
            pltpu.SemaphoreType.DMA((GZ - 1,)),
            pltpu.SemaphoreType.DMA((2 * REACH,)),
            pltpu.SemaphoreType.DMA((2 * REACH,)),
        ],
        compiler_params=pltpu.CompilerParams(collective_id=1, has_side_effects=True),
        cost_estimate=pl.CostEstimate(flops=0, bytes_accessed=8 * 1024 * 1024, transcendentals=0),
    )(own)


def conf_kernel(tile_count, own_ref, window_ref, held, packed, send_a, recv_a, send_b, recv_b):
    gz = lax.axis_index("gz")
    group_barrier(gz_peers() + tile_peers(tile_count)[1])
    copies = exchange_gz(lambda peer: own_ref, held, send_a, recv_a)
    held[gz] = own_ref[...]
    for copy in copies:
        copy.wait()
    for s in range(GZ):
        packed[s : s + 1, :] = held[s, 0:1, :]
    copies = exchange_tiles(tile_count, packed, window_ref, send_b, recv_b)
    window_ref[REACH] = packed[...]
    for copy in copies:
        copy.wait()


def gather_conf(tile_count, conf_cols):
    own = jnp.broadcast_to(conf_cols[None, :], (8,) + conf_cols.shape)
    return pl.pallas_call(
        functools.partial(conf_kernel, tile_count),
        out_shape=jax.ShapeDtypeStruct((2 * REACH + 1,) + own.shape, own.dtype),
        in_specs=[pl.BlockSpec(memory_space=pltpu.VMEM)],
        out_specs=pl.BlockSpec(memory_space=pltpu.VMEM),
        scratch_shapes=[
            pltpu.VMEM((GZ,) + own.shape, own.dtype),
            pltpu.VMEM(own.shape, own.dtype),
            pltpu.SemaphoreType.DMA((GZ - 1,)),
            pltpu.SemaphoreType.DMA((GZ - 1,)),
            pltpu.SemaphoreType.DMA((2 * REACH,)),
            pltpu.SemaphoreType.DMA((2 * REACH,)),
        ],
        compiler_params=pltpu.CompilerParams(collective_id=2, has_side_effects=True),
    )(own)


def spread_kernel(own_ref, out_ref, source, held, send, recv):
    gz = lax.axis_index("gz")
    group_barrier(gz_peers())
    for s in range(GZ):
        for r in range(2):
            source[s, r : r + 1, :] = own_ref[r, s : s + 1, :]
    copies = exchange_gz(lambda peer: source.at[peer], held, send, recv)
    held[gz] = source[gz]
    for copy in copies:
        copy.wait()
    for g in range(GZ):
        out_ref[g % 2, 2 * (g // 2) : 2 * (g // 2) + 2, :] = held[g, 0:2, :]


def spread_result(own):
    columns = own.shape[-1]
    return pl.pallas_call(
        spread_kernel,
        out_shape=jax.ShapeDtypeStruct((2, 8, columns), own.dtype),
        in_specs=[pl.BlockSpec(memory_space=pltpu.VMEM)],
        out_specs=pl.BlockSpec(memory_space=pltpu.VMEM),
        scratch_shapes=[
            pltpu.VMEM((GZ, 8, columns), own.dtype),
            pltpu.VMEM((GZ, 8, columns), own.dtype),
            pltpu.SemaphoreType.DMA((GZ - 1,)),
            pltpu.SemaphoreType.DMA((GZ - 1,)),
        ],
        compiler_params=pltpu.CompilerParams(collective_id=3, has_side_effects=True),
    )(own)


def relax_kernel(total, place_ref, window_ref, conf_ref, out_ref, s_buf, a_buf, w_buf, n_buf, c_buf, u_buf):
    tile, part = place_ref[0], place_ref[1]
    start = tile * 8 + 2 * part - (ITERS - 1)
    rows = a_buf.shape[0]
    lane = lax.broadcasted_iota(jnp.int32, (1, 8, 128), 2)
    first_col, last_col = lane == 0, lane == 127
    section = lax.broadcasted_iota(jnp.int32, (8, 256), 0)
    u_buf[...] = jnp.zeros_like(u_buf)

    def picked(j):
        return jnp.concatenate([s_buf[h, pl.ds(j, 8, stride=16), :] for h in range(2)], axis=1)

    def prepare(k, carry):
        at = tile + k - REACH
        inside = (at >= 0) & (at < total // 8)
        conf = conf_ref[k]
        nodes = window_ref[k].astype(jnp.float32).reshape(128, 256)
        s_buf[0], s_buf[1] = nodes[:, :128], nodes[:, 128:]
        for j in range(8):
            i = 8 * k + j - 2 * part - 1

            @pl.when((i >= 0) & (i < rows) & inside)
            def _():
                w = 0.15 * picked(j) * conf
                w = jnp.where(section == 0, 0.0, w)
                wf = w * picked(8 + j)
                wn = pltpu.roll(w, 7, 0)
                c = wf - pltpu.roll(wf, 7, 0)
                w_buf[i] = w
                n_buf[i] = wn
                a_buf[i] = 0.4 - w - wn
                c_buf[i] = c
                u_buf[0, i + GROUP] = c

            @pl.when((i >= 0) & (i < rows) & jnp.logical_not(inside))
            def _():
                zero = jnp.zeros((8, 256), jnp.float32)
                w_buf[i] = zero
                n_buf[i] = zero
                a_buf[i] = zero
                c_buf[i] = zero

        return carry

    lax.fori_loop(0, 2 * REACH + 1, prepare, 0)

    def step(source, target, s):
        low = (s - 1) // GROUP
        high = (129 - s + GROUP - 1) // GROUP

        def group(g, carry):
            i = g * GROUP
            x = [u_buf[source, pl.ds(i + GROUP - 1, GROUP + 2), :, 128 * h : 128 * h + 128] for h in range(2)]
            mid = [v[1:-1] for v in x]
            rot_up = [pltpu.roll(v, 1, 2) for v in mid]
            rot_down = [pltpu.roll(v, 127, 2) for v in mid]
            left = [jnp.where(first_col, 0.0, rot_up[0]), jnp.where(first_col, rot_up[0], rot_up[1])]
            right = [jnp.where(last_col, rot_down[1], rot_down[0]), jnp.where(last_col, 0.0, rot_down[1])]
            for h in range(2):
                at = (pl.ds(i, GROUP), slice(None), slice(128 * h, 128 * h + 128))
                around = x[h][:-2] + x[h][2:] + left[h] + right[h]
                r = start + i
                row = lax.broadcasted_iota(jnp.int32, (GROUP, 1, 1), 0) + r
                share = jnp.where((row >= 0) & (row < total), 0.15, 0.0)
                new = a_buf[at] * mid[h] + c_buf[at] + share * around
                new = new + w_buf[at] * pltpu.roll(mid[h], 1, 1) + n_buf[at] * pltpu.roll(mid[h], 7, 1)
                u_buf[target, pl.ds(i + GROUP, GROUP), :, 128 * h : 128 * h + 128] = new
            return carry

        lax.fori_loop(low, high, group, 0)

    def pair(k, carry):
        step(0, 1, 2 * k + 2)
        step(1, 0, 2 * k + 3)
        return carry

    lax.fori_loop(0, (ITERS - 2) // 2, pair, 0)
    step(0, 1, ITERS)
    out_ref[...] = u_buf[1, pl.ds(63 + GROUP, 2)]


def relax(place, total, window, conf):
    rows = 2 * ITERS
    return pl.pallas_call(
        functools.partial(relax_kernel, total),
        out_shape=jax.ShapeDtypeStruct((2, 8, 256), jnp.float32),
        grid_spec=pltpu.PrefetchScalarGridSpec(
            num_scalar_prefetch=1,
            grid=(1,),
            in_specs=[
                pl.BlockSpec(window.shape, lambda i, s: (0, 0, 0, 0)),
                pl.BlockSpec(conf.shape, lambda i, s: (0, 0, 0)),
            ],
            out_specs=pl.BlockSpec((2, 8, 256), lambda i, s: (0, 0, 0)),
            scratch_shapes=[pltpu.VMEM((2, 128, 128), jnp.float32)]
            + [pltpu.VMEM((rows, 8, 256), jnp.float32)] * 4
            + [pltpu.VMEM((2, rows + 2 * GROUP, 8, 256), jnp.float32)],
        ),
        compiler_params=pltpu.CompilerParams(vmem_limit_bytes=40 * 1024 * 1024),
    )(place, window, conf)


def on_device(patches, prior_patches, blocks, dest, target, flows, valid, stiffness):
    cos_t, sin_t = dft_tables(P_SIZE)
    tile_count = lax.axis_size("tile")
    gz_index = lax.axis_index("gz")
    tile_index = lax.axis_index("tile")

    node_rows, node_cols = flows.shape[2:]
    spring = (stiffness * valid.astype(jnp.float32))[0]
    own_nodes = jnp.stack([jnp.concatenate([spring, flows[0, c]]) for c in range(2)]).astype(jnp.bfloat16)
    window = gather_springs(tile_count, own_nodes)

    shifted = from_behind(patches, "gz", 1)
    earlier = jnp.where(gz_index == 0, prior_patches[None], shifted)[0]
    owner_tile = dest[0, :, 0]
    wanted = target[0]
    own_blocks = blocks[0]
    block_count = own_blocks.shape[0]
    tile_ids = jnp.arange(tile_count, dtype=jnp.int32)
    slot_ids = jnp.arange(tile_count * CAP, dtype=jnp.int32)
    tile_hits = (owner_tile[:, None] == tile_ids[None, :]).astype(jnp.int32)
    slot_rank = jnp.sum((jnp.cumsum(tile_hits, axis=0) - tile_hits) * tile_hits, axis=1)
    slot_index = owner_tile * CAP + slot_rank
    slot_picks = slot_index[:, None] == slot_ids[None, :]
    requested = jnp.sum(jnp.where(slot_picks, wanted[:, None], 0), axis=0).reshape(tile_count, CAP)
    asked_rows = lax.all_to_all(requested, "tile", split_axis=0, concat_axis=0, tiled=True)
    outgoing = jnp.take(earlier, asked_rows.reshape(-1), axis=0).reshape(tile_count, CAP, PIX)
    arrived = lax.all_to_all(outgoing, "tile", split_axis=0, concat_axis=0, tiled=True)
    spec_b = spectrum(own_blocks, cos_t, sin_t)
    chosen = jnp.take(arrived.reshape(tile_count * CAP, PIX), slot_index, axis=0)
    spec_a = spectrum(chosen, cos_t, sin_t)
    corr_maps = correlate(spec_a, spec_b, cos_t, sin_t)
    peak = jnp.max(corr_maps.astype(jnp.float32), axis=-1)
    confidence = peak / (1.0 + peak)

    conf_window = gather_conf(tile_count, jnp.repeat(confidence, node_cols // block_count))
    place = jnp.stack([tile_index, gz_index // 2]).astype(jnp.int32)
    mine = relax(place, tile_count * node_rows, window, conf_window)
    mesh_nodes = spread_result(mine)[None]
    return (corr_maps[None], mesh_nodes)


def solution(mesh):
    return jax.shard_map(
        on_device,
        mesh=mesh,
        in_specs=(
            P("gz", "tile", None),
            P("tile", None),
            P("gz", "tile", None),
            P("gz", "tile", None),
            P("gz", "tile"),
            P("gz", None, "tile", None),
            P("gz", "tile", None),
            P("gz", "tile", None),
        ),
        out_specs=(P("gz", "tile", None), P("gz", None, "tile", None)),
        check_vma=False,
    )
```

```python
import functools

import jax
import jax.numpy as jnp
import ml_dtypes
import numpy as np
from jax import lax
from jax.experimental import pallas as pl
from jax.experimental.pallas import tpu as pltpu
from jax.sharding import PartitionSpec as P

P_SIZE = 160
PIX = 25600
CAP = 2
ITERS = 64
GROUP = 8


def from_behind(value, axis, steps):
    count = lax.axis_size(axis)
    first, last = (max(0, -steps), min(count, count - steps))
    return lax.ppermute(value, axis, [(source, source + steps) for source in range(first, last)])


LANES = 128
HALF = 64
WIRE = 208
BATCH = 16


def tables():
    size = P_SIZE
    line = np.arange(size)
    angles = (np.outer(line, line) % size).astype(np.float32) * np.float32(2.0 * np.pi / size)
    rounded = lambda x: x.astype(ml_dtypes.bfloat16).astype(np.float32)
    cos_t, sin_t = rounded(np.cos(angles)), rounded(np.sin(angles))
    lane = np.arange(2 * LANES)
    column = HALF * (lane // LANES) + lane % HALF
    used = column <= size // 2
    column = np.where(used, column, 0)
    real = lane % LANES < HALF
    c, s = cos_t[:, column] * used, sin_t[:, column] * used
    first = np.zeros((2 * LANES, 4 * LANES), np.float32)
    first[:size, : 2 * LANES] = np.where(real, c, s)
    first[:size, 2 * LANES :] = np.where(real, -s, c)
    second = np.concatenate([cos_t, sin_t], axis=1)
    third = np.concatenate([cos_t, sin_t], axis=0)
    twice = np.where((column == 0) | (column == size // 2), 1.0, 2.0)
    fourth = np.zeros((4 * LANES, 2 * LANES), np.float32)
    fourth[: 2 * LANES, :size] = (np.where(real, c, -s) * twice).T
    fourth[2 * LANES :, :size] = (np.where(real, -s, -c) * twice).T
    return [jnp.asarray(x, jnp.bfloat16) for x in (first, second, third, fourth)]


def to_images(rows_ref, low_buf, high_buf):
    parts = PIX // 640
    chunk = lambda m: rows_ref[:, pl.ds(pl.multiple_of(640 * m, LANES), 640)].astype(jnp.float32)
    fold = lambda x: sum(x[:, LANES * k : LANES * k + LANES] for k in range(5))
    zero = jnp.zeros((BATCH, LANES), jnp.float32)
    sums = lax.fori_loop(0, parts, lambda m, t: t + fold(chunk(m)), zero)
    mean = jnp.sum(sums, axis=1, keepdims=True) * (1.0 / PIX)

    def square(m, t):
        x = chunk(m) - mean
        return t + fold(x * x)

    sums = lax.fori_loop(0, parts, square, zero)
    scale = lax.rsqrt(jnp.sum(sums, axis=1, keepdims=True) * (1.0 / PIX) + 1e-05)
    lane = lax.broadcasted_iota(jnp.int32, (BATCH, LANES), 1)

    def place(m, carry):
        x = (chunk(m) - mean) * scale
        t = [x[:, LANES * k : LANES * k + LANES] for k in range(5)]
        low = [
            t[0],
            pltpu.roll(jnp.where(lane < 32, t[2], t[1]), 96, 1),
            pltpu.roll(jnp.where(lane < 64, t[3], t[2]), 64, 1),
            pltpu.roll(jnp.where(lane < 96, t[4], t[3]), 32, 1),
        ]
        high = [t[1], pltpu.roll(t[2], 96, 1), pltpu.roll(t[3], 64, 1), pltpu.roll(t[4], 32, 1)]
        for k in range(4):
            at = pl.ds(4 * m + k, BATCH, stride=P_SIZE)
            low_buf[at, :] = low[k]
            high_buf[at, :] = high[k]
        return carry

    lax.fori_loop(0, parts, place, 0)


def image_spectrum(n, low_buf, high_buf, first_ref, second_ref):
    at = pl.ds(pl.multiple_of(P_SIZE * n, 8), P_SIZE)
    image = jnp.concatenate([low_buf[at, :], high_buf[at, :]], axis=1).astype(jnp.bfloat16)
    first = jnp.dot(image, first_ref[...], preferred_element_type=jnp.float32).astype(jnp.bfloat16)
    both = jnp.concatenate([first[:, : 2 * LANES], first[:, 2 * LANES :]], axis=0)
    return jnp.dot(second_ref[...], both, preferred_element_type=jnp.float32)


def block_kernel(rows_ref, first_ref, second_ref, out_ref, low_buf, high_buf):
    to_images(rows_ref, low_buf, high_buf)
    low_half = lax.broadcasted_iota(jnp.int32, (P_SIZE, LANES), 1) < HALF

    def image(n, carry):
        spec = image_spectrum(n, low_buf, high_buf, first_ref, second_ref)
        for h in range(2):
            x = spec[:, LANES * h : LANES * h + LANES]
            swapped = pltpu.roll(x, HALF, 1)
            out_ref[n, :, LANES * h : LANES * h + LANES] = jnp.where(low_half, x, swapped).astype(jnp.bfloat16)
            at = slice(LANES * (2 + h), LANES * (3 + h))
            out_ref[n, :, at] = jnp.where(low_half, swapped, -x).astype(jnp.bfloat16)
        return carry

    lax.fori_loop(0, BATCH, image, 0)


def block_spectra(rows, first, second):
    count = rows.shape[0]
    fixed = lambda x: pl.BlockSpec(x.shape, lambda i: (0, 0))
    return pl.pallas_call(
        block_kernel,
        out_shape=jax.ShapeDtypeStruct((count, P_SIZE, 4 * LANES), jnp.bfloat16),
        grid=(count // BATCH,),
        in_specs=[pl.BlockSpec((BATCH, PIX), lambda i: (i, 0)), fixed(first), fixed(second)],
        out_specs=pl.BlockSpec((BATCH, P_SIZE, 4 * LANES), lambda i: (i, 0, 0)),
        scratch_shapes=[pltpu.VMEM((BATCH * P_SIZE, LANES), jnp.float32)] * 2,
        compiler_params=pltpu.CompilerParams(vmem_limit_bytes=40 * 1024 * 1024),
        cost_estimate=pl.CostEstimate(flops=20_000_000_000, bytes_accessed=8_000_000, transcendentals=0),
    )(rows, first, second)


def patch_kernel(asked_ref, rows_ref, first_ref, second_ref, out_ref, low_buf, high_buf, wire_buf, sems):
    to_images(rows_ref, low_buf, high_buf)
    lane = lax.broadcasted_iota(jnp.int32, (8, LANES), 1) % HALF

    def image(n, carry):
        spec = image_spectrum(n, low_buf, high_buf, first_ref, second_ref)
        rest = [spec[8 * i : 8 * i + 8, LANES:] for i in range(20)]
        pieces = [spec[:, :LANES]]
        for i in range(5):
            pieces.append(sum(pltpu.roll(jnp.where(lane < 16, rest[5 * b + i], 0.0), 16 * b, 1) for b in range(4)))
        pieces.append(sum(pltpu.roll(jnp.where(lane == 16, rest[i], 0.0), (i + 112) % LANES, 1) for i in range(20)))
        wire_buf[n] = jnp.concatenate(pieces, axis=0).astype(jnp.bfloat16)
        return carry

    lax.fori_loop(0, BATCH, image, 0)
    copy = lambda s: pltpu.make_async_copy(wire_buf.at[asked_ref[s]], out_ref.at[s], sems.at[s])
    slots = out_ref.shape[0]

    def begin(s, carry):
        copy(s).start()
        return carry

    def finish(s, carry):
        copy(s).wait()
        return carry

    lax.fori_loop(0, slots, begin, 0)
    lax.fori_loop(0, slots, finish, 0)


def patch_spectra(asked, rows, first, second):
    slots = asked.shape[0]
    fixed = lambda x: pl.BlockSpec(x.shape, lambda i, s: (0, 0))
    return pl.pallas_call(
        patch_kernel,
        out_shape=jax.ShapeDtypeStruct((slots, WIRE, LANES), jnp.bfloat16),
        grid_spec=pltpu.PrefetchScalarGridSpec(
            num_scalar_prefetch=1,
            grid=(1,),
            in_specs=[fixed(rows), fixed(first), fixed(second)],
            out_specs=pl.BlockSpec(memory_space=pl.ANY),
            scratch_shapes=[pltpu.VMEM((BATCH * P_SIZE, LANES), jnp.float32)] * 2
            + [pltpu.VMEM((BATCH, WIRE, LANES), jnp.bfloat16), pltpu.SemaphoreType.DMA((slots,))],
        ),
        compiler_params=pltpu.CompilerParams(vmem_limit_bytes=40 * 1024 * 1024),
        cost_estimate=pl.CostEstimate(flops=10_000_000_000, bytes_accessed=8_000_000, transcendentals=0),
    )(asked, rows, first, second)


def match_kernel(slot_ref, wire_ref, block_ref, third_ref, fourth_ref, map_ref, peak_ref, low_buf, high_buf):
    step = pl.program_id(0)
    lane8 = lax.broadcasted_iota(jnp.int32, (8, LANES), 1) % HALF == 16

    def image(n, carry):
        wire = wire_ref[slot_ref[BATCH * step + n]].astype(jnp.float32)
        last = wire[200:208]
        rest = []
        for i in range(20):
            part = wire[160 + 8 * (i % 5) : 168 + 8 * (i % 5)]
            part = pltpu.roll(part, (LANES - 16 * (i // 5)) % LANES, 1)
            rest.append(jnp.where(lane8, pltpu.roll(last, (16 - i) % LANES, 1), part))
        cross = []
        for h, a in enumerate((wire[:P_SIZE], jnp.concatenate(rest, axis=0))):
            straight = block_ref[n, :, LANES * h : LANES * h + LANES].astype(jnp.float32)
            swapped = block_ref[n, :, LANES * (2 + h) : LANES * (3 + h)].astype(jnp.float32)
            cross.append((a * straight + pltpu.roll(a, HALF, 1) * swapped).astype(jnp.bfloat16))
        back = jnp.dot(third_ref[...], jnp.concatenate(cross, axis=1), preferred_element_type=jnp.float32)
        back = back.astype(jnp.bfloat16)
        back = jnp.concatenate([back[:P_SIZE], back[P_SIZE:]], axis=1)
        field = jnp.dot(back, fourth_ref[...], preferred_element_type=jnp.float32) * (1.0 / float(P_SIZE) ** 3)
        at = pl.ds(pl.multiple_of(P_SIZE * n, 8), P_SIZE)
        low_buf[at, :] = field[:, :LANES]
        high_buf[at, :] = field[:, LANES:]
        return carry

    lax.fori_loop(0, BATCH, image, 0)
    lane = lax.broadcasted_iota(jnp.int32, (BATCH, LANES), 1)

    def place(m, top):
        load = lambda buf, k: buf[pl.ds(4 * m + k, BATCH, stride=P_SIZE), :]
        low = [load(low_buf, 0)] + [pltpu.roll(load(low_buf, k), 32 * k, 1) for k in range(1, 4)]
        high = [load(high_buf, 0)] + [pltpu.roll(load(high_buf, k), 32 * k, 1) for k in range(1, 4)]
        tiles = [
            low[0],
            jnp.where(lane < 32, high[0], low[1]),
            jnp.where(lane < 32, low[1], jnp.where(lane < 64, high[1], low[2])),
            jnp.where(lane < 64, low[2], jnp.where(lane < 96, high[2], low[3])),
            jnp.where(lane < 96, low[3], high[3]),
        ]
        rows = jnp.concatenate(tiles, axis=1).astype(jnp.bfloat16)
        map_ref[:, pl.ds(pl.multiple_of(640 * m, LANES), 640)] = rows
        for tile in tiles:
            top = jnp.maximum(top, tile)
        return top

    top = lax.fori_loop(0, P_SIZE // 4, place, jnp.full((BATCH, LANES), -jnp.inf, jnp.float32))
    top = jnp.max(top, axis=1, keepdims=True).astype(jnp.bfloat16).astype(jnp.float32)
    peak_ref[...] = jnp.broadcast_to(top, (BATCH, LANES))


def match(slot_index, wire, block_spec, third, fourth):
    count = block_spec.shape[0]
    fixed = lambda x: pl.BlockSpec(x.shape, lambda i, s: (0,) * x.ndim)
    return pl.pallas_call(
        match_kernel,
        out_shape=(
            jax.ShapeDtypeStruct((count, PIX), jnp.bfloat16),
            jax.ShapeDtypeStruct((count, LANES), jnp.float32),
        ),
        grid_spec=pltpu.PrefetchScalarGridSpec(
            num_scalar_prefetch=1,
            grid=(count // BATCH,),
            in_specs=[
                fixed(wire),
                pl.BlockSpec((BATCH, P_SIZE, 4 * LANES), lambda i, s: (i, 0, 0)),
                fixed(third),
                fixed(fourth),
            ],
            out_specs=[
                pl.BlockSpec((BATCH, PIX), lambda i, s: (i, 0)),
                pl.BlockSpec((BATCH, LANES), lambda i, s: (i, 0)),
            ],
            scratch_shapes=[pltpu.VMEM((BATCH * P_SIZE, LANES), jnp.float32)] * 2,
        ),
        compiler_params=pltpu.CompilerParams(vmem_limit_bytes=48 * 1024 * 1024),
        cost_estimate=pl.CostEstimate(flops=20_000_000_000, bytes_accessed=10_000_000, transcendentals=0),
    )(slot_index, wire, block_spec, third, fourth)


MESH = pl.DeviceIdType.MESH
GZ = 8
REACH = 8


def group_barrier(peers):
    barrier = pltpu.get_barrier_semaphore()
    for peer in peers:
        pl.semaphore_signal(barrier, inc=1, device_id=peer, device_id_type=MESH)
    pl.semaphore_wait(barrier, len(peers))


def gz_peers():
    gz, tile = lax.axis_index("gz"), lax.axis_index("tile")
    return [(lax.rem(gz + d, GZ), tile) for d in range(1, GZ)]


def tile_peers(tile_count):
    gz, tile = lax.axis_index("gz"), lax.axis_index("tile")
    offsets = [e for k in range(1, REACH + 1) for e in (k, -k)]
    return offsets, [(gz, lax.rem(tile + e + tile_count, tile_count)) for e in offsets]


def exchange_gz(source_of, held, send, recv):
    gz = lax.axis_index("gz")
    copies = []
    for d, peer in enumerate(gz_peers()):
        copies.append(
            pltpu.make_async_remote_copy(
                src_ref=source_of(peer[0]), dst_ref=held.at[gz], send_sem=send.at[d], recv_sem=recv.at[d],
                device_id=peer, device_id_type=MESH,
            )
        )
    for copy in copies:
        copy.start()
    return copies


def exchange_tiles(tile_count, source, window, send, recv):
    offsets, peers = tile_peers(tile_count)
    copies = []
    for n, (e, peer) in enumerate(zip(offsets, peers)):
        copies.append(
            pltpu.make_async_remote_copy(
                src_ref=source, dst_ref=window.at[REACH - e], send_sem=send.at[n], recv_sem=recv.at[n],
                device_id=peer, device_id_type=MESH,
            )
        )
    for copy in copies:
        copy.start()
    return copies


def gather_kernel(tile_count, own_ref, window_ref, held, local, send_a, recv_a, send_b, recv_b):
    gz = lax.axis_index("gz")
    group_barrier(gz_peers() + tile_peers(tile_count)[1])
    copies = exchange_gz(lambda peer: own_ref.at[lax.rem(peer, 2)], held, send_a, recv_a)
    mine = pltpu.make_async_copy(own_ref.at[lax.rem(gz, 2)], held.at[gz], local.at[0])
    mine.start()
    mine.wait()
    for copy in copies:
        copy.wait()
    copies = exchange_tiles(tile_count, held, window_ref, send_b, recv_b)
    mine = pltpu.make_async_copy(held, window_ref.at[REACH], local.at[1])
    mine.start()
    mine.wait()
    for copy in copies:
        copy.wait()


def gather_springs(tile_count, own):
    return pl.pallas_call(
        functools.partial(gather_kernel, tile_count),
        out_shape=jax.ShapeDtypeStruct((2 * REACH + 1, GZ) + own.shape[1:], own.dtype),
        in_specs=[pl.BlockSpec(memory_space=pltpu.VMEM)],
        out_specs=pl.BlockSpec(memory_space=pl.ANY),
        scratch_shapes=[
            pltpu.VMEM((GZ,) + own.shape[1:], own.dtype),
            pltpu.SemaphoreType.DMA((2,)),
            pltpu.SemaphoreType.DMA((GZ - 1,)),
            pltpu.SemaphoreType.DMA((GZ - 1,)),
            pltpu.SemaphoreType.DMA((2 * REACH,)),
            pltpu.SemaphoreType.DMA((2 * REACH,)),
        ],
        compiler_params=pltpu.CompilerParams(collective_id=1, has_side_effects=True),
        cost_estimate=pl.CostEstimate(flops=0, bytes_accessed=8 * 1024 * 1024, transcendentals=0),
    )(own)


def conf_kernel(tile_count, peak_ref, window_ref, own_ref, held, packed, send_a, recv_a, send_b, recv_b):
    gz = lax.axis_index("gz")
    count, columns = peak_ref.shape[0], own_ref.shape[1]
    peak = jnp.concatenate([peak_ref[...]] * (columns // LANES), axis=1)
    block = lax.broadcasted_iota(jnp.int32, (count, columns), 1) // (columns // count)
    mine = block == lax.broadcasted_iota(jnp.int32, (count, columns), 0)
    confidence = jnp.sum(jnp.where(mine, peak / (1.0 + peak), 0.0), axis=0, keepdims=True)
    own_ref[...] = jnp.broadcast_to(confidence, own_ref.shape)
    group_barrier(gz_peers() + tile_peers(tile_count)[1])
    copies = exchange_gz(lambda peer: own_ref, held, send_a, recv_a)
    held[gz] = own_ref[...]
    for copy in copies:
        copy.wait()
    for s in range(GZ):
        packed[s : s + 1, :] = held[s, 0:1, :]
    copies = exchange_tiles(tile_count, packed, window_ref, send_b, recv_b)
    window_ref[REACH] = packed[...]
    for copy in copies:
        copy.wait()


def gather_conf(tile_count, peaks, columns):
    own = jax.ShapeDtypeStruct((8, columns), jnp.float32)
    return pl.pallas_call(
        functools.partial(conf_kernel, tile_count),
        out_shape=jax.ShapeDtypeStruct((2 * REACH + 1,) + own.shape, own.dtype),
        in_specs=[pl.BlockSpec(memory_space=pltpu.VMEM)],
        out_specs=pl.BlockSpec(memory_space=pltpu.VMEM),
        scratch_shapes=[
            pltpu.VMEM(own.shape, own.dtype),
            pltpu.VMEM((GZ,) + own.shape, own.dtype),
            pltpu.VMEM(own.shape, own.dtype),
            pltpu.SemaphoreType.DMA((GZ - 1,)),
            pltpu.SemaphoreType.DMA((GZ - 1,)),
            pltpu.SemaphoreType.DMA((2 * REACH,)),
            pltpu.SemaphoreType.DMA((2 * REACH,)),
        ],
        compiler_params=pltpu.CompilerParams(collective_id=2, has_side_effects=True),
    )(peaks)


def spread_kernel(own_ref, out_ref, source, held, send, recv):
    gz = lax.axis_index("gz")
    group_barrier(gz_peers())
    for s in range(GZ):
        for r in range(2):
            source[s, r : r + 1, :] = own_ref[r, s : s + 1, :]
    copies = exchange_gz(lambda peer: source.at[peer], held, send, recv)
    held[gz] = source[gz]
    for copy in copies:
        copy.wait()
    for g in range(GZ):
        out_ref[g % 2, 2 * (g // 2) : 2 * (g // 2) + 2, :] = held[g, 0:2, :]


def spread_result(own):
    columns = own.shape[-1]
    return pl.pallas_call(
        spread_kernel,
        out_shape=jax.ShapeDtypeStruct((2, 8, columns), own.dtype),
        in_specs=[pl.BlockSpec(memory_space=pltpu.VMEM)],
        out_specs=pl.BlockSpec(memory_space=pltpu.VMEM),
        scratch_shapes=[
            pltpu.VMEM((GZ, 8, columns), own.dtype),
            pltpu.VMEM((GZ, 8, columns), own.dtype),
            pltpu.SemaphoreType.DMA((GZ - 1,)),
            pltpu.SemaphoreType.DMA((GZ - 1,)),
        ],
        compiler_params=pltpu.CompilerParams(collective_id=3, has_side_effects=True),
    )(own)


def relax_kernel(total, place_ref, window_ref, conf_ref, out_ref, s_buf, a_buf, w_buf, n_buf, c_buf, u_buf):
    tile, part = place_ref[0], place_ref[1]
    start = tile * 8 + 2 * part - (ITERS - 1)
    rows = a_buf.shape[0]
    lane = lax.broadcasted_iota(jnp.int32, (1, 8, 128), 2)
    first_col, last_col = lane == 0, lane == 127
    section = lax.broadcasted_iota(jnp.int32, (8, 256), 0)
    u_buf[...] = jnp.zeros_like(u_buf)

    def picked(j):
        return jnp.concatenate([s_buf[h, pl.ds(j, 8, stride=16), :] for h in range(2)], axis=1)

    def prepare(k, carry):
        at = tile + k - REACH
        inside = (at >= 0) & (at < total // 8)
        conf = conf_ref[k]
        nodes = window_ref[k].astype(jnp.float32).reshape(128, 256)
        s_buf[0], s_buf[1] = nodes[:, :128], nodes[:, 128:]
        for j in range(8):
            i = 8 * k + j - 2 * part - 1

            @pl.when((i >= 0) & (i < rows) & inside)
            def _():
                w = 0.15 * picked(j) * conf
                w = jnp.where(section == 0, 0.0, w)
                wf = w * picked(8 + j)
                wn = pltpu.roll(w, 7, 0)
                c = wf - pltpu.roll(wf, 7, 0)
                w_buf[i] = w
                n_buf[i] = wn
                a_buf[i] = 0.4 - w - wn
                c_buf[i] = c
                u_buf[0, i + GROUP] = c

            @pl.when((i >= 0) & (i < rows) & jnp.logical_not(inside))
            def _():
                zero = jnp.zeros((8, 256), jnp.float32)
                w_buf[i] = zero
                n_buf[i] = zero
                a_buf[i] = zero
                c_buf[i] = zero

        return carry

    lax.fori_loop(0, 2 * REACH + 1, prepare, 0)

    def step(source, target, s):
        low = (s - 1) // GROUP
        high = (129 - s + GROUP - 1) // GROUP

        def group(g, carry):
            i = g * GROUP
            x = [u_buf[source, pl.ds(i + GROUP - 1, GROUP + 2), :, 128 * h : 128 * h + 128] for h in range(2)]
            mid = [v[1:-1] for v in x]
            rot_up = [pltpu.roll(v, 1, 2) for v in mid]
            rot_down = [pltpu.roll(v, 127, 2) for v in mid]
            left = [jnp.where(first_col, 0.0, rot_up[0]), jnp.where(first_col, rot_up[0], rot_up[1])]
            right = [jnp.where(last_col, rot_down[1], rot_down[0]), jnp.where(last_col, 0.0, rot_down[1])]
            for h in range(2):
                at = (pl.ds(i, GROUP), slice(None), slice(128 * h, 128 * h + 128))
                around = x[h][:-2] + x[h][2:] + left[h] + right[h]
                r = start + i
                row = lax.broadcasted_iota(jnp.int32, (GROUP, 1, 1), 0) + r
                share = jnp.where((row >= 0) & (row < total), 0.15, 0.0)
                new = a_buf[at] * mid[h] + c_buf[at] + share * around
                new = new + w_buf[at] * pltpu.roll(mid[h], 1, 1) + n_buf[at] * pltpu.roll(mid[h], 7, 1)
                u_buf[target, pl.ds(i + GROUP, GROUP), :, 128 * h : 128 * h + 128] = new
            return carry

        lax.fori_loop(low, high, group, 0)

    def pair(k, carry):
        step(0, 1, 2 * k + 2)
        step(1, 0, 2 * k + 3)
        return carry

    lax.fori_loop(0, (ITERS - 2) // 2, pair, 0)
    step(0, 1, ITERS)
    out_ref[...] = u_buf[1, pl.ds(63 + GROUP, 2)]


def relax(place, total, window, conf):
    rows = 2 * ITERS
    return pl.pallas_call(
        functools.partial(relax_kernel, total),
        out_shape=jax.ShapeDtypeStruct((2, 8, 256), jnp.float32),
        grid_spec=pltpu.PrefetchScalarGridSpec(
            num_scalar_prefetch=1,
            grid=(1,),
            in_specs=[
                pl.BlockSpec(window.shape, lambda i, s: (0, 0, 0, 0)),
                pl.BlockSpec(conf.shape, lambda i, s: (0, 0, 0)),
            ],
            out_specs=pl.BlockSpec((2, 8, 256), lambda i, s: (0, 0, 0)),
            scratch_shapes=[pltpu.VMEM((2, 128, 128), jnp.float32)]
            + [pltpu.VMEM((rows, 8, 256), jnp.float32)] * 4
            + [pltpu.VMEM((2, rows + 2 * GROUP, 8, 256), jnp.float32)],
        ),
        compiler_params=pltpu.CompilerParams(vmem_limit_bytes=40 * 1024 * 1024),
    )(place, window, conf)


def on_device(patches, prior_patches, blocks, dest, target, flows, valid, stiffness):
    first, second, third, fourth = tables()
    tile_count = lax.axis_size("tile")
    gz_index = lax.axis_index("gz")
    tile_index = lax.axis_index("tile")

    node_rows, node_cols = flows.shape[2:]
    spring = (stiffness * valid.astype(jnp.float32))[0]
    own_nodes = jnp.stack([jnp.concatenate([spring, flows[0, c]]) for c in range(2)]).astype(jnp.bfloat16)
    window = gather_springs(tile_count, own_nodes)

    shifted = from_behind(patches, "gz", 1)
    earlier = jnp.where(gz_index == 0, prior_patches[None], shifted)[0]
    owner_tile = dest[0, :, 0]
    wanted = target[0]
    own_blocks = blocks[0]
    block_count = own_blocks.shape[0]
    tile_ids = jnp.arange(tile_count, dtype=jnp.int32)
    slot_ids = jnp.arange(tile_count * CAP, dtype=jnp.int32)
    tile_hits = (owner_tile[:, None] == tile_ids[None, :]).astype(jnp.int32)
    slot_rank = jnp.sum((jnp.cumsum(tile_hits, axis=0) - tile_hits) * tile_hits, axis=1)
    slot_index = owner_tile * CAP + slot_rank
    slot_picks = slot_index[:, None] == slot_ids[None, :]
    requested = jnp.sum(jnp.where(slot_picks, wanted[:, None], 0), axis=0).reshape(tile_count, CAP)
    asked_rows = lax.all_to_all(requested, "tile", split_axis=0, concat_axis=0, tiled=True)
    outgoing = patch_spectra(asked_rows.reshape(-1), earlier, first, second)
    outgoing = outgoing.reshape(tile_count, CAP * WIRE, LANES)
    arrived = lax.all_to_all(outgoing, "tile", split_axis=0, concat_axis=0, tiled=True)
    block_spec = block_spectra(own_blocks, first, second)
    corr_maps, peaks = match(slot_index, arrived.reshape(tile_count * CAP, WIRE, LANES), block_spec, third, fourth)

    conf_window = gather_conf(tile_count, peaks, node_cols)
    place = jnp.stack([tile_index, gz_index // 2]).astype(jnp.int32)
    mine = relax(place, tile_count * node_rows, window, conf_window)
    mesh_nodes = spread_result(mine)[None]
    return (corr_maps[None], mesh_nodes)


def solution(mesh):
    return jax.shard_map(
        on_device,
        mesh=mesh,
        in_specs=(
            P("gz", "tile", None),
            P("tile", None),
            P("gz", "tile", None),
            P("gz", "tile", None),
            P("gz", "tile"),
            P("gz", None, "tile", None),
            P("gz", "tile", None),
            P("gz", "tile", None),
        ),
        out_specs=(P("gz", "tile", None), P("gz", None, "tile", None)),
        check_vma=False,
    )
```

```python
import functools

import jax
import jax.numpy as jnp
import ml_dtypes
import numpy as np
from jax import lax
from jax.experimental import pallas as pl
from jax.experimental.pallas import tpu as pltpu
from jax.sharding import PartitionSpec as P

P_SIZE = 160
PIX = 25600
CAP = 2
ITERS = 64
GROUP = 4
UNROLL = 8


def from_behind(value, axis, steps):
    count = lax.axis_size(axis)
    first, last = (max(0, -steps), min(count, count - steps))
    return lax.ppermute(value, axis, [(source, source + steps) for source in range(first, last)])


LANES = 128
HALF = 64
WIRE = 208
BATCH = 16


def tables():
    size = P_SIZE
    line = np.arange(size)
    angles = (np.outer(line, line) % size).astype(np.float32) * np.float32(2.0 * np.pi / size)
    rounded = lambda x: x.astype(ml_dtypes.bfloat16).astype(np.float32)
    cos_t, sin_t = rounded(np.cos(angles)), rounded(np.sin(angles))
    lane = np.arange(2 * LANES)
    column = HALF * (lane // LANES) + lane % HALF
    used = column <= size // 2
    column = np.where(used, column, 0)
    real = lane % LANES < HALF
    c, s = cos_t[:, column] * used, sin_t[:, column] * used
    first = np.zeros((2 * LANES, 4 * LANES), np.float32)
    first[:size, : 2 * LANES] = np.where(real, c, s)
    first[:size, 2 * LANES :] = np.where(real, -s, c)
    second = np.concatenate([cos_t, sin_t], axis=1)
    third = np.concatenate([cos_t, sin_t], axis=0)
    twice = np.where((column == 0) | (column == size // 2), 1.0, 2.0)
    fourth = np.zeros((4 * LANES, 2 * LANES), np.float32)
    fourth[: 2 * LANES, :size] = (np.where(real, c, -s) * twice).T
    fourth[2 * LANES :, :size] = (np.where(real, -s, -c) * twice).T
    return [jnp.asarray(x, jnp.bfloat16) for x in (first, second, third, fourth)]


def to_images(rows_ref, low_buf, high_buf):
    parts = PIX // 640
    chunk = lambda m: rows_ref[:, pl.ds(pl.multiple_of(640 * m, LANES), 640)].astype(jnp.float32)
    fold = lambda x: sum(x[:, LANES * k : LANES * k + LANES] for k in range(5))
    zero = jnp.zeros((BATCH, LANES), jnp.float32)
    sums = lax.fori_loop(0, parts, lambda m, t: t + fold(chunk(m)), zero)
    mean = jnp.sum(sums, axis=1, keepdims=True) * (1.0 / PIX)

    def square(m, t):
        x = chunk(m) - mean
        return t + fold(x * x)

    sums = lax.fori_loop(0, parts, square, zero)
    scale = lax.rsqrt(jnp.sum(sums, axis=1, keepdims=True) * (1.0 / PIX) + 1e-05)
    lane = lax.broadcasted_iota(jnp.int32, (BATCH, LANES), 1)

    def place(m, carry):
        x = (chunk(m) - mean) * scale
        t = [x[:, LANES * k : LANES * k + LANES] for k in range(5)]
        low = [
            t[0],
            pltpu.roll(jnp.where(lane < 32, t[2], t[1]), 96, 1),
            pltpu.roll(jnp.where(lane < 64, t[3], t[2]), 64, 1),
            pltpu.roll(jnp.where(lane < 96, t[4], t[3]), 32, 1),
        ]
        high = [t[1], pltpu.roll(t[2], 96, 1), pltpu.roll(t[3], 64, 1), pltpu.roll(t[4], 32, 1)]
        for k in range(4):
            at = pl.ds(4 * m + k, BATCH, stride=P_SIZE)
            low_buf[at, :] = low[k]
            high_buf[at, :] = high[k]
        return carry

    lax.fori_loop(0, parts, place, 0)


def image_spectrum(n, low_buf, high_buf, first_ref, second_ref):
    at = pl.ds(pl.multiple_of(P_SIZE * n, 8), P_SIZE)
    image = jnp.concatenate([low_buf[at, :], high_buf[at, :]], axis=1).astype(jnp.bfloat16)
    first = jnp.dot(image, first_ref[...], preferred_element_type=jnp.float32).astype(jnp.bfloat16)
    both = jnp.concatenate([first[:, : 2 * LANES], first[:, 2 * LANES :]], axis=0)
    return jnp.dot(second_ref[...], both, preferred_element_type=jnp.float32)


def block_kernel(rows_ref, first_ref, second_ref, out_ref, low_buf, high_buf):
    to_images(rows_ref, low_buf, high_buf)
    low_half = lax.broadcasted_iota(jnp.int32, (P_SIZE, LANES), 1) < HALF

    def image(n, carry):
        spec = image_spectrum(n, low_buf, high_buf, first_ref, second_ref)
        for h in range(2):
            x = spec[:, LANES * h : LANES * h + LANES]
            swapped = pltpu.roll(x, HALF, 1)
            out_ref[n, :, LANES * h : LANES * h + LANES] = jnp.where(low_half, x, swapped).astype(jnp.bfloat16)
            at = slice(LANES * (2 + h), LANES * (3 + h))
            out_ref[n, :, at] = jnp.where(low_half, swapped, -x).astype(jnp.bfloat16)
        return carry

    lax.fori_loop(0, BATCH, image, 0, unroll=UNROLL)


def block_spectra(rows, first, second):
    count = rows.shape[0]
    fixed = lambda x: pl.BlockSpec(x.shape, lambda i: (0, 0))
    return pl.pallas_call(
        block_kernel,
        out_shape=jax.ShapeDtypeStruct((count, P_SIZE, 4 * LANES), jnp.bfloat16),
        grid=(count // BATCH,),
        in_specs=[pl.BlockSpec((BATCH, PIX), lambda i: (i, 0)), fixed(first), fixed(second)],
        out_specs=pl.BlockSpec((BATCH, P_SIZE, 4 * LANES), lambda i: (i, 0, 0)),
        scratch_shapes=[pltpu.VMEM((BATCH * P_SIZE, LANES), jnp.float32)] * 2,
        compiler_params=pltpu.CompilerParams(vmem_limit_bytes=40 * 1024 * 1024),
        cost_estimate=pl.CostEstimate(flops=20_000_000_000, bytes_accessed=8_000_000, transcendentals=0),
    )(rows, first, second)


def patch_kernel(asked_ref, rows_ref, first_ref, second_ref, out_ref, low_buf, high_buf, wire_buf, sems):
    to_images(rows_ref, low_buf, high_buf)
    lane = lax.broadcasted_iota(jnp.int32, (8, LANES), 1) % HALF

    def image(n, carry):
        spec = image_spectrum(n, low_buf, high_buf, first_ref, second_ref)
        rest = [spec[8 * i : 8 * i + 8, LANES:] for i in range(20)]
        pieces = [spec[:, :LANES]]
        for i in range(5):
            pieces.append(sum(pltpu.roll(jnp.where(lane < 16, rest[5 * b + i], 0.0), 16 * b, 1) for b in range(4)))
        pieces.append(sum(pltpu.roll(jnp.where(lane == 16, rest[i], 0.0), (i + 112) % LANES, 1) for i in range(20)))
        wire_buf[n] = jnp.concatenate(pieces, axis=0).astype(jnp.bfloat16)
        return carry

    lax.fori_loop(0, BATCH, image, 0, unroll=UNROLL)
    copy = lambda s: pltpu.make_async_copy(wire_buf.at[asked_ref[s]], out_ref.at[s], sems.at[s])
    slots = out_ref.shape[0]

    def begin(s, carry):
        copy(s).start()
        return carry

    def finish(s, carry):
        copy(s).wait()
        return carry

    lax.fori_loop(0, slots, begin, 0)
    lax.fori_loop(0, slots, finish, 0)


def patch_spectra(asked, rows, first, second):
    slots = asked.shape[0]
    fixed = lambda x: pl.BlockSpec(x.shape, lambda i, s: (0, 0))
    return pl.pallas_call(
        patch_kernel,
        out_shape=jax.ShapeDtypeStruct((slots, WIRE, LANES), jnp.bfloat16),
        grid_spec=pltpu.PrefetchScalarGridSpec(
            num_scalar_prefetch=1,
            grid=(1,),
            in_specs=[fixed(rows), fixed(first), fixed(second)],
            out_specs=pl.BlockSpec(memory_space=pl.ANY),
            scratch_shapes=[pltpu.VMEM((BATCH * P_SIZE, LANES), jnp.float32)] * 2
            + [pltpu.VMEM((BATCH, WIRE, LANES), jnp.bfloat16), pltpu.SemaphoreType.DMA((slots,))],
        ),
        compiler_params=pltpu.CompilerParams(vmem_limit_bytes=40 * 1024 * 1024),
        cost_estimate=pl.CostEstimate(flops=10_000_000_000, bytes_accessed=8_000_000, transcendentals=0),
    )(asked, rows, first, second)


def match_kernel(slot_ref, wire_ref, block_ref, third_ref, fourth_ref, map_ref, peak_ref, low_buf, high_buf):
    step = pl.program_id(0)
    lane8 = lax.broadcasted_iota(jnp.int32, (8, LANES), 1) % HALF == 16

    def image(n, carry):
        wire = wire_ref[slot_ref[BATCH * step + n]].astype(jnp.float32)
        last = wire[200:208]
        rest = []
        for i in range(20):
            part = wire[160 + 8 * (i % 5) : 168 + 8 * (i % 5)]
            part = pltpu.roll(part, (LANES - 16 * (i // 5)) % LANES, 1)
            rest.append(jnp.where(lane8, pltpu.roll(last, (16 - i) % LANES, 1), part))
        cross = []
        for h, a in enumerate((wire[:P_SIZE], jnp.concatenate(rest, axis=0))):
            straight = block_ref[n, :, LANES * h : LANES * h + LANES].astype(jnp.float32)
            swapped = block_ref[n, :, LANES * (2 + h) : LANES * (3 + h)].astype(jnp.float32)
            cross.append((a * straight + pltpu.roll(a, HALF, 1) * swapped).astype(jnp.bfloat16))
        back = jnp.dot(third_ref[...], jnp.concatenate(cross, axis=1), preferred_element_type=jnp.float32)
        back = back.astype(jnp.bfloat16)
        back = jnp.concatenate([back[:P_SIZE], back[P_SIZE:]], axis=1)
        field = jnp.dot(back, fourth_ref[...], preferred_element_type=jnp.float32) * (1.0 / float(P_SIZE) ** 3)
        at = pl.ds(pl.multiple_of(P_SIZE * n, 8), P_SIZE)
        low_buf[at, :] = field[:, :LANES]
        high_buf[at, :] = field[:, LANES:]
        return carry

    lax.fori_loop(0, BATCH, image, 0, unroll=UNROLL)
    lane = lax.broadcasted_iota(jnp.int32, (BATCH, LANES), 1)

    def place(m, top):
        load = lambda buf, k: buf[pl.ds(4 * m + k, BATCH, stride=P_SIZE), :]
        low = [load(low_buf, 0)] + [pltpu.roll(load(low_buf, k), 32 * k, 1) for k in range(1, 4)]
        high = [load(high_buf, 0)] + [pltpu.roll(load(high_buf, k), 32 * k, 1) for k in range(1, 4)]
        tiles = [
            low[0],
            jnp.where(lane < 32, high[0], low[1]),
            jnp.where(lane < 32, low[1], jnp.where(lane < 64, high[1], low[2])),
            jnp.where(lane < 64, low[2], jnp.where(lane < 96, high[2], low[3])),
            jnp.where(lane < 96, low[3], high[3]),
        ]
        rows = jnp.concatenate(tiles, axis=1).astype(jnp.bfloat16)
        map_ref[:, pl.ds(pl.multiple_of(640 * m, LANES), 640)] = rows
        for tile in tiles:
            top = jnp.maximum(top, tile)
        return top

    top = lax.fori_loop(0, P_SIZE // 4, place, jnp.full((BATCH, LANES), -jnp.inf, jnp.float32))
    top = jnp.max(top, axis=1, keepdims=True).astype(jnp.bfloat16).astype(jnp.float32)
    peak_ref[...] = jnp.broadcast_to(top, (BATCH, LANES))


def match(slot_index, wire, block_spec, third, fourth):
    count = block_spec.shape[0]
    fixed = lambda x: pl.BlockSpec(x.shape, lambda i, s: (0,) * x.ndim)
    return pl.pallas_call(
        match_kernel,
        out_shape=(
            jax.ShapeDtypeStruct((count, PIX), jnp.bfloat16),
            jax.ShapeDtypeStruct((count, LANES), jnp.float32),
        ),
        grid_spec=pltpu.PrefetchScalarGridSpec(
            num_scalar_prefetch=1,
            grid=(count // BATCH,),
            in_specs=[
                fixed(wire),
                pl.BlockSpec((BATCH, P_SIZE, 4 * LANES), lambda i, s: (i, 0, 0)),
                fixed(third),
                fixed(fourth),
            ],
            out_specs=[
                pl.BlockSpec((BATCH, PIX), lambda i, s: (i, 0)),
                pl.BlockSpec((BATCH, LANES), lambda i, s: (i, 0)),
            ],
            scratch_shapes=[pltpu.VMEM((BATCH * P_SIZE, LANES), jnp.float32)] * 2,
        ),
        compiler_params=pltpu.CompilerParams(vmem_limit_bytes=48 * 1024 * 1024),
        cost_estimate=pl.CostEstimate(flops=20_000_000_000, bytes_accessed=10_000_000, transcendentals=0),
    )(slot_index, wire, block_spec, third, fourth)


MESH = pl.DeviceIdType.MESH
GZ = 8
REACH = 8


def group_barrier(peers):
    barrier = pltpu.get_barrier_semaphore()
    for peer in peers:
        pl.semaphore_signal(barrier, inc=1, device_id=peer, device_id_type=MESH)
    pl.semaphore_wait(barrier, len(peers))


def gz_peers():
    gz, tile = lax.axis_index("gz"), lax.axis_index("tile")
    return [(lax.rem(gz + d, GZ), tile) for d in range(1, GZ)]


def tile_peers(tile_count):
    gz, tile = lax.axis_index("gz"), lax.axis_index("tile")
    offsets = [e for k in range(1, REACH + 1) for e in (k, -k)]
    return offsets, [(gz, lax.rem(tile + e + tile_count, tile_count)) for e in offsets]


def exchange_gz(source_of, held, send, recv):
    gz = lax.axis_index("gz")
    copies = []
    for d, peer in enumerate(gz_peers()):
        copies.append(
            pltpu.make_async_remote_copy(
                src_ref=source_of(peer[0]), dst_ref=held.at[gz], send_sem=send.at[d], recv_sem=recv.at[d],
                device_id=peer, device_id_type=MESH,
            )
        )
    for copy in copies:
        copy.start()
    return copies


def exchange_tiles(tile_count, source, window, send, recv):
    offsets, peers = tile_peers(tile_count)
    copies = []
    for n, (e, peer) in enumerate(zip(offsets, peers)):
        copies.append(
            pltpu.make_async_remote_copy(
                src_ref=source, dst_ref=window.at[REACH - e], send_sem=send.at[n], recv_sem=recv.at[n],
                device_id=peer, device_id_type=MESH,
            )
        )
    for copy in copies:
        copy.start()
    return copies


def ask_kernel(tile_count, request_ref, own_ref, asked_ref, window_ref, held, local, send_r, recv_r, send_a, recv_a, send_b, recv_b):
    gz, tile = lax.axis_index("gz"), lax.axis_index("tile")
    others = [(gz, lax.rem(tile + d, tile_count)) for d in range(1, tile_count)]
    group_barrier(gz_peers() + others)
    copies = exchange_gz(lambda peer: own_ref.at[lax.rem(peer, 2)], held, send_a, recv_a)
    mine = pltpu.make_async_copy(own_ref.at[lax.rem(gz, 2)], held.at[gz], local.at[0])
    mine.start()
    requests = []
    for d, peer in enumerate(others):
        requests.append(
            pltpu.make_async_remote_copy(
                src_ref=request_ref.at[peer[1]], dst_ref=asked_ref.at[tile], send_sem=send_r.at[d],
                recv_sem=recv_r.at[d], device_id=peer, device_id_type=MESH,
            )
        )
        requests[-1].start()
    asked_ref[tile] = request_ref[tile]
    mine.wait()
    for copy in copies:
        copy.wait()
    copies = exchange_tiles(tile_count, held, window_ref, send_b, recv_b)
    mine = pltpu.make_async_copy(held, window_ref.at[REACH], local.at[1])
    mine.start()
    for copy in requests:
        copy.wait()
    mine.wait()
    for copy in copies:
        copy.wait()


def ask_and_gather(request, own):
    tile_count = request.shape[0]
    dma = lambda count: pltpu.SemaphoreType.DMA((count,))
    return pl.pallas_call(
        functools.partial(ask_kernel, tile_count),
        out_shape=(
            jax.ShapeDtypeStruct(request.shape, request.dtype),
            jax.ShapeDtypeStruct((2 * REACH + 1, GZ) + own.shape[1:], own.dtype),
        ),
        in_specs=[pl.BlockSpec(memory_space=pltpu.VMEM)] * 2,
        out_specs=(pl.BlockSpec(memory_space=pltpu.VMEM), pl.BlockSpec(memory_space=pl.ANY)),
        scratch_shapes=[
            pltpu.VMEM((GZ,) + own.shape[1:], own.dtype),
            dma(2),
            dma(tile_count - 1),
            dma(tile_count - 1),
            dma(GZ - 1),
            dma(GZ - 1),
            dma(2 * REACH),
            dma(2 * REACH),
        ],
        compiler_params=pltpu.CompilerParams(collective_id=1, has_side_effects=True),
        cost_estimate=pl.CostEstimate(flops=0, bytes_accessed=32 * 1024 * 1024, transcendentals=0),
    )(request, own)


def conf_kernel(tile_count, peak_ref, window_ref, own_ref, held, packed, send_a, recv_a, send_b, recv_b):
    gz = lax.axis_index("gz")
    count, columns = peak_ref.shape[0], own_ref.shape[1]
    peak = jnp.concatenate([peak_ref[...]] * (columns // LANES), axis=1)
    half = columns // 2
    block = lax.rem(lax.broadcasted_iota(jnp.int32, (count, columns), 1), half) // (half // count)
    mine = block == lax.broadcasted_iota(jnp.int32, (count, columns), 0)
    confidence = jnp.sum(jnp.where(mine, peak / (1.0 + peak), 0.0), axis=0, keepdims=True)
    own_ref[...] = jnp.broadcast_to(confidence, own_ref.shape)
    group_barrier(gz_peers() + tile_peers(tile_count)[1])
    copies = exchange_gz(lambda peer: own_ref, held, send_a, recv_a)
    held[gz] = own_ref[...]
    for copy in copies:
        copy.wait()
    for s in range(GZ):
        packed[s : s + 1, :] = held[s, 0:1, :]
    copies = exchange_tiles(tile_count, packed, window_ref, send_b, recv_b)
    window_ref[REACH] = packed[...]
    for copy in copies:
        copy.wait()


def gather_conf(tile_count, peaks, columns):
    own = jax.ShapeDtypeStruct((8, columns), jnp.float32)
    return pl.pallas_call(
        functools.partial(conf_kernel, tile_count),
        out_shape=jax.ShapeDtypeStruct((2 * REACH + 1,) + own.shape, own.dtype),
        in_specs=[pl.BlockSpec(memory_space=pltpu.VMEM)],
        out_specs=pl.BlockSpec(memory_space=pltpu.VMEM),
        scratch_shapes=[
            pltpu.VMEM(own.shape, own.dtype),
            pltpu.VMEM((GZ,) + own.shape, own.dtype),
            pltpu.VMEM(own.shape, own.dtype),
            pltpu.SemaphoreType.DMA((GZ - 1,)),
            pltpu.SemaphoreType.DMA((GZ - 1,)),
            pltpu.SemaphoreType.DMA((2 * REACH,)),
            pltpu.SemaphoreType.DMA((2 * REACH,)),
        ],
        compiler_params=pltpu.CompilerParams(collective_id=2, has_side_effects=True),
    )(peaks)


def spread_kernel(own_ref, out_ref, source, held, send, recv):
    gz = lax.axis_index("gz")
    group_barrier(gz_peers())
    for s in range(GZ):
        for r in range(2):
            source[s, r : r + 1, :] = own_ref[r, s : s + 1, :]
    copies = exchange_gz(lambda peer: source.at[peer], held, send, recv)
    held[gz] = source[gz]
    for copy in copies:
        copy.wait()
    columns = own_ref.shape[2]
    order = lax.broadcasted_iota(jnp.int32, (columns, columns), 1)
    order = order // 2 + lax.rem(order, 2) * (columns // 2)
    spot = lax.broadcasted_iota(jnp.int32, (columns, columns), 0) == order
    pick = jnp.where(spot, 1.0, 0.0).astype(jnp.bfloat16)
    rest = jnp.concatenate([held[2 * h + c, 0:2, :] for c in range(2) for h in range(4)], axis=0)
    total = jnp.zeros_like(rest)
    for _ in range(3):
        part = rest.astype(jnp.bfloat16)
        rest = rest - part.astype(jnp.float32)
        total = total + jnp.dot(part, pick, preferred_element_type=jnp.float32)
    out_ref[0] = total[:8]
    out_ref[1] = total[8:]


def spread_result(own):
    columns = own.shape[-1]
    return pl.pallas_call(
        spread_kernel,
        out_shape=jax.ShapeDtypeStruct((2, 8, columns), own.dtype),
        in_specs=[pl.BlockSpec(memory_space=pltpu.VMEM)],
        out_specs=pl.BlockSpec(memory_space=pltpu.VMEM),
        scratch_shapes=[
            pltpu.VMEM((GZ, 8, columns), own.dtype),
            pltpu.VMEM((GZ, 8, columns), own.dtype),
            pltpu.SemaphoreType.DMA((GZ - 1,)),
            pltpu.SemaphoreType.DMA((GZ - 1,)),
        ],
        compiler_params=pltpu.CompilerParams(collective_id=3, has_side_effects=True),
    )(own)


FRONT = 32
SPAN = 8 * (2 * REACH + 1)


def relax_kernel(total, place_ref, window_ref, conf_ref, out_ref, s_buf, w_buf, f_buf, u_buf):
    tile, part = place_ref[0], place_ref[1]
    first_slot = jnp.maximum(REACH - tile, 0)
    last_slot = jnp.minimum(REACH + total // 8 - tile, 2 * REACH + 1)
    lane = lax.broadcasted_iota(jnp.int32, (1, 8, 128), 2)
    first_lane, last_lane = lane == 0, lane == 127
    section = lax.broadcasted_iota(jnp.int32, (8, 256), 0)
    for buf in (w_buf, f_buf, u_buf):
        buf[...] = jnp.zeros_like(buf)

    def picked(j):
        return jnp.concatenate([s_buf[h, pl.ds(j, 8, stride=16), :] for h in range(2)], axis=1)

    def prepare(k, carry):
        conf = jnp.where(section == 0, 0.0, 0.15 * conf_ref[k])
        nodes = window_ref[k].astype(jnp.float32).reshape(128, 256)
        s_buf[0], s_buf[1] = nodes[:, :128], nodes[:, 128:]
        for j in range(8):
            i = FRONT + 8 * k + j
            w = picked(j) * conf
            wf = w * picked(8 + j)
            w_buf[i] = w
            f_buf[i] = wf
            u_buf[0, i] = wf - pltpu.roll(wf, 7, 0)
        return carry

    lax.fori_loop(first_slot, last_slot, prepare, 0)

    def step(source, target, s):
        low = jnp.maximum((2 * part + s) // 8, first_slot)
        high = jnp.minimum((130 + 2 * part - s + 7) // 8, last_slot)
        count = (high - low + GROUP - 1) // GROUP
        low = jnp.where(tile < REACH, low, high - count * GROUP)

        def group(g, carry):
            i = FRONT + 8 * low + 8 * GROUP * g
            rows = 8 * GROUP
            even, odd = [u_buf[source, pl.ds(i - 1, rows + 2), :, 128 * h : 128 * h + 128] for h in range(2)]
            to_left = jnp.where(first_lane, 0.0, pltpu.roll(odd[1:-1], 1, 2))
            to_right = jnp.where(last_lane, 0.0, pltpu.roll(even[1:-1], 127, 2))
            for h, (x, beside, other) in enumerate(((even, odd[1:-1], to_left), (odd, even[1:-1], to_right))):
                at = (pl.ds(i, rows), slice(None), slice(128 * h, 128 * h + 128))
                mid = x[1:-1]
                around = (x[:-2] + x[2:]) + (beside + other)
                force = w_buf[at] * (pltpu.roll(mid, 1, 1) - mid) + f_buf[at]
                new = (0.4 * mid + 0.15 * around) + (force - pltpu.roll(force, 7, 1))
                u_buf[target, pl.ds(i, rows), :, 128 * h : 128 * h + 128] = new
            return carry

        lax.fori_loop(0, count, group, 0)

    def pair(k, carry):
        step(0, 1, 2 * k + 2)
        step(1, 0, 2 * k + 3)
        return carry

    lax.fori_loop(0, (ITERS - 2) // 2, pair, 0)
    step(0, 1, ITERS)
    out_ref[...] = u_buf[1, pl.ds(FRONT + 8 * REACH + 2 * part, 2)]


def relax(place, total, window, conf):
    rows = SPAN + 2 * FRONT
    return pl.pallas_call(
        functools.partial(relax_kernel, total),
        out_shape=jax.ShapeDtypeStruct((2, 8, 256), jnp.float32),
        grid_spec=pltpu.PrefetchScalarGridSpec(
            num_scalar_prefetch=1,
            grid=(1,),
            in_specs=[
                pl.BlockSpec(window.shape, lambda i, s: (0, 0, 0, 0)),
                pl.BlockSpec(conf.shape, lambda i, s: (0, 0, 0)),
            ],
            out_specs=pl.BlockSpec((2, 8, 256), lambda i, s: (0, 0, 0)),
            scratch_shapes=[pltpu.VMEM((2, 128, 128), jnp.float32)]
            + [pltpu.VMEM((rows, 8, 256), jnp.float32)] * 2
            + [pltpu.VMEM((2, rows, 8, 256), jnp.float32)],
        ),
        compiler_params=pltpu.CompilerParams(vmem_limit_bytes=40 * 1024 * 1024),
    )(place, window, conf)


def on_device(patches, prior_patches, blocks, dest, target, flows, valid, stiffness):
    first, second, third, fourth = tables()
    tile_count = lax.axis_size("tile")
    gz_index = lax.axis_index("gz")
    tile_index = lax.axis_index("tile")

    node_rows, node_cols = flows.shape[2:]
    spring = (stiffness * valid.astype(jnp.float32))[0]
    own_nodes = jnp.stack([jnp.concatenate([spring, flows[0, c]]) for c in range(2)])
    own_nodes = jnp.concatenate([own_nodes[..., 0::2], own_nodes[..., 1::2]], axis=-1).astype(jnp.bfloat16)

    shifted = from_behind(patches, "gz", 1)
    earlier = jnp.where(gz_index == 0, prior_patches[None], shifted)[0]
    owner_tile = dest[0, :, 0]
    wanted = target[0]
    own_blocks = blocks[0]
    block_ids = jnp.arange(own_blocks.shape[0], dtype=jnp.int32)
    slot_ids = jnp.arange(tile_count * CAP, dtype=jnp.int32)
    before = (owner_tile[:, None] == owner_tile[None, :]) & (block_ids[None, :] < block_ids[:, None])
    slot_index = owner_tile * CAP + jnp.sum(before.astype(jnp.int32), axis=1)
    slot_picks = slot_index[:, None] == slot_ids[None, :]
    requested = jnp.sum(jnp.where(slot_picks, wanted[:, None], 0), axis=0).reshape(tile_count, 1, CAP)
    request = jnp.pad(requested, ((0, 0), (0, 7), (0, LANES - CAP)))
    asked, window = ask_and_gather(request, own_nodes)
    asked_rows = asked[:, 0, :CAP]
    outgoing = patch_spectra(asked_rows.reshape(-1), earlier, first, second)
    outgoing = outgoing.reshape(tile_count, CAP * WIRE, LANES)
    arrived = lax.all_to_all(outgoing, "tile", split_axis=0, concat_axis=0, tiled=True)
    block_spec = block_spectra(own_blocks, first, second)
    corr_maps, peaks = match(slot_index, arrived.reshape(tile_count * CAP, WIRE, LANES), block_spec, third, fourth)

    conf_window = gather_conf(tile_count, peaks, node_cols)
    place = jnp.stack([tile_index, gz_index // 2]).astype(jnp.int32)
    mine = relax(place, tile_count * node_rows, window, conf_window)
    mesh_nodes = spread_result(mine)[None]
    return (corr_maps[None], mesh_nodes)


def solution(mesh):
    return jax.shard_map(
        on_device,
        mesh=mesh,
        in_specs=(
            P("gz", "tile", None),
            P("tile", None),
            P("gz", "tile", None),
            P("gz", "tile", None),
            P("gz", "tile"),
            P("gz", None, "tile", None),
            P("gz", "tile", None),
            P("gz", "tile", None),
        ),
        out_specs=(P("gz", "tile", None), P("gz", None, "tile", None)),
        check_vma=False,
    )
```

```python
import functools

import jax
import jax.numpy as jnp
import ml_dtypes
import numpy as np
from jax import lax
from jax.experimental import pallas as pl
from jax.experimental.pallas import tpu as pltpu
from jax.sharding import PartitionSpec as P

P_SIZE = 160
PIX = 25600
CAP = 2
ITERS = 64
GROUP = 4
UNROLL = 8


LANES = 128
HALF = 64
WIRE = 208
BATCH = 16


def tables():
    size = P_SIZE
    line = np.arange(size)
    angles = (np.outer(line, line) % size).astype(np.float32) * np.float32(2.0 * np.pi / size)
    rounded = lambda x: x.astype(ml_dtypes.bfloat16).astype(np.float32)
    cos_t, sin_t = rounded(np.cos(angles)), rounded(np.sin(angles))
    lane = np.arange(2 * LANES)
    column = HALF * (lane // LANES) + lane % HALF
    used = column <= size // 2
    column = np.where(used, column, 0)
    real = lane % LANES < HALF
    c, s = cos_t[:, column] * used, sin_t[:, column] * used
    first = np.zeros((2 * LANES, 4 * LANES), np.float32)
    first[:size, : 2 * LANES] = np.where(real, c, s)
    first[:size, 2 * LANES :] = np.where(real, -s, c)
    second = np.concatenate([cos_t, sin_t], axis=1)
    third = np.concatenate([cos_t, sin_t], axis=0)
    twice = np.where((column == 0) | (column == size // 2), 1.0, 2.0)
    fourth = np.zeros((4 * LANES, 2 * LANES), np.float32)
    fourth[: 2 * LANES, :size] = (np.where(real, c, -s) * twice).T
    fourth[2 * LANES :, :size] = (np.where(real, -s, -c) * twice).T
    return [jnp.asarray(x, jnp.bfloat16) for x in (first, second, third, fourth)]


def to_images(rows_ref, low_buf, high_buf):
    parts = PIX // 640
    chunk = lambda m: rows_ref[:, pl.ds(pl.multiple_of(640 * m, LANES), 640)].astype(jnp.float32)
    fold = lambda x: sum(x[:, LANES * k : LANES * k + LANES] for k in range(5))
    zero = jnp.zeros((BATCH, LANES), jnp.float32)
    sums = lax.fori_loop(0, parts, lambda m, t: t + fold(chunk(m)), zero)
    mean = jnp.sum(sums, axis=1, keepdims=True) * (1.0 / PIX)

    def square(m, t):
        x = chunk(m) - mean
        return t + fold(x * x)

    sums = lax.fori_loop(0, parts, square, zero)
    scale = lax.rsqrt(jnp.sum(sums, axis=1, keepdims=True) * (1.0 / PIX) + 1e-05)
    lane = lax.broadcasted_iota(jnp.int32, (BATCH, LANES), 1)

    def place(m, carry):
        x = (chunk(m) - mean) * scale
        t = [x[:, LANES * k : LANES * k + LANES] for k in range(5)]
        low = [
            t[0],
            pltpu.roll(jnp.where(lane < 32, t[2], t[1]), 96, 1),
            pltpu.roll(jnp.where(lane < 64, t[3], t[2]), 64, 1),
            pltpu.roll(jnp.where(lane < 96, t[4], t[3]), 32, 1),
        ]
        high = [t[1], pltpu.roll(t[2], 96, 1), pltpu.roll(t[3], 64, 1), pltpu.roll(t[4], 32, 1)]
        for k in range(4):
            at = pl.ds(4 * m + k, BATCH, stride=P_SIZE)
            low_buf[at, :] = low[k]
            high_buf[at, :] = high[k]
        return carry

    lax.fori_loop(0, parts, place, 0)


def image_spectrum(n, low_buf, high_buf, first_ref, second_ref):
    at = pl.ds(pl.multiple_of(P_SIZE * n, 8), P_SIZE)
    image = jnp.concatenate([low_buf[at, :], high_buf[at, :]], axis=1).astype(jnp.bfloat16)
    first = jnp.dot(image, first_ref[...], preferred_element_type=jnp.float32).astype(jnp.bfloat16)
    both = jnp.concatenate([first[:, : 2 * LANES], first[:, 2 * LANES :]], axis=0)
    return jnp.dot(second_ref[...], both, preferred_element_type=jnp.float32)


def block_batch(low_buf, high_buf, first_ref, second_ref, out_ref):
    low_half = lax.broadcasted_iota(jnp.int32, (P_SIZE, LANES), 1) < HALF

    def image(n, carry):
        spec = image_spectrum(n, low_buf, high_buf, first_ref, second_ref)
        for h in range(2):
            x = spec[:, LANES * h : LANES * h + LANES]
            swapped = pltpu.roll(x, HALF, 1)
            out_ref[n, :, LANES * h : LANES * h + LANES] = jnp.where(low_half, x, swapped).astype(jnp.bfloat16)
            at = slice(LANES * (2 + h), LANES * (3 + h))
            out_ref[n, :, at] = jnp.where(low_half, swapped, -x).astype(jnp.bfloat16)
        return carry

    lax.fori_loop(0, BATCH, image, 0, unroll=UNROLL)


def patch_batch(low_buf, high_buf, first_ref, second_ref, wire_buf):
    lane = lax.broadcasted_iota(jnp.int32, (8, LANES), 1) % HALF

    def image(n, carry):
        spec = image_spectrum(n, low_buf, high_buf, first_ref, second_ref)
        rest = [spec[8 * i : 8 * i + 8, LANES:] for i in range(20)]
        pieces = [spec[:, :LANES]]
        for i in range(5):
            pieces.append(sum(pltpu.roll(jnp.where(lane < 16, rest[5 * b + i], 0.0), 16 * b, 1) for b in range(4)))
        pieces.append(sum(pltpu.roll(jnp.where(lane == 16, rest[i], 0.0), (i + 112) % LANES, 1) for i in range(20)))
        wire_buf[n] = jnp.concatenate(pieces, axis=0).astype(jnp.bfloat16)
        return carry

    lax.fori_loop(0, BATCH, image, 0, unroll=UNROLL)


def match_kernel(slot_ref, wire_ref, block_ref, third_ref, fourth_ref, map_ref, peak_ref, low_buf, high_buf):
    step = pl.program_id(0)
    lane8 = lax.broadcasted_iota(jnp.int32, (8, LANES), 1) % HALF == 16

    def image(n, carry):
        wire = wire_ref[slot_ref[BATCH * step + n]].astype(jnp.float32)
        last = wire[200:208]
        rest = []
        for i in range(20):
            part = wire[160 + 8 * (i % 5) : 168 + 8 * (i % 5)]
            part = pltpu.roll(part, (LANES - 16 * (i // 5)) % LANES, 1)
            rest.append(jnp.where(lane8, pltpu.roll(last, (16 - i) % LANES, 1), part))
        cross = []
        for h, a in enumerate((wire[:P_SIZE], jnp.concatenate(rest, axis=0))):
            straight = block_ref[n, :, LANES * h : LANES * h + LANES].astype(jnp.float32)
            swapped = block_ref[n, :, LANES * (2 + h) : LANES * (3 + h)].astype(jnp.float32)
            cross.append((a * straight + pltpu.roll(a, HALF, 1) * swapped).astype(jnp.bfloat16))
        back = jnp.dot(third_ref[...], jnp.concatenate(cross, axis=1), preferred_element_type=jnp.float32)
        back = back.astype(jnp.bfloat16)
        back = jnp.concatenate([back[:P_SIZE], back[P_SIZE:]], axis=1)
        field = jnp.dot(back, fourth_ref[...], preferred_element_type=jnp.float32) * (1.0 / float(P_SIZE) ** 3)
        at = pl.ds(pl.multiple_of(P_SIZE * n, 8), P_SIZE)
        low_buf[at, :] = field[:, :LANES]
        high_buf[at, :] = field[:, LANES:]
        return carry

    lax.fori_loop(0, BATCH, image, 0, unroll=UNROLL)
    lane = lax.broadcasted_iota(jnp.int32, (BATCH, LANES), 1)

    def place(m, top):
        load = lambda buf, k: buf[pl.ds(4 * m + k, BATCH, stride=P_SIZE), :]
        low = [load(low_buf, 0)] + [pltpu.roll(load(low_buf, k), 32 * k, 1) for k in range(1, 4)]
        high = [load(high_buf, 0)] + [pltpu.roll(load(high_buf, k), 32 * k, 1) for k in range(1, 4)]
        tiles = [
            low[0],
            jnp.where(lane < 32, high[0], low[1]),
            jnp.where(lane < 32, low[1], jnp.where(lane < 64, high[1], low[2])),
            jnp.where(lane < 64, low[2], jnp.where(lane < 96, high[2], low[3])),
            jnp.where(lane < 96, low[3], high[3]),
        ]
        rows = jnp.concatenate(tiles, axis=1).astype(jnp.bfloat16)
        map_ref[:, pl.ds(pl.multiple_of(640 * m, LANES), 640)] = rows
        for tile in tiles:
            top = jnp.maximum(top, tile)
        return top

    top = lax.fori_loop(0, P_SIZE // 4, place, jnp.full((BATCH, LANES), -jnp.inf, jnp.float32))
    top = jnp.max(top, axis=1, keepdims=True).astype(jnp.bfloat16).astype(jnp.float32)
    peak_ref[...] = jnp.broadcast_to(top, (BATCH, LANES))


def match(slot_index, wire, block_spec, third, fourth):
    count = block_spec.shape[0]
    fixed = lambda x: pl.BlockSpec(x.shape, lambda i, s: (0,) * x.ndim)
    return pl.pallas_call(
        match_kernel,
        out_shape=(
            jax.ShapeDtypeStruct((count, PIX), jnp.bfloat16),
            jax.ShapeDtypeStruct((count, LANES), jnp.float32),
        ),
        grid_spec=pltpu.PrefetchScalarGridSpec(
            num_scalar_prefetch=1,
            grid=(count // BATCH,),
            in_specs=[
                fixed(wire),
                pl.BlockSpec((BATCH, P_SIZE, 4 * LANES), lambda i, s: (i, 0, 0)),
                fixed(third),
                fixed(fourth),
            ],
            out_specs=[
                pl.BlockSpec((BATCH, PIX), lambda i, s: (i, 0)),
                pl.BlockSpec((BATCH, LANES), lambda i, s: (i, 0)),
            ],
            scratch_shapes=[pltpu.VMEM((BATCH * P_SIZE, LANES), jnp.float32)] * 2,
        ),
        compiler_params=pltpu.CompilerParams(vmem_limit_bytes=48 * 1024 * 1024),
        cost_estimate=pl.CostEstimate(flops=20_000_000_000, bytes_accessed=10_000_000, transcendentals=0),
    )(slot_index, wire, block_spec, third, fourth)


MESH = pl.DeviceIdType.MESH
GZ = 8
REACH = 8


def group_barrier(peers):
    barrier = pltpu.get_barrier_semaphore()
    for peer in peers:
        pl.semaphore_signal(barrier, inc=1, device_id=peer, device_id_type=MESH)
    pl.semaphore_wait(barrier, len(peers))


def gz_peers():
    gz, tile = lax.axis_index("gz"), lax.axis_index("tile")
    return [(lax.rem(gz + d, GZ), tile) for d in range(1, GZ)]


def tile_peers(tile_count):
    gz, tile = lax.axis_index("gz"), lax.axis_index("tile")
    offsets = [e for k in range(1, REACH + 1) for e in (k, -k)]
    return offsets, [(gz, lax.rem(tile + e + tile_count, tile_count)) for e in offsets]


def exchange_gz(source_of, held, send, recv):
    gz = lax.axis_index("gz")
    copies = []
    for d, peer in enumerate(gz_peers()):
        copies.append(
            pltpu.make_async_remote_copy(
                src_ref=source_of(peer[0]), dst_ref=held.at[gz], send_sem=send.at[d], recv_sem=recv.at[d],
                device_id=peer, device_id_type=MESH,
            )
        )
    for copy in copies:
        copy.start()
    return copies


def exchange_tiles(tile_count, source, window, send, recv):
    offsets, peers = tile_peers(tile_count)
    copies = []
    for n, (e, peer) in enumerate(zip(offsets, peers)):
        copies.append(
            pltpu.make_async_remote_copy(
                src_ref=source, dst_ref=window.at[REACH - e], send_sem=send.at[n], recv_sem=recv.at[n],
                device_id=peer, device_id_type=MESH,
            )
        )
    for copy in copies:
        copy.start()
    return copies


def request_rows(owner_col, owner_row, wanted_row, tile_count):
    count = owner_col.shape[0]
    earlier = lax.broadcasted_iota(jnp.int32, (count, count), 0) < lax.broadcasted_iota(jnp.int32, (count, count), 1)
    rank = jnp.sum(jnp.where(earlier & (owner_col == owner_row), 1, 0), axis=0, keepdims=True)
    hit = owner_row == lax.broadcasted_iota(jnp.int32, (tile_count, count), 0)
    lane = lax.broadcasted_iota(jnp.int32, (tile_count, LANES), 1)
    rows = jnp.zeros((tile_count, LANES), jnp.int32)
    for c in range(CAP):
        asked = jnp.sum(jnp.where(hit & (rank == c), wanted_row, 0), axis=1, keepdims=True)
        rows = jnp.where(lane == c, asked, rows)
    return rows


def trade_kernel(
    tile_count, patch_ref, prior_ref, block_ref, col_ref, row_ref, want_ref, flow_ref, valid_ref, stiff_ref, first_ref,
    second_ref, arrived_ref, spec_ref, window_ref, rows_buf, block_buf, low_buf, high_buf, wire_buf, send_buf, spec_buf,
    own_buf, held, ask_buf, heard_buf, list_buf, told_buf, told_smem, local, send_r, recv_r, send_a, recv_a, send_b,
    recv_b, send_f, recv_f, send_p, recv_p,
):
    gz, tile = lax.axis_index("gz"), lax.axis_index("tile")
    after, before = lax.rem(gz + 1, GZ), lax.rem(gz + GZ - 1, GZ)
    barrier = pltpu.get_barrier_semaphore()

    def greet(peer):
        pl.semaphore_signal(barrier, inc=1, device_id=peer, device_id_type=MESH)

    def greet_tiles(d, carry):
        peer = lax.rem(tile + d, tile_count)
        greet((after, peer))
        greet((before, peer))

        @pl.when(d > 0)
        def _():
            greet((gz, peer))

        return carry

    lax.fori_loop(0, tile_count, greet_tiles, 0)
    for d in range(2, GZ - 1):
        greet((lax.rem(gz + d, GZ), tile))

    from_prior = pltpu.make_async_copy(prior_ref, rows_buf, local.at[0])
    from_patches = pltpu.make_async_copy(patch_ref.at[0], rows_buf, local.at[0])
    load_blocks = pltpu.make_async_copy(block_ref.at[0], block_buf, local.at[1])

    @pl.when(gz == GZ - 1)
    def _():
        from_prior.start()

    @pl.when(gz != GZ - 1)
    def _():
        from_patches.start()

    load_blocks.start()

    rows = request_rows(col_ref[...], row_ref[...], want_ref[...], tile_count)
    for j in range(8):
        ask_buf[pl.ds(j, tile_count, stride=8), :] = rows
    columns = stiff_ref.shape[2]
    lane = lax.broadcasted_iota(jnp.int32, (columns, columns), 1)
    order = 2 * lax.rem(lane, columns // 2) + lane // (columns // 2)
    pick = jnp.where(lax.broadcasted_iota(jnp.int32, (columns, columns), 0) == order, 1.0, 0.0).astype(jnp.bfloat16)
    spring = stiff_ref[0] * valid_ref[0].astype(jnp.float32)
    for c in range(2):
        nodes = jnp.concatenate([spring, flow_ref[0, c]], axis=0).astype(jnp.bfloat16)
        own_buf[c] = jnp.dot(nodes, pick, preferred_element_type=jnp.float32).astype(jnp.bfloat16)

    pl.semaphore_wait(barrier, 3 * tile_count - 1 + GZ - 3)

    springs = exchange_gz(lambda peer: own_buf.at[lax.rem(peer, 2)], held, send_a, recv_a)
    mine = pltpu.make_async_copy(own_buf.at[lax.rem(gz, 2)], held.at[gz], local.at[2])
    mine.start()

    def request(d):
        peer = lax.rem(tile + d, tile_count)
        part = lambda t: pl.ds(pl.multiple_of(8 * t, 8), 8)
        return pltpu.make_async_remote_copy(
            src_ref=ask_buf.at[part(peer)], dst_ref=heard_buf.at[part(tile)], send_sem=send_r.at[d],
            recv_sem=recv_r.at[d], device_id=(gz, peer), device_id_type=MESH,
        )

    def each(first, last, act):
        def body(d, carry):
            act(d)
            return carry

        lax.fori_loop(first, last, body, 0)

    each(1, tile_count, lambda d: request(d).start())
    own_part = pl.ds(pl.multiple_of(8 * tile, 8), 8)
    heard_buf[own_part, :] = ask_buf[own_part, :]

    @pl.when(gz == GZ - 1)
    def _():
        from_prior.wait()

    @pl.when(gz != GZ - 1)
    def _():
        from_patches.wait()

    to_images(rows_buf, low_buf, high_buf)

    mine.wait()
    for copy in springs:
        copy.wait()
    springs = exchange_tiles(tile_count, held, window_ref, send_b, recv_b)
    mine = pltpu.make_async_copy(held, window_ref.at[REACH], local.at[2])
    mine.start()
    each(1, tile_count, lambda d: request(d).wait())
    list_buf[...] = heard_buf[pl.ds(0, tile_count, stride=8), :]
    forward = pltpu.make_async_remote_copy(
        src_ref=list_buf, dst_ref=told_buf, send_sem=send_f.at[0], recv_sem=recv_f.at[0], device_id=(before, tile),
        device_id_type=MESH,
    )
    forward.start()
    patch_batch(low_buf, high_buf, first_ref, second_ref, wire_buf)
    forward.wait()
    told = pltpu.make_async_copy(told_buf, told_smem, local.at[3])
    told.start()
    told.wait()

    def parcel(d):
        peer = lax.rem(tile + d, tile_count)
        return pltpu.make_async_remote_copy(
            src_ref=send_buf.at[peer], dst_ref=arrived_ref.at[tile], send_sem=send_p.at[d], recv_sem=recv_p.at[d],
            device_id=(after, peer), device_id_type=MESH,
        )

    def post(d):
        peer = lax.rem(tile + d, tile_count)
        for c in range(CAP):
            send_buf[peer, WIRE * c : WIRE * c + WIRE, :] = wire_buf[told_smem[peer, c]]
        parcel(d).start()

    each(0, tile_count, post)

    load_blocks.wait()
    stores = []
    for half in range(2):
        to_images(block_buf.at[pl.ds(BATCH * half, BATCH)], low_buf, high_buf)
        block_batch(low_buf, high_buf, first_ref, second_ref, spec_buf.at[pl.ds(BATCH * half, BATCH)])
        part = pl.ds(BATCH * half, BATCH)
        stores.append(pltpu.make_async_copy(spec_buf.at[part], spec_ref.at[part], local.at[4 + half]))
        stores[-1].start()

    mine.wait()
    for copy in springs + stores:
        copy.wait()
    each(0, tile_count, lambda d: parcel(d).wait())


def trade(tile_count, patches, prior, blocks, col, row, want, flows, valid, stiffness, first, second):
    count = blocks.shape[1]
    columns = flows.shape[3]
    dma = lambda number: pltpu.SemaphoreType.DMA((number,))
    vmem, anywhere = pl.BlockSpec(memory_space=pltpu.VMEM), pl.BlockSpec(memory_space=pl.ANY)
    f32, bf16 = jnp.float32, jnp.bfloat16
    return pl.pallas_call(
        functools.partial(trade_kernel, tile_count),
        out_shape=(
            jax.ShapeDtypeStruct((tile_count, CAP * WIRE, LANES), bf16),
            jax.ShapeDtypeStruct((count, P_SIZE, 4 * LANES), bf16),
            jax.ShapeDtypeStruct((2 * REACH + 1, GZ, 16, columns), bf16),
        ),
        in_specs=[anywhere] * 3 + [vmem] * 8,
        out_specs=(anywhere,) * 3,
        scratch_shapes=[
            pltpu.VMEM((BATCH, PIX), bf16),
            pltpu.VMEM((count, PIX), bf16),
            pltpu.VMEM((BATCH * P_SIZE, LANES), f32),
            pltpu.VMEM((BATCH * P_SIZE, LANES), f32),
            pltpu.VMEM((BATCH, WIRE, LANES), bf16),
            pltpu.VMEM((tile_count, CAP * WIRE, LANES), bf16),
            pltpu.VMEM((count, P_SIZE, 4 * LANES), bf16),
            pltpu.VMEM((2, 16, columns), bf16),
            pltpu.VMEM((GZ, 16, columns), bf16),
            pltpu.VMEM((8 * tile_count, LANES), jnp.int32),
            pltpu.VMEM((8 * tile_count, LANES), jnp.int32),
            pltpu.VMEM((tile_count, LANES), jnp.int32),
            pltpu.VMEM((tile_count, LANES), jnp.int32),
            pltpu.SMEM((tile_count, LANES), jnp.int32),
            dma(6),
            dma(tile_count),
            dma(tile_count),
            dma(GZ - 1),
            dma(GZ - 1),
            dma(2 * REACH),
            dma(2 * REACH),
            dma(1),
            dma(1),
            dma(tile_count),
            dma(tile_count),
        ],
        compiler_params=pltpu.CompilerParams(
            collective_id=1, has_side_effects=True, vmem_limit_bytes=60 * 1024 * 1024
        ),
        cost_estimate=pl.CostEstimate(flops=30_000_000_000, bytes_accessed=32_000_000, transcendentals=0),
    )(patches, prior, blocks, col, row, want, flows, valid, stiffness, first, second)


def conf_kernel(tile_count, peak_ref, window_ref, own_ref, held, packed, send_a, recv_a, send_b, recv_b):
    gz = lax.axis_index("gz")
    count, columns = peak_ref.shape[0], own_ref.shape[1]
    peak = jnp.concatenate([peak_ref[...]] * (columns // LANES), axis=1)
    half = columns // 2
    block = lax.rem(lax.broadcasted_iota(jnp.int32, (count, columns), 1), half) // (half // count)
    mine = block == lax.broadcasted_iota(jnp.int32, (count, columns), 0)
    confidence = jnp.sum(jnp.where(mine, peak / (1.0 + peak), 0.0), axis=0, keepdims=True)
    own_ref[...] = jnp.broadcast_to(confidence, own_ref.shape)
    group_barrier(gz_peers() + tile_peers(tile_count)[1])
    copies = exchange_gz(lambda peer: own_ref, held, send_a, recv_a)
    held[gz] = own_ref[...]
    for copy in copies:
        copy.wait()
    for s in range(GZ):
        packed[s : s + 1, :] = held[s, 0:1, :]
    copies = exchange_tiles(tile_count, packed, window_ref, send_b, recv_b)
    window_ref[REACH] = packed[...]
    for copy in copies:
        copy.wait()


def gather_conf(tile_count, peaks, columns):
    own = jax.ShapeDtypeStruct((8, columns), jnp.float32)
    return pl.pallas_call(
        functools.partial(conf_kernel, tile_count),
        out_shape=jax.ShapeDtypeStruct((2 * REACH + 1,) + own.shape, own.dtype),
        in_specs=[pl.BlockSpec(memory_space=pltpu.VMEM)],
        out_specs=pl.BlockSpec(memory_space=pltpu.VMEM),
        scratch_shapes=[
            pltpu.VMEM(own.shape, own.dtype),
            pltpu.VMEM((GZ,) + own.shape, own.dtype),
            pltpu.VMEM(own.shape, own.dtype),
            pltpu.SemaphoreType.DMA((GZ - 1,)),
            pltpu.SemaphoreType.DMA((GZ - 1,)),
            pltpu.SemaphoreType.DMA((2 * REACH,)),
            pltpu.SemaphoreType.DMA((2 * REACH,)),
        ],
        compiler_params=pltpu.CompilerParams(collective_id=2, has_side_effects=True),
    )(peaks)


def spread_kernel(own_ref, out_ref, source, held, send, recv):
    gz = lax.axis_index("gz")
    group_barrier(gz_peers())
    for s in range(GZ):
        for r in range(2):
            source[s, r : r + 1, :] = own_ref[r, s : s + 1, :]
    copies = exchange_gz(lambda peer: source.at[peer], held, send, recv)
    held[gz] = source[gz]
    for copy in copies:
        copy.wait()
    columns = own_ref.shape[2]
    order = lax.broadcasted_iota(jnp.int32, (columns, columns), 1)
    order = order // 2 + lax.rem(order, 2) * (columns // 2)
    spot = lax.broadcasted_iota(jnp.int32, (columns, columns), 0) == order
    pick = jnp.where(spot, 1.0, 0.0).astype(jnp.bfloat16)
    rest = jnp.concatenate([held[2 * h + c, 0:2, :] for c in range(2) for h in range(4)], axis=0)
    total = jnp.zeros_like(rest)
    for _ in range(3):
        part = rest.astype(jnp.bfloat16)
        rest = rest - part.astype(jnp.float32)
        total = total + jnp.dot(part, pick, preferred_element_type=jnp.float32)
    out_ref[0] = total[:8]
    out_ref[1] = total[8:]


def spread_result(own):
    columns = own.shape[-1]
    return pl.pallas_call(
        spread_kernel,
        out_shape=jax.ShapeDtypeStruct((2, 8, columns), own.dtype),
        in_specs=[pl.BlockSpec(memory_space=pltpu.VMEM)],
        out_specs=pl.BlockSpec(memory_space=pltpu.VMEM),
        scratch_shapes=[
            pltpu.VMEM((GZ, 8, columns), own.dtype),
            pltpu.VMEM((GZ, 8, columns), own.dtype),
            pltpu.SemaphoreType.DMA((GZ - 1,)),
            pltpu.SemaphoreType.DMA((GZ - 1,)),
        ],
        compiler_params=pltpu.CompilerParams(collective_id=3, has_side_effects=True),
    )(own)


FRONT = 32
SPAN = 8 * (2 * REACH + 1)


def relax_kernel(total, place_ref, window_ref, conf_ref, out_ref, s_buf, w_buf, f_buf, u_buf):
    tile, part = place_ref[0], place_ref[1]
    first_slot = jnp.maximum(REACH - tile, 0)
    last_slot = jnp.minimum(REACH + total // 8 - tile, 2 * REACH + 1)
    lane = lax.broadcasted_iota(jnp.int32, (1, 8, 128), 2)
    first_lane, last_lane = lane == 0, lane == 127
    section = lax.broadcasted_iota(jnp.int32, (8, 256), 0)
    for buf in (w_buf, f_buf, u_buf):
        buf[...] = jnp.zeros_like(buf)

    def picked(j):
        return jnp.concatenate([s_buf[h, pl.ds(j, 8, stride=16), :] for h in range(2)], axis=1)

    def prepare(k, carry):
        conf = jnp.where(section == 0, 0.0, 0.15 * conf_ref[k])
        nodes = window_ref[k].astype(jnp.float32).reshape(128, 256)
        s_buf[0], s_buf[1] = nodes[:, :128], nodes[:, 128:]
        for j in range(8):
            i = FRONT + 8 * k + j
            w = picked(j) * conf
            wf = w * picked(8 + j)
            w_buf[i] = w
            f_buf[i] = wf
            u_buf[0, i] = wf - pltpu.roll(wf, 7, 0)
        return carry

    lax.fori_loop(first_slot, last_slot, prepare, 0)

    def step(source, target, s):
        low = jnp.maximum((2 * part + s) // 8, first_slot)
        high = jnp.minimum((130 + 2 * part - s + 7) // 8, last_slot)
        count = (high - low + GROUP - 1) // GROUP
        low = jnp.where(tile < REACH, low, high - count * GROUP)

        def group(g, carry):
            i = FRONT + 8 * low + 8 * GROUP * g
            rows = 8 * GROUP
            even, odd = [u_buf[source, pl.ds(i - 1, rows + 2), :, 128 * h : 128 * h + 128] for h in range(2)]
            to_left = jnp.where(first_lane, 0.0, pltpu.roll(odd[1:-1], 1, 2))
            to_right = jnp.where(last_lane, 0.0, pltpu.roll(even[1:-1], 127, 2))
            for h, (x, beside, other) in enumerate(((even, odd[1:-1], to_left), (odd, even[1:-1], to_right))):
                at = (pl.ds(i, rows), slice(None), slice(128 * h, 128 * h + 128))
                mid = x[1:-1]
                around = (x[:-2] + x[2:]) + (beside + other)
                force = w_buf[at] * (pltpu.roll(mid, 1, 1) - mid) + f_buf[at]
                new = (0.4 * mid + 0.15 * around) + (force - pltpu.roll(force, 7, 1))
                u_buf[target, pl.ds(i, rows), :, 128 * h : 128 * h + 128] = new
            return carry

        lax.fori_loop(0, count, group, 0)

    def pair(k, carry):
        step(0, 1, 2 * k + 2)
        step(1, 0, 2 * k + 3)
        return carry

    lax.fori_loop(0, (ITERS - 2) // 2, pair, 0)
    step(0, 1, ITERS)
    out_ref[...] = u_buf[1, pl.ds(FRONT + 8 * REACH + 2 * part, 2)]


def relax(place, total, window, conf):
    rows = SPAN + 2 * FRONT
    return pl.pallas_call(
        functools.partial(relax_kernel, total),
        out_shape=jax.ShapeDtypeStruct((2, 8, 256), jnp.float32),
        grid_spec=pltpu.PrefetchScalarGridSpec(
            num_scalar_prefetch=1,
            grid=(1,),
            in_specs=[
                pl.BlockSpec(window.shape, lambda i, s: (0, 0, 0, 0)),
                pl.BlockSpec(conf.shape, lambda i, s: (0, 0, 0)),
            ],
            out_specs=pl.BlockSpec((2, 8, 256), lambda i, s: (0, 0, 0)),
            scratch_shapes=[pltpu.VMEM((2, 128, 128), jnp.float32)]
            + [pltpu.VMEM((rows, 8, 256), jnp.float32)] * 2
            + [pltpu.VMEM((2, rows, 8, 256), jnp.float32)],
        ),
        compiler_params=pltpu.CompilerParams(vmem_limit_bytes=40 * 1024 * 1024),
    )(place, window, conf)


def on_device(patches, prior_patches, blocks, dest, target, flows, valid, stiffness):
    first, second, third, fourth = tables()
    tile_count = lax.axis_size("tile")
    gz_index = lax.axis_index("gz")
    tile_index = lax.axis_index("tile")

    node_rows, node_cols = flows.shape[2:]
    owner_tile = dest[0, :, 0]
    block_ids = jnp.arange(blocks.shape[1], dtype=jnp.int32)
    before = (owner_tile[:, None] == owner_tile[None, :]) & (block_ids[None, :] < block_ids[:, None])
    slot_index = owner_tile * CAP + jnp.sum(before.astype(jnp.int32), axis=1)
    arrived, block_spec, window = trade(
        tile_count, patches, prior_patches, blocks, dest[0], owner_tile[None], target, flows, valid, stiffness, first, second
    )
    corr_maps, peaks = match(slot_index, arrived.reshape(tile_count * CAP, WIRE, LANES), block_spec, third, fourth)

    conf_window = gather_conf(tile_count, peaks, node_cols)
    place = jnp.stack([tile_index, gz_index // 2]).astype(jnp.int32)
    mine = relax(place, tile_count * node_rows, window, conf_window)
    mesh_nodes = spread_result(mine)[None]
    return (corr_maps[None], mesh_nodes)


def solution(mesh):
    return jax.shard_map(
        on_device,
        mesh=mesh,
        in_specs=(
            P("gz", "tile", None),
            P("tile", None),
            P("gz", "tile", None),
            P("gz", "tile", None),
            P("gz", "tile"),
            P("gz", None, "tile", None),
            P("gz", "tile", None),
            P("gz", "tile", None),
        ),
        out_specs=(P("gz", "tile", None), P("gz", None, "tile", None)),
        check_vma=False,
    )
```

```python
import functools

import jax
import jax.numpy as jnp
import ml_dtypes
import numpy as np
from jax import lax
from jax.experimental import pallas as pl
from jax.experimental.pallas import tpu as pltpu
from jax.sharding import PartitionSpec as P

P_SIZE = 160
PIX = 25600
CAP = 2
ITERS = 64
GROUP = 4
PHASE = ITERS // 2
UNROLL = 8


LANES = 128
HALF = 64
WIRE = 208
BATCH = 16


def tables():
    size = P_SIZE
    line = np.arange(size)
    angles = (np.outer(line, line) % size).astype(np.float32) * np.float32(2.0 * np.pi / size)
    rounded = lambda x: x.astype(ml_dtypes.bfloat16).astype(np.float32)
    cos_t, sin_t = rounded(np.cos(angles)), rounded(np.sin(angles))
    lane = np.arange(2 * LANES)
    column = HALF * (lane // LANES) + lane % HALF
    used = column <= size // 2
    column = np.where(used, column, 0)
    real = lane % LANES < HALF
    c, s = cos_t[:, column] * used, sin_t[:, column] * used
    first = np.zeros((2 * LANES, 4 * LANES), np.float32)
    first[:size, : 2 * LANES] = np.where(real, c, s)
    first[:size, 2 * LANES :] = np.where(real, -s, c)
    second = np.concatenate([cos_t, sin_t], axis=1)
    third = np.concatenate([cos_t, sin_t], axis=0)
    twice = np.where((column == 0) | (column == size // 2), 1.0, 2.0)
    fourth = np.zeros((4 * LANES, 2 * LANES), np.float32)
    fourth[: 2 * LANES, :size] = (np.where(real, c, -s) * twice).T
    fourth[2 * LANES :, :size] = (np.where(real, -s, -c) * twice).T
    return [jnp.asarray(x, jnp.bfloat16) for x in (first, second, third, fourth)]


def to_images(rows_ref, low_buf, high_buf):
    parts = PIX // 640
    chunk = lambda m: rows_ref[:, pl.ds(pl.multiple_of(640 * m, LANES), 640)].astype(jnp.float32)
    fold = lambda x: sum(x[:, LANES * k : LANES * k + LANES] for k in range(5))
    zero = jnp.zeros((BATCH, LANES), jnp.float32)
    sums = lax.fori_loop(0, parts, lambda m, t: t + fold(chunk(m)), zero)
    mean = jnp.sum(sums, axis=1, keepdims=True) * (1.0 / PIX)

    def square(m, t):
        x = chunk(m) - mean
        return t + fold(x * x)

    sums = lax.fori_loop(0, parts, square, zero)
    scale = lax.rsqrt(jnp.sum(sums, axis=1, keepdims=True) * (1.0 / PIX) + 1e-05)
    lane = lax.broadcasted_iota(jnp.int32, (BATCH, LANES), 1)

    def place(m, carry):
        x = (chunk(m) - mean) * scale
        t = [x[:, LANES * k : LANES * k + LANES] for k in range(5)]
        low = [
            t[0],
            pltpu.roll(jnp.where(lane < 32, t[2], t[1]), 96, 1),
            pltpu.roll(jnp.where(lane < 64, t[3], t[2]), 64, 1),
            pltpu.roll(jnp.where(lane < 96, t[4], t[3]), 32, 1),
        ]
        high = [t[1], pltpu.roll(t[2], 96, 1), pltpu.roll(t[3], 64, 1), pltpu.roll(t[4], 32, 1)]
        for k in range(4):
            at = pl.ds(4 * m + k, BATCH, stride=P_SIZE)
            low_buf[at, :] = low[k]
            high_buf[at, :] = high[k]
        return carry

    lax.fori_loop(0, parts, place, 0)


def image_spectrum(n, low_buf, high_buf, first_ref, second_ref):
    at = pl.ds(pl.multiple_of(P_SIZE * n, 8), P_SIZE)
    image = jnp.concatenate([low_buf[at, :], high_buf[at, :]], axis=1).astype(jnp.bfloat16)
    first = jnp.dot(image, first_ref[...], preferred_element_type=jnp.float32).astype(jnp.bfloat16)
    both = jnp.concatenate([first[:, : 2 * LANES], first[:, 2 * LANES :]], axis=0)
    return jnp.dot(second_ref[...], both, preferred_element_type=jnp.float32)


def block_batch(low_buf, high_buf, first_ref, second_ref, out_ref):
    low_half = lax.broadcasted_iota(jnp.int32, (P_SIZE, LANES), 1) < HALF

    def image(n, carry):
        spec = image_spectrum(n, low_buf, high_buf, first_ref, second_ref)
        for h in range(2):
            x = spec[:, LANES * h : LANES * h + LANES]
            swapped = pltpu.roll(x, HALF, 1)
            out_ref[n, :, LANES * h : LANES * h + LANES] = jnp.where(low_half, x, swapped).astype(jnp.bfloat16)
            at = slice(LANES * (2 + h), LANES * (3 + h))
            out_ref[n, :, at] = jnp.where(low_half, swapped, -x).astype(jnp.bfloat16)
        return carry

    lax.fori_loop(0, BATCH, image, 0, unroll=UNROLL)


def patch_batch(low_buf, high_buf, first_ref, second_ref, wire_buf):
    lane = lax.broadcasted_iota(jnp.int32, (8, LANES), 1) % HALF

    def image(n, carry):
        spec = image_spectrum(n, low_buf, high_buf, first_ref, second_ref)
        rest = [spec[8 * i : 8 * i + 8, LANES:] for i in range(20)]
        pieces = [spec[:, :LANES]]
        for i in range(5):
            pieces.append(sum(pltpu.roll(jnp.where(lane < 16, rest[5 * b + i], 0.0), 16 * b, 1) for b in range(4)))
        pieces.append(sum(pltpu.roll(jnp.where(lane == 16, rest[i], 0.0), (i + 112) % LANES, 1) for i in range(20)))
        wire_buf[n] = jnp.concatenate(pieces, axis=0).astype(jnp.bfloat16)
        return carry

    lax.fori_loop(0, BATCH, image, 0, unroll=UNROLL)


def match_one(wire, block_of, third_ref, fourth_ref):
    lane8 = lax.broadcasted_iota(jnp.int32, (8, LANES), 1) % HALF == 16
    last = wire[200:208]
    rest = []
    for i in range(20):
        part = wire[160 + 8 * (i % 5) : 168 + 8 * (i % 5)]
        part = pltpu.roll(part, (LANES - 16 * (i // 5)) % LANES, 1)
        rest.append(jnp.where(lane8, pltpu.roll(last, (16 - i) % LANES, 1), part))
    cross = []
    for h, a in enumerate((wire[:P_SIZE], jnp.concatenate(rest, axis=0))):
        straight, swapped = block_of(h).astype(jnp.float32), block_of(2 + h).astype(jnp.float32)
        cross.append((a * straight + pltpu.roll(a, HALF, 1) * swapped).astype(jnp.bfloat16))
    back = jnp.dot(third_ref[...], jnp.concatenate(cross, axis=1), preferred_element_type=jnp.float32)
    back = back.astype(jnp.bfloat16)
    back = jnp.concatenate([back[:P_SIZE], back[P_SIZE:]], axis=1)
    return jnp.dot(back, fourth_ref[...], preferred_element_type=jnp.float32) * (1.0 / float(P_SIZE) ** 3)


def to_rows(low_buf, high_buf, map_ref, peak_ref):
    lane = lax.broadcasted_iota(jnp.int32, (BATCH, LANES), 1)

    def place(m, top):
        load = lambda buf, k: buf[pl.ds(4 * m + k, BATCH, stride=P_SIZE), :]
        low = [load(low_buf, 0)] + [pltpu.roll(load(low_buf, k), 32 * k, 1) for k in range(1, 4)]
        high = [load(high_buf, 0)] + [pltpu.roll(load(high_buf, k), 32 * k, 1) for k in range(1, 4)]
        tiles = [
            low[0],
            jnp.where(lane < 32, high[0], low[1]),
            jnp.where(lane < 32, low[1], jnp.where(lane < 64, high[1], low[2])),
            jnp.where(lane < 64, low[2], jnp.where(lane < 96, high[2], low[3])),
            jnp.where(lane < 96, low[3], high[3]),
        ]
        rows = jnp.concatenate(tiles, axis=1).astype(jnp.bfloat16)
        map_ref[:, pl.ds(pl.multiple_of(640 * m, LANES), 640)] = rows
        for tile in tiles:
            top = jnp.maximum(top, tile)
        return top

    start = jnp.full((BATCH, LANES), -jnp.inf, jnp.float32)
    top = lax.fori_loop(0, P_SIZE // 4, place, start, unroll=2)
    top = jnp.max(top, axis=1, keepdims=True).astype(jnp.bfloat16).astype(jnp.float32)
    peak_ref[...] = jnp.broadcast_to(top, (BATCH, LANES))


MESH = pl.DeviceIdType.MESH
GZ = 8
REACH = 4


def group_barrier(peers):
    barrier = pltpu.get_barrier_semaphore()
    for peer in peers:
        pl.semaphore_signal(barrier, inc=1, device_id=peer, device_id_type=MESH)
    pl.semaphore_wait(barrier, len(peers))


def gz_peers():
    gz, tile = lax.axis_index("gz"), lax.axis_index("tile")
    return [(lax.rem(gz + d, GZ), tile) for d in range(1, GZ)]


def tile_peers(tile_count):
    gz, tile = lax.axis_index("gz"), lax.axis_index("tile")
    offsets = [e for k in range(1, REACH + 1) for e in (k, -k)]
    return offsets, [(gz, lax.rem(tile + e + tile_count, tile_count)) for e in offsets]


def exchange_gz(source_of, held, send, recv):
    gz = lax.axis_index("gz")
    copies = []
    for d, peer in enumerate(gz_peers()):
        copies.append(
            pltpu.make_async_remote_copy(
                src_ref=source_of(peer[0]), dst_ref=held.at[gz], send_sem=send.at[d], recv_sem=recv.at[d],
                device_id=peer, device_id_type=MESH,
            )
        )
    for copy in copies:
        copy.start()
    return copies


def exchange_tiles(tile_count, source, window, send, recv):
    offsets, peers = tile_peers(tile_count)
    copies = []
    for n, (e, peer) in enumerate(zip(offsets, peers)):
        copies.append(
            pltpu.make_async_remote_copy(
                src_ref=source, dst_ref=window.at[REACH - e], send_sem=send.at[n], recv_sem=recv.at[n],
                device_id=peer, device_id_type=MESH,
            )
        )
    for copy in copies:
        copy.start()
    return copies


def request_rows(owner_row, wanted_row, tile_count):
    count = owner_row.shape[1]
    grid = lambda axis: lax.broadcasted_iota(jnp.int32, (count, count), axis)
    owner_col = jnp.sum(jnp.where(grid(0) == grid(1), owner_row, 0), axis=1, keepdims=True)
    same = owner_col == owner_row
    rank = jnp.sum(jnp.where((grid(0) < grid(1)) & same, 1, 0), axis=0, keepdims=True)
    rank_col = jnp.sum(jnp.where((grid(1) < grid(0)) & same, 1, 0), axis=1, keepdims=True)
    hit = owner_row == lax.broadcasted_iota(jnp.int32, (tile_count, count), 0)
    lane = lax.broadcasted_iota(jnp.int32, (tile_count, LANES), 1)
    rows = jnp.zeros((tile_count, LANES), jnp.int32)
    for c in range(CAP):
        asked = jnp.sum(jnp.where(hit & (rank == c), wanted_row, 0), axis=1, keepdims=True)
        rows = jnp.where(lane == c, asked, rows)
    used = owner_col * CAP + rank_col == lax.broadcasted_iota(jnp.int32, (count, LANES), 1)
    block = jnp.sum(jnp.where(used, lax.broadcasted_iota(jnp.int32, (count, LANES), 0), 0), axis=0, keepdims=True)
    return rows, owner_row * CAP + rank, block


FRONT = 32
SPAN = 8 * (2 * REACH + 1)


def whole_kernel(
    tile_count, patch_ref, prior_ref, block_ref, row_ref, want_ref, flow_ref, valid_ref, stiff_ref, first_ref,
    second_ref, third_ref, fourth_ref, map_ref, mesh_ref, rows_buf, block_buf, low_buf, high_buf, wire_buf, send_buf,
    arrived_buf, spec_buf, field_buf, map_buf, peak_buf, own_buf, held, window_buf, ask_buf, heard_buf, list_buf,
    told_buf, index_buf, told_smem, index_smem, conf_own, conf_held, conf_pack, conf_window, s_buf, w_buf, f_buf, u_buf,
    mid_buf, spread_own, spread_held, local, send_r, recv_r, send_a, recv_a, send_b, recv_b, send_f, recv_f, send_p,
    recv_p, send_c, recv_c, send_d, recv_d, send_m, recv_m, send_s, recv_s,
):
    gz, tile = lax.axis_index("gz"), lax.axis_index("tile")
    component, part = lax.rem(gz, 2), gz // 2
    mid_buf[...] = jnp.zeros_like(mid_buf)
    after, before = lax.rem(gz + 1, GZ), lax.rem(gz + GZ - 1, GZ)
    barrier = pltpu.get_barrier_semaphore()

    def greet(peer):
        pl.semaphore_signal(barrier, inc=1, device_id=peer, device_id_type=MESH)

    def greet_tiles(d, carry):
        peer = lax.rem(tile + d, tile_count)
        greet((after, peer))
        greet((before, peer))

        @pl.when(d > 0)
        def _():
            greet((gz, peer))

        return carry

    lax.fori_loop(0, tile_count, greet_tiles, 0)
    for d in range(2, GZ - 1):
        greet((lax.rem(gz + d, GZ), tile))
    for d in (2, 4, 6):
        for e in range(1, REACH + 1):
            for sign in (e, tile_count - e):
                greet((lax.rem(gz + d, GZ), lax.rem(tile + sign, tile_count)))

    from_prior = pltpu.make_async_copy(prior_ref, rows_buf, local.at[0])
    from_patches = pltpu.make_async_copy(patch_ref.at[0], rows_buf, local.at[0])
    load_blocks = pltpu.make_async_copy(block_ref.at[0], block_buf, local.at[1])

    @pl.when(gz == GZ - 1)
    def _():
        from_prior.start()

    @pl.when(gz != GZ - 1)
    def _():
        from_patches.start()

    load_blocks.start()

    rows, slot_row, block_row = request_rows(row_ref[...], want_ref[...], tile_count)
    count = slot_row.shape[1]
    index_buf[0:1, 0:count] = slot_row
    index_buf[1:2, :] = block_row
    index = pltpu.make_async_copy(index_buf, index_smem, local.at[6])
    index.start()
    for j in range(8):
        ask_buf[pl.ds(j, tile_count, stride=8), :] = rows
    columns = stiff_ref.shape[2]
    lane = lax.broadcasted_iota(jnp.int32, (columns, columns), 1)
    order = 2 * lax.rem(lane, columns // 2) + lane // (columns // 2)
    pick = jnp.where(lax.broadcasted_iota(jnp.int32, (columns, columns), 0) == order, 1.0, 0.0).astype(jnp.bfloat16)
    spring = stiff_ref[0] * valid_ref[0].astype(jnp.float32)
    for c in range(2):
        nodes = jnp.concatenate([spring, flow_ref[0, c]], axis=0).astype(jnp.bfloat16)
        own_buf[c] = jnp.dot(nodes, pick, preferred_element_type=jnp.float32).astype(jnp.bfloat16)

    pl.semaphore_wait(barrier, 3 * tile_count - 1 + GZ - 3 + 6 * REACH)

    springs = exchange_gz(lambda peer: own_buf.at[lax.rem(peer, 2)], held, send_a, recv_a)
    mine = pltpu.make_async_copy(own_buf.at[lax.rem(gz, 2)], held.at[gz], local.at[2])
    mine.start()

    def request(d):
        peer = lax.rem(tile + d, tile_count)
        part = lambda t: pl.ds(pl.multiple_of(8 * t, 8), 8)
        return pltpu.make_async_remote_copy(
            src_ref=ask_buf.at[part(peer)], dst_ref=heard_buf.at[part(tile)], send_sem=send_r.at[d],
            recv_sem=recv_r.at[d], device_id=(gz, peer), device_id_type=MESH,
        )

    def each(first, last, act):
        def body(d, carry):
            act(d)
            return carry

        lax.fori_loop(first, last, body, 0)

    each(1, tile_count, lambda d: request(d).start())
    own_part = pl.ds(pl.multiple_of(8 * tile, 8), 8)
    heard_buf[own_part, :] = ask_buf[own_part, :]

    @pl.when(gz == GZ - 1)
    def _():
        from_prior.wait()

    @pl.when(gz != GZ - 1)
    def _():
        from_patches.wait()

    to_images(rows_buf, low_buf, high_buf)

    mine.wait()
    for copy in springs:
        copy.wait()
    springs = exchange_tiles(tile_count, held, window_buf, send_b, recv_b)
    mine = pltpu.make_async_copy(held, window_buf.at[REACH], local.at[2])
    mine.start()
    each(1, tile_count, lambda d: request(d).wait())
    list_buf[...] = heard_buf[pl.ds(0, tile_count, stride=8), :]
    forward = pltpu.make_async_remote_copy(
        src_ref=list_buf, dst_ref=told_buf, send_sem=send_f.at[0], recv_sem=recv_f.at[0], device_id=(before, tile),
        device_id_type=MESH,
    )
    forward.start()
    patch_batch(low_buf, high_buf, first_ref, second_ref, wire_buf)
    forward.wait()
    told = pltpu.make_async_copy(told_buf, told_smem, local.at[3])
    told.start()
    told.wait()

    def parcel(d):
        peer = lax.rem(tile + d, tile_count)
        return pltpu.make_async_remote_copy(
            src_ref=send_buf.at[peer], dst_ref=arrived_buf.at[tile], send_sem=send_p.at[d], recv_sem=recv_p.at[d],
            device_id=(after, peer), device_id_type=MESH,
        )

    halfway = tile_count // 2

    def post(k):
        for d in (k, k + halfway):
            peer = lax.rem(tile + d, tile_count)
            for c in range(CAP):
                send_buf[peer, WIRE * c : WIRE * c + WIRE, :] = wire_buf[told_smem[peer, c]]
            parcel(d).start()

    each(0, halfway, post)

    load_blocks.wait()
    for half in range(2):
        batch = pl.ds(BATCH * half, BATCH)
        to_images(block_buf.at[batch], low_buf, high_buf)
        block_batch(low_buf, high_buf, first_ref, second_ref, spec_buf.at[batch])
    index.wait()
    mine.wait()
    for copy in springs:
        copy.wait()

    def match(k):
        for d in (k, k + halfway):
            parcel(d).wait_recv()
        for d in (k, k + halfway):
            source = lax.rem(tile - d + tile_count, tile_count)
            for c in range(CAP):
                wire = arrived_buf[source, WIRE * c : WIRE * c + WIRE, :].astype(jnp.float32)
                block = index_smem[1, CAP * source + c]
                quarter = lambda q: spec_buf[block, :, LANES * q : LANES * q + LANES]
                field_buf[CAP * source + c] = match_one(wire, quarter, third_ref, fourth_ref)

    each(0, halfway, match)
    stores = []
    for half in range(2):
        batch = pl.ds(BATCH * half, BATCH)

        def collect(n):
            field = field_buf[index_smem[0, BATCH * half + n]]
            at = pl.ds(pl.multiple_of(P_SIZE * n, 8), P_SIZE)
            low_buf[at, :] = field[:, :LANES]
            high_buf[at, :] = field[:, LANES:]

        each(0, BATCH, collect)
        to_rows(low_buf, high_buf, map_buf.at[batch], peak_buf.at[batch])
        stores.append(pltpu.make_async_copy(map_buf.at[batch], map_ref.at[batch], local.at[4 + half]))
        stores[-1].start()

    peak = jnp.concatenate([peak_buf[...]] * (columns // LANES), axis=1)
    block = lax.rem(lax.broadcasted_iota(jnp.int32, (count, columns), 1), columns // 2) // (columns // 2 // count)
    own = block == lax.broadcasted_iota(jnp.int32, (count, columns), 0)
    confidence = jnp.sum(jnp.where(own, peak / (1.0 + peak), 0.0), axis=0, keepdims=True)
    conf_own[...] = jnp.broadcast_to(confidence, conf_own.shape)
    copies = exchange_gz(lambda peer: conf_own, conf_held, send_c, recv_c)
    conf_held[gz] = conf_own[...]
    for buf in (w_buf, f_buf, u_buf):
        buf[...] = jnp.zeros_like(buf)
    for copy in copies:
        copy.wait()
    for s in range(GZ):
        conf_pack[s : s + 1, :] = conf_held[s, 0:1, :]
    copies = exchange_tiles(tile_count, conf_pack, conf_window, send_d, recv_d)
    conf_window[REACH] = conf_pack[...]
    for copy in copies:
        copy.wait()

    first_slot = jnp.maximum(REACH - tile, 0)
    last_slot = jnp.minimum(REACH + tile_count - tile, 2 * REACH + 1)
    lane = lax.broadcasted_iota(jnp.int32, (1, 8, LANES), 2)
    first_lane, last_lane = lane == 0, lane == LANES - 1
    section = lax.broadcasted_iota(jnp.int32, (8, columns), 0)

    def picked(j):
        return jnp.concatenate([s_buf[h, pl.ds(j, 8, stride=16), :] for h in range(2)], axis=1)

    def prepare(k, carry):
        conf = jnp.where(section == 0, 0.0, 0.15 * conf_window[k])
        nodes = window_buf[k].astype(jnp.float32).reshape(LANES, columns)
        s_buf[0], s_buf[1] = nodes[:, :LANES], nodes[:, LANES:]
        for j in range(8):
            i = FRONT + 8 * k + j
            w = picked(j) * conf
            wf = w * picked(8 + j)
            w_buf[i] = w
            f_buf[i] = wf
            u_buf[0, i] = wf - pltpu.roll(wf, 7, 0)
        return carry

    lax.fori_loop(first_slot, last_slot, prepare, 0)

    def step(source, target, s):
        low = jnp.maximum((2 * part + s) // 8, first_slot)
        high = jnp.minimum((2 * part + 2 * PHASE + 2 - s + 7) // 8, last_slot)
        groups = (high - low + GROUP - 1) // GROUP
        low = jnp.where(tile < REACH, low, high - groups * GROUP)

        def group(g, carry):
            i = FRONT + 8 * low + 8 * GROUP * g
            rows = 8 * GROUP
            even, odd = [source[pl.ds(i - 1, rows + 2), :, LANES * h : LANES * h + LANES] for h in range(2)]
            to_left = jnp.where(first_lane, 0.0, pltpu.roll(odd[1:-1], 1, 2))
            to_right = jnp.where(last_lane, 0.0, pltpu.roll(even[1:-1], LANES - 1, 2))
            for h, (x, beside, other) in enumerate(((even, odd[1:-1], to_left), (odd, even[1:-1], to_right))):
                at = (pl.ds(i, rows), slice(None), slice(LANES * h, LANES * h + LANES))
                mid = x[1:-1]
                around = (x[:-2] + x[2:]) + (beside + other)
                force = w_buf[at] * (pltpu.roll(mid, 1, 1) - mid) + f_buf[at]
                target[at] = (0.4 * mid + 0.15 * around) + (force - pltpu.roll(force, 7, 1))
            return carry

        lax.fori_loop(0, groups, group, 0)

    ping, pong = u_buf.at[0], u_buf.at[1]

    def pair(k, carry):
        step(ping, pong, 2 * k + 2)
        step(pong, ping, 2 * k + 3)
        return carry

    def rest_of_phase():
        lax.fori_loop(0, (PHASE - 2) // 2, pair, 0)
        step(ping, pong, PHASE)

    base = FRONT + 8 * REACH + 2 * part
    rest_of_phase()

    place = 4 * tile + part
    places = 4 * tile_count

    def handover(n):
        e = jnp.where(n < 4 * REACH, n + 1, 4 * REACH - 1 - n)
        peer = lax.rem(place + e + places, places)
        row = FRONT + 8 * REACH + 2 * lax.rem(part + e + 4 * REACH, 4) - 2 * e
        copy = pltpu.make_async_remote_copy(
            src_ref=pong.at[pl.ds(base, 2)], dst_ref=mid_buf.at[pl.ds(row, 2)], send_sem=send_m.at[n],
            recv_sem=recv_m.at[n], device_id=(2 * lax.rem(peer, 4) + component, peer // 4), device_id_type=MESH,
        )
        sends = (place + e >= 0) & (place + e < places)
        receives = (place - e >= 0) & (place - e < places)
        return copy, sends, receives

    def hand_out(n):
        copy, sends, _ = handover(n)

        @pl.when(sends)
        def _():
            copy.start()

    def take_in(n):
        copy, sends, receives = handover(n)

        @pl.when(sends)
        def _():
            copy.wait_send()

        @pl.when(receives)
        def _():
            copy.wait_recv()

    each(0, 8 * REACH, hand_out)
    mid_buf[pl.ds(base, 2)] = pong[pl.ds(base, 2)]
    each(0, 8 * REACH, take_in)
    step(mid_buf, ping, 1)
    rest_of_phase()

    for s in range(GZ):
        for r in range(2):
            spread_own[s, r : r + 1, :] = pong[base + r, s : s + 1, :]
    copies = exchange_gz(lambda peer: spread_own.at[peer], spread_held, send_s, recv_s)
    spread_held[gz] = spread_own[gz]
    order = lax.broadcasted_iota(jnp.int32, (columns, columns), 1)
    order = order // 2 + lax.rem(order, 2) * (columns // 2)
    spot = lax.broadcasted_iota(jnp.int32, (columns, columns), 0) == order
    pick = jnp.where(spot, 1.0, 0.0).astype(jnp.bfloat16)
    for copy in copies:
        copy.wait()
    rest = jnp.concatenate([spread_held[2 * h + c, 0:2, :] for c in range(2) for h in range(4)], axis=0)
    total = jnp.zeros_like(rest)
    for _ in range(3):
        piece = rest.astype(jnp.bfloat16)
        rest = rest - piece.astype(jnp.float32)
        total = total + jnp.dot(piece, pick, preferred_element_type=jnp.float32)
    mesh_ref[0] = total[:8]
    mesh_ref[1] = total[8:]
    for copy in stores:
        copy.wait()
    each(0, tile_count, lambda d: parcel(d).wait_send())


def whole(tile_count, patches, prior, blocks, row, want, flows, valid, stiffness, *fixed):
    count = blocks.shape[1]
    columns = flows.shape[3]
    rows = SPAN + 2 * FRONT
    dma = lambda number: pltpu.SemaphoreType.DMA((number,))
    vmem, anywhere = pl.BlockSpec(memory_space=pltpu.VMEM), pl.BlockSpec(memory_space=pl.ANY)
    f32, bf16, i32 = jnp.float32, jnp.bfloat16, jnp.int32
    images = pltpu.VMEM((BATCH * P_SIZE, LANES), f32)
    parcels = pltpu.VMEM((tile_count, CAP * WIRE, LANES), bf16)
    near = pltpu.VMEM((GZ, 8, columns), f32)
    return pl.pallas_call(
        functools.partial(whole_kernel, tile_count),
        out_shape=(
            jax.ShapeDtypeStruct((count, PIX), bf16),
            jax.ShapeDtypeStruct((2, 8, columns), f32),
        ),
        in_specs=[anywhere] * 3 + [vmem] * 9,
        out_specs=(anywhere, vmem),
        scratch_shapes=[
            pltpu.VMEM((BATCH, PIX), bf16),
            pltpu.VMEM((count, PIX), bf16),
            images,
            images,
            pltpu.VMEM((BATCH, WIRE, LANES), bf16),
            parcels,
            parcels,
            pltpu.VMEM((count, P_SIZE, 4 * LANES), bf16),
            pltpu.VMEM((CAP * tile_count, P_SIZE, 2 * LANES), f32),
            pltpu.VMEM((count, PIX), bf16),
            pltpu.VMEM((count, LANES), f32),
            pltpu.VMEM((2, 16, columns), bf16),
            pltpu.VMEM((GZ, 16, columns), bf16),
            pltpu.VMEM((2 * REACH + 1, GZ, 16, columns), bf16),
            pltpu.VMEM((8 * tile_count, LANES), i32),
            pltpu.VMEM((8 * tile_count, LANES), i32),
            pltpu.VMEM((tile_count, LANES), i32),
            pltpu.VMEM((tile_count, LANES), i32),
            pltpu.VMEM((8, LANES), i32),
            pltpu.SMEM((tile_count, LANES), i32),
            pltpu.SMEM((8, LANES), i32),
            pltpu.VMEM((8, columns), f32),
            near,
            pltpu.VMEM((GZ, columns), f32),
            pltpu.VMEM((2 * REACH + 1, GZ, columns), f32),
            pltpu.VMEM((2, LANES, LANES), f32),
            pltpu.VMEM((rows, 8, columns), f32),
            pltpu.VMEM((rows, 8, columns), f32),
            pltpu.VMEM((2, rows, 8, columns), f32),
            pltpu.VMEM((rows, 8, columns), f32),
            near,
            near,
            dma(7),
        ]
        + [dma(tile_count)] * 2
        + [dma(GZ - 1)] * 2
        + [dma(2 * REACH)] * 2
        + [dma(1)] * 2
        + [dma(tile_count)] * 2
        + [dma(GZ - 1)] * 2
        + [dma(2 * REACH)] * 2
        + [dma(8 * REACH)] * 2
        + [dma(GZ - 1)] * 2,
        compiler_params=pltpu.CompilerParams(
            collective_id=1, has_side_effects=True, vmem_limit_bytes=60 * 1024 * 1024
        ),
        cost_estimate=pl.CostEstimate(flops=30_000_000_000, bytes_accessed=32_000_000, transcendentals=0),
    )(patches, prior, blocks, row, want, flows, valid, stiffness, *fixed)


def on_device(patches, prior_patches, blocks, dest, target, flows, valid, stiffness):
    corr_maps, mesh_nodes = whole(
        lax.axis_size("tile"), patches, prior_patches, blocks, dest[:, :, 0], target, flows, valid, stiffness, *tables()
    )
    return (corr_maps[None], mesh_nodes[None])


def solution(mesh):
    return jax.shard_map(
        on_device,
        mesh=mesh,
        in_specs=(
            P("gz", "tile", None),
            P("tile", None),
            P("gz", "tile", None),
            P("gz", "tile", None),
            P("gz", "tile"),
            P("gz", None, "tile", None),
            P("gz", "tile", None),
            P("gz", "tile", None),
        ),
        out_specs=(P("gz", "tile", None), P("gz", None, "tile", None)),
        check_vma=False,
    )
```

```python
import functools

import jax
import jax.numpy as jnp
import ml_dtypes
import numpy as np
from jax import lax
from jax.experimental import pallas as pl
from jax.experimental.pallas import tpu as pltpu
from jax.sharding import PartitionSpec as P

P_SIZE = 160
PIX = 25600
CAP = 2
ITERS = 64
PHASE = ITERS // 2
UNROLL = 8


LANES = 128
HALF = 64
WIRE = 208
BATCH = 16


def tables():
    size = P_SIZE
    line = np.arange(size)
    angles = (np.outer(line, line) % size).astype(np.float32) * np.float32(2.0 * np.pi / size)
    rounded = lambda x: x.astype(ml_dtypes.bfloat16).astype(np.float32)
    cos_t, sin_t = rounded(np.cos(angles)), rounded(np.sin(angles))
    lane = np.arange(2 * LANES)
    column = HALF * (lane // LANES) + lane % HALF
    used = column <= size // 2
    column = np.where(used, column, 0)
    real = lane % LANES < HALF
    c, s = cos_t[:, column] * used, sin_t[:, column] * used
    first = np.zeros((2 * LANES, 4 * LANES), np.float32)
    first[:size, : 2 * LANES] = np.where(real, c, s)
    first[:size, 2 * LANES :] = np.where(real, -s, c)
    second = np.concatenate([cos_t, sin_t], axis=1)
    third = np.concatenate([cos_t, sin_t], axis=0)
    twice = np.where((column == 0) | (column == size // 2), 1.0, 2.0)
    fourth = np.zeros((4 * LANES, 2 * LANES), np.float32)
    fourth[: 2 * LANES, :size] = (np.where(real, c, -s) * twice).T
    fourth[2 * LANES :, :size] = (np.where(real, -s, -c) * twice).T
    return [jnp.asarray(x, jnp.bfloat16) for x in (first, second, third, fourth)]


def to_images(rows_ref, low_buf, high_buf):
    parts = PIX // 640
    chunk = lambda m: rows_ref[:, pl.ds(pl.multiple_of(640 * m, LANES), 640)].astype(jnp.float32)
    fold = lambda x: sum(x[:, LANES * k : LANES * k + LANES] for k in range(5))
    zero = jnp.zeros((BATCH, LANES), jnp.float32)
    sums = lax.fori_loop(0, parts, lambda m, t: t + fold(chunk(m)), zero)
    mean = jnp.sum(sums, axis=1, keepdims=True) * (1.0 / PIX)

    def square(m, t):
        x = chunk(m) - mean
        return t + fold(x * x)

    sums = lax.fori_loop(0, parts, square, zero)
    scale = lax.rsqrt(jnp.sum(sums, axis=1, keepdims=True) * (1.0 / PIX) + 1e-05)
    lane = lax.broadcasted_iota(jnp.int32, (BATCH, LANES), 1)

    def place(m, carry):
        x = (chunk(m) - mean) * scale
        t = [x[:, LANES * k : LANES * k + LANES] for k in range(5)]
        low = [
            t[0],
            pltpu.roll(jnp.where(lane < 32, t[2], t[1]), 96, 1),
            pltpu.roll(jnp.where(lane < 64, t[3], t[2]), 64, 1),
            pltpu.roll(jnp.where(lane < 96, t[4], t[3]), 32, 1),
        ]
        high = [t[1], pltpu.roll(t[2], 96, 1), pltpu.roll(t[3], 64, 1), pltpu.roll(t[4], 32, 1)]
        for k in range(4):
            at = pl.ds(4 * m + k, BATCH, stride=P_SIZE)
            low_buf[at, :] = low[k]
            high_buf[at, :] = high[k]
        return carry

    lax.fori_loop(0, parts, place, 0)


def image_spectrum(n, low_buf, high_buf, first_ref, second_ref):
    at = pl.ds(pl.multiple_of(P_SIZE * n, 8), P_SIZE)
    image = jnp.concatenate([low_buf[at, :], high_buf[at, :]], axis=1).astype(jnp.bfloat16)
    first = jnp.dot(image, first_ref[...], preferred_element_type=jnp.float32).astype(jnp.bfloat16)
    both = jnp.concatenate([first[:, : 2 * LANES], first[:, 2 * LANES :]], axis=0)
    return jnp.dot(second_ref[...], both, preferred_element_type=jnp.float32)


def block_batch(low_buf, high_buf, first_ref, second_ref, out_ref):
    low_half = lax.broadcasted_iota(jnp.int32, (P_SIZE, LANES), 1) < HALF

    def image(n, carry):
        spec = image_spectrum(n, low_buf, high_buf, first_ref, second_ref)
        for h in range(2):
            x = spec[:, LANES * h : LANES * h + LANES]
            swapped = pltpu.roll(x, HALF, 1)
            out_ref[n, :, LANES * h : LANES * h + LANES] = jnp.where(low_half, x, swapped).astype(jnp.bfloat16)
            at = slice(LANES * (2 + h), LANES * (3 + h))
            out_ref[n, :, at] = jnp.where(low_half, swapped, -x).astype(jnp.bfloat16)
        return carry

    lax.fori_loop(0, BATCH, image, 0, unroll=UNROLL)


def patch_batch(low_buf, high_buf, first_ref, second_ref, wire_buf):
    lane = lax.broadcasted_iota(jnp.int32, (8, LANES), 1) % HALF

    def image(n, carry):
        spec = image_spectrum(n, low_buf, high_buf, first_ref, second_ref)
        rest = [spec[8 * i : 8 * i + 8, LANES:] for i in range(20)]
        pieces = [spec[:, :LANES]]
        for i in range(5):
            pieces.append(sum(pltpu.roll(jnp.where(lane < 16, rest[5 * b + i], 0.0), 16 * b, 1) for b in range(4)))
        pieces.append(sum(pltpu.roll(jnp.where(lane == 16, rest[i], 0.0), (i + 112) % LANES, 1) for i in range(20)))
        wire_buf[n] = jnp.concatenate(pieces, axis=0).astype(jnp.bfloat16)
        return carry

    lax.fori_loop(0, BATCH, image, 0, unroll=UNROLL)


def match_one(wire, block_of, third_ref, fourth_ref):
    lane8 = lax.broadcasted_iota(jnp.int32, (8, LANES), 1) % HALF == 16
    last = wire[200:208]
    rest = []
    for i in range(20):
        part = wire[160 + 8 * (i % 5) : 168 + 8 * (i % 5)]
        part = pltpu.roll(part, (LANES - 16 * (i // 5)) % LANES, 1)
        rest.append(jnp.where(lane8, pltpu.roll(last, (16 - i) % LANES, 1), part))
    cross = []
    for h, a in enumerate((wire[:P_SIZE], jnp.concatenate(rest, axis=0))):
        straight, swapped = block_of(h).astype(jnp.float32), block_of(2 + h).astype(jnp.float32)
        cross.append((a * straight + pltpu.roll(a, HALF, 1) * swapped).astype(jnp.bfloat16))
    back = jnp.dot(third_ref[...], jnp.concatenate(cross, axis=1), preferred_element_type=jnp.float32)
    back = back.astype(jnp.bfloat16)
    back = jnp.concatenate([back[:P_SIZE], back[P_SIZE:]], axis=1)
    return jnp.dot(back, fourth_ref[...], preferred_element_type=jnp.float32) * (1.0 / float(P_SIZE) ** 3)


def to_rows(low_buf, high_buf, map_ref):
    lane = lax.broadcasted_iota(jnp.int32, (BATCH, LANES), 1)

    def place(m, carry):
        load = lambda buf, k: buf[pl.ds(4 * m + k, BATCH, stride=P_SIZE), :]
        low = [load(low_buf, 0)] + [pltpu.roll(load(low_buf, k), 32 * k, 1) for k in range(1, 4)]
        high = [load(high_buf, 0)] + [pltpu.roll(load(high_buf, k), 32 * k, 1) for k in range(1, 4)]
        tiles = [
            low[0],
            jnp.where(lane < 32, high[0], low[1]),
            jnp.where(lane < 32, low[1], jnp.where(lane < 64, high[1], low[2])),
            jnp.where(lane < 64, low[2], jnp.where(lane < 96, high[2], low[3])),
            jnp.where(lane < 96, low[3], high[3]),
        ]
        rows = jnp.concatenate(tiles, axis=1).astype(jnp.bfloat16)
        map_ref[:, pl.ds(pl.multiple_of(640 * m, LANES), 640)] = rows
        return carry

    lax.fori_loop(0, P_SIZE // 4, place, 0, unroll=2)


MESH = pl.DeviceIdType.MESH
GZ = 8
REACH = 4


def group_barrier(peers):
    barrier = pltpu.get_barrier_semaphore()
    for peer in peers:
        pl.semaphore_signal(barrier, inc=1, device_id=peer, device_id_type=MESH)
    pl.semaphore_wait(barrier, len(peers))


def gz_peers():
    gz, tile = lax.axis_index("gz"), lax.axis_index("tile")
    return [(lax.rem(gz + d, GZ), tile) for d in range(1, GZ)]


def tile_peers(tile_count):
    gz, tile = lax.axis_index("gz"), lax.axis_index("tile")
    offsets = [e for k in range(1, REACH + 1) for e in (k, -k)]
    return offsets, [(gz, lax.rem(tile + e + tile_count, tile_count)) for e in offsets]


def exchange_gz(source_of, held, send, recv):
    gz = lax.axis_index("gz")
    copies = []
    for d, peer in enumerate(gz_peers()):
        copies.append(
            pltpu.make_async_remote_copy(
                src_ref=source_of(peer[0]), dst_ref=held.at[gz], send_sem=send.at[d], recv_sem=recv.at[d],
                device_id=peer, device_id_type=MESH,
            )
        )
    for copy in copies:
        copy.start()
    return copies


def exchange_tiles(tile_count, source, window, send, recv):
    offsets, peers = tile_peers(tile_count)
    copies = []
    for n, (e, peer) in enumerate(zip(offsets, peers)):
        copies.append(
            pltpu.make_async_remote_copy(
                src_ref=source, dst_ref=window.at[REACH - e], send_sem=send.at[n], recv_sem=recv.at[n],
                device_id=peer, device_id_type=MESH,
            )
        )
    for copy in copies:
        copy.start()
    return copies


def request_rows(owner_row, wanted_row, tile_count):
    count = owner_row.shape[1]
    grid = lambda axis: lax.broadcasted_iota(jnp.int32, (count, count), axis)
    owner_col = jnp.sum(jnp.where(grid(0) == grid(1), owner_row, 0), axis=1, keepdims=True)
    same = owner_col == owner_row
    rank = jnp.sum(jnp.where((grid(0) < grid(1)) & same, 1, 0), axis=0, keepdims=True)
    rank_col = jnp.sum(jnp.where((grid(1) < grid(0)) & same, 1, 0), axis=1, keepdims=True)
    hit = owner_row == lax.broadcasted_iota(jnp.int32, (tile_count, count), 0)
    lane = lax.broadcasted_iota(jnp.int32, (tile_count, LANES), 1)
    rows = jnp.zeros((tile_count, LANES), jnp.int32)
    for c in range(CAP):
        asked = jnp.sum(jnp.where(hit & (rank == c), wanted_row, 0), axis=1, keepdims=True)
        rows = jnp.where(lane == c, asked, rows)
    used = owner_col * CAP + rank_col == lax.broadcasted_iota(jnp.int32, (count, LANES), 1)
    block = jnp.sum(jnp.where(used, lax.broadcasted_iota(jnp.int32, (count, LANES), 0), 0), axis=0, keepdims=True)
    return rows, owner_row * CAP + rank, block


FRONT = 32
SPAN = 8 * (2 * REACH + 1)


def whole_kernel(
    tile_count, patch_ref, prior_ref, block_ref, row_ref, want_ref, flow_ref, valid_ref, stiff_ref, first_ref,
    second_ref, third_ref, fourth_ref, map_ref, mesh_ref, rows_buf, block_buf, low_buf, high_buf, wire_buf, send_buf,
    arrived_buf, spec_buf, field_buf, map_buf, slot_peak, peak_buf, own_buf, held, window_buf, ask_buf, heard_buf, list_buf,
    index_buf, told_smem, index_smem, conf_own, conf_held, conf_pack, conf_window, s_buf, w_buf, f_buf, u_buf,
    mid_buf, spread_own, spread_held, local, send_r, recv_r, send_a, recv_a, send_b, recv_b, send_p,
    recv_p, send_c, recv_c, send_d, recv_d, send_m, recv_m, send_s, recv_s,
):
    gz, tile = lax.axis_index("gz"), lax.axis_index("tile")
    component, part = lax.rem(gz, 2), gz // 2
    mid_buf[...] = jnp.zeros_like(mid_buf)
    after, before = lax.rem(gz + 1, GZ), lax.rem(gz + GZ - 1, GZ)
    barrier = pltpu.get_barrier_semaphore()

    def greet(peer):
        pl.semaphore_signal(barrier, inc=1, device_id=peer, device_id_type=MESH)

    def greet_tiles(d, carry):
        peer = lax.rem(tile + d, tile_count)
        greet((after, peer))
        greet((before, peer))

        return carry

    lax.fori_loop(0, tile_count, greet_tiles, 0)
    for d in range(2, GZ - 1):
        greet((lax.rem(gz + d, GZ), tile))
    for d in (0, 2, 4, 6):
        for e in range(1, REACH + 1):
            for sign in (e, tile_count - e):
                greet((lax.rem(gz + d, GZ), lax.rem(tile + sign, tile_count)))

    from_prior = pltpu.make_async_copy(prior_ref, rows_buf, local.at[0])
    from_patches = pltpu.make_async_copy(patch_ref.at[0], rows_buf, local.at[0])
    load_blocks = pltpu.make_async_copy(block_ref.at[0], block_buf, local.at[1])

    @pl.when(gz == GZ - 1)
    def _():
        from_prior.start()

    @pl.when(gz != GZ - 1)
    def _():
        from_patches.start()

    load_blocks.start()

    rows, slot_row, block_row = request_rows(row_ref[...], want_ref[...], tile_count)
    count = slot_row.shape[1]
    index_buf[0:1, 0:count] = slot_row
    index_buf[1:2, :] = block_row
    index = pltpu.make_async_copy(index_buf, index_smem, local.at[6])
    index.start()
    for j in range(8):
        ask_buf[pl.ds(j, tile_count, stride=8), :] = rows
    columns = stiff_ref.shape[2]
    lane = lax.broadcasted_iota(jnp.int32, (columns, columns), 1)
    order = 2 * lax.rem(lane, columns // 2) + lane // (columns // 2)
    pick = jnp.where(lax.broadcasted_iota(jnp.int32, (columns, columns), 0) == order, 1.0, 0.0).astype(jnp.bfloat16)
    spring = stiff_ref[0] * valid_ref[0].astype(jnp.float32)
    for c in range(2):
        nodes = jnp.concatenate([spring, flow_ref[0, c]], axis=0).astype(jnp.bfloat16)
        own_buf[c] = jnp.dot(nodes, pick, preferred_element_type=jnp.float32).astype(jnp.bfloat16)

    @pl.when(gz == GZ - 1)
    def _():
        from_prior.wait()

    @pl.when(gz != GZ - 1)
    def _():
        from_patches.wait()

    to_images(rows_buf, low_buf, high_buf)

    pl.semaphore_wait(barrier, 2 * tile_count + GZ - 3 + 8 * REACH)

    springs = exchange_gz(lambda peer: own_buf.at[lax.rem(peer, 2)], held, send_a, recv_a)
    mine = pltpu.make_async_copy(own_buf.at[lax.rem(gz, 2)], held.at[gz], local.at[2])
    mine.start()

    def request(d):
        peer = lax.rem(tile + d, tile_count)
        part = lambda t: pl.ds(pl.multiple_of(8 * t, 8), 8)
        return pltpu.make_async_remote_copy(
            src_ref=ask_buf.at[part(peer)], dst_ref=heard_buf.at[part(tile)], send_sem=send_r.at[d],
            recv_sem=recv_r.at[d], device_id=(before, peer), device_id_type=MESH,
        )

    def each(first, last, act):
        def body(d, carry):
            act(d)
            return carry

        lax.fori_loop(first, last, body, 0)

    each(0, tile_count, lambda d: request(d).start())

    mine.wait()
    for copy in springs:
        copy.wait()
    springs = exchange_tiles(tile_count, held, window_buf, send_b, recv_b)
    mine = pltpu.make_async_copy(held, window_buf.at[REACH], local.at[2])
    mine.start()
    each(0, tile_count, lambda d: request(d).wait())
    list_buf[...] = heard_buf[pl.ds(0, tile_count, stride=8), :]
    told = pltpu.make_async_copy(list_buf, told_smem, local.at[3])
    told.start()
    patch_batch(low_buf, high_buf, first_ref, second_ref, wire_buf)
    told.wait()

    def parcel(d):
        peer = lax.rem(tile + d, tile_count)
        return pltpu.make_async_remote_copy(
            src_ref=send_buf.at[peer], dst_ref=arrived_buf.at[tile], send_sem=send_p.at[d], recv_sem=recv_p.at[d],
            device_id=(after, peer), device_id_type=MESH,
        )

    halfway = tile_count // 2

    def post(k):
        for d in (k, k + halfway):
            peer = lax.rem(tile + d, tile_count)
            for c in range(CAP):
                send_buf[peer, WIRE * c : WIRE * c + WIRE, :] = wire_buf[told_smem[peer, c]]
            parcel(d).start()

    each(0, halfway, post)
    for buf in (w_buf, f_buf, u_buf):
        buf[...] = jnp.zeros_like(buf)

    load_blocks.wait()
    for half in range(2):
        batch = pl.ds(BATCH * half, BATCH)
        to_images(block_buf.at[batch], low_buf, high_buf)
        block_batch(low_buf, high_buf, first_ref, second_ref, spec_buf.at[batch])
    index.wait()
    mine.wait()
    for copy in springs:
        copy.wait()

    inner = lax.broadcasted_iota(jnp.int32, (P_SIZE, LANES), 1) < P_SIZE - LANES

    def match(k):
        for d in (k, k + halfway):
            parcel(d).wait_recv()
        for d in (k, k + halfway):
            source = lax.rem(tile - d + tile_count, tile_count)
            for c in range(CAP):
                wire = arrived_buf[source, WIRE * c : WIRE * c + WIRE, :].astype(jnp.float32)
                block = index_smem[1, CAP * source + c]
                quarter = lambda q: spec_buf[block, :, LANES * q : LANES * q + LANES]
                field = match_one(wire, quarter, third_ref, fourth_ref)
                field_buf[CAP * source + c] = field
                top = jnp.maximum(field[:, :LANES], jnp.where(inner, field[:, LANES:], field[:, :LANES]))
                top = jnp.max(jnp.max(top, axis=0, keepdims=True), axis=1, keepdims=True)
                slot_peak[pl.ds(CAP * source + c, 1), :] = jnp.broadcast_to(top, (1, LANES))

    each(0, halfway, match)

    def store_maps(half):
        batch = pl.ds(BATCH * half, BATCH)

        def collect(n):
            field = field_buf[index_smem[0, BATCH * half + n]]
            at = pl.ds(pl.multiple_of(P_SIZE * n, 8), P_SIZE)
            low_buf[at, :] = field[:, :LANES]
            high_buf[at, :] = field[:, LANES:]

        each(0, BATCH, collect)
        to_rows(low_buf, high_buf, map_buf.at[batch])
        store = pltpu.make_async_copy(map_buf.at[batch], map_ref.at[batch], local.at[4 + half])
        store.start()
        return store

    for n in range(count):
        peak_buf[n : n + 1, :] = slot_peak[pl.ds(index_smem[0, n], 1), :]
    peak = peak_buf[...].astype(jnp.bfloat16).astype(jnp.float32)
    peak = jnp.concatenate([peak] * (columns // LANES), axis=1)
    block = lax.rem(lax.broadcasted_iota(jnp.int32, (count, columns), 1), columns // 2) // (columns // 2 // count)
    own = block == lax.broadcasted_iota(jnp.int32, (count, columns), 0)
    confidence = jnp.sum(jnp.where(own, peak / (1.0 + peak), 0.0), axis=0, keepdims=True)
    conf_own[...] = jnp.broadcast_to(confidence, conf_own.shape)
    copies = exchange_gz(lambda peer: conf_own, conf_held, send_c, recv_c)
    conf_held[gz] = conf_own[...]
    stores = [store_maps(0)]
    for copy in copies:
        copy.wait()
    for s in range(GZ):
        conf_pack[s : s + 1, :] = conf_held[s, 0:1, :]
    copies = exchange_tiles(tile_count, conf_pack, conf_window, send_d, recv_d)
    conf_window[REACH] = conf_pack[...]
    stores.append(store_maps(1))
    for copy in copies:
        copy.wait()

    first_slot = jnp.maximum(REACH - tile, 0)
    last_slot = jnp.minimum(REACH + tile_count - tile, 2 * REACH + 1)
    lane = lax.broadcasted_iota(jnp.int32, (1, 8, LANES), 2)
    first_lane, last_lane = lane == 0, lane == LANES - 1
    section = lax.broadcasted_iota(jnp.int32, (8, columns), 0)

    def picked(j):
        return jnp.concatenate([s_buf[h, pl.ds(j, 8, stride=16), :] for h in range(2)], axis=1)

    def prepare(k, carry):
        conf = jnp.where(section == 0, 0.0, 0.15 * conf_window[k])
        nodes = window_buf[k].astype(jnp.float32).reshape(LANES, columns)
        s_buf[0], s_buf[1] = nodes[:, :LANES], nodes[:, LANES:]
        for j in range(8):
            i = FRONT + 8 * k + j
            w = picked(j) * conf
            wf = w * picked(8 + j)
            w_buf[i] = w
            f_buf[i] = wf
            u_buf[0, i] = wf - pltpu.roll(wf, 7, 0)
        return carry

    lax.fori_loop(first_slot, last_slot, prepare, 0)

    def step(source, target, s):
        low = jnp.maximum((2 * part + s) // 8, first_slot)
        high = jnp.minimum((2 * part + 2 * PHASE + 2 - s + 7) // 8, last_slot)
        i = FRONT + 8 * low

        def advance(slots):
            rows = 8 * slots
            even, odd = [source[pl.ds(i - 1, rows + 2), :, LANES * h : LANES * h + LANES] for h in range(2)]
            to_left = jnp.where(first_lane, 0.0, pltpu.roll(odd[1:-1], 1, 2))
            to_right = jnp.where(last_lane, 0.0, pltpu.roll(even[1:-1], LANES - 1, 2))
            for h, (x, beside, other) in enumerate(((even, odd[1:-1], to_left), (odd, even[1:-1], to_right))):
                at = (pl.ds(i, rows), slice(None), slice(LANES * h, LANES * h + LANES))
                mid = x[1:-1]
                around = (x[:-2] + x[2:]) + (beside + other)
                force = w_buf[at] * (pltpu.roll(mid, 1, 1) - mid) + f_buf[at]
                target[at] = (0.4 * mid + 0.15 * around) + (force - pltpu.roll(force, 7, 1))

        for slots in range(1, 2 * REACH + 2):

            @pl.when(high - low == slots)
            def _():
                advance(slots)

    ping, pong = u_buf.at[0], u_buf.at[1]

    def run_step(s, carry):
        step(u_buf.at[lax.rem(s, 2)], u_buf.at[1 - lax.rem(s, 2)], s)
        return carry

    def rest_of_phase():
        lax.fori_loop(2, PHASE + 1, run_step, 0)

    base = FRONT + 8 * REACH + 2 * part
    rest_of_phase()

    place = 4 * tile + part
    places = 4 * tile_count

    def handover(n):
        e = jnp.where(n < 4 * REACH, n + 1, 4 * REACH - 1 - n)
        peer = lax.rem(place + e + places, places)
        row = FRONT + 8 * REACH + 2 * lax.rem(part + e + 4 * REACH, 4) - 2 * e
        copy = pltpu.make_async_remote_copy(
            src_ref=pong.at[pl.ds(base, 2)], dst_ref=mid_buf.at[pl.ds(row, 2)], send_sem=send_m.at[n],
            recv_sem=recv_m.at[n], device_id=(2 * lax.rem(peer, 4) + component, peer // 4), device_id_type=MESH,
        )
        sends = (place + e >= 0) & (place + e < places)
        receives = (place - e >= 0) & (place - e < places)
        return copy, sends, receives

    def hand_out(n):
        copy, sends, _ = handover(n)

        @pl.when(sends)
        def _():
            copy.start()

    def take_in(n):
        copy, sends, receives = handover(n)

        @pl.when(sends)
        def _():
            copy.wait_send()

        @pl.when(receives)
        def _():
            copy.wait_recv()

    each(0, 8 * REACH, hand_out)
    mid_buf[pl.ds(base, 2)] = pong[pl.ds(base, 2)]
    each(0, 8 * REACH, take_in)
    step(mid_buf, ping, 1)
    rest_of_phase()

    for s in range(GZ):
        for r in range(2):
            spread_own[s, r : r + 1, :] = pong[base + r, s : s + 1, :]
    copies = exchange_gz(lambda peer: spread_own.at[peer], spread_held, send_s, recv_s)
    spread_held[gz] = spread_own[gz]
    order = lax.broadcasted_iota(jnp.int32, (columns, columns), 1)
    order = order // 2 + lax.rem(order, 2) * (columns // 2)
    spot = lax.broadcasted_iota(jnp.int32, (columns, columns), 0) == order
    pick = jnp.where(spot, 1.0, 0.0).astype(jnp.bfloat16)
    for copy in copies:
        copy.wait()
    rest = jnp.concatenate([spread_held[2 * h + c, 0:2, :] for c in range(2) for h in range(4)], axis=0)
    total = jnp.zeros_like(rest)
    for _ in range(3):
        piece = rest.astype(jnp.bfloat16)
        rest = rest - piece.astype(jnp.float32)
        total = total + jnp.dot(piece, pick, preferred_element_type=jnp.float32)
    mesh_ref[0] = total[:8]
    mesh_ref[1] = total[8:]
    for copy in stores:
        copy.wait()
    each(0, tile_count, lambda d: parcel(d).wait_send())


def whole(tile_count, patches, prior, blocks, row, want, flows, valid, stiffness, *fixed):
    count = blocks.shape[1]
    columns = flows.shape[3]
    rows = SPAN + 2 * FRONT
    dma = lambda number: pltpu.SemaphoreType.DMA((number,))
    vmem, anywhere = pl.BlockSpec(memory_space=pltpu.VMEM), pl.BlockSpec(memory_space=pl.ANY)
    f32, bf16, i32 = jnp.float32, jnp.bfloat16, jnp.int32
    images = pltpu.VMEM((BATCH * P_SIZE, LANES), f32)
    parcels = pltpu.VMEM((tile_count, CAP * WIRE, LANES), bf16)
    near = pltpu.VMEM((GZ, 8, columns), f32)
    return pl.pallas_call(
        functools.partial(whole_kernel, tile_count),
        out_shape=(
            jax.ShapeDtypeStruct((count, PIX), bf16),
            jax.ShapeDtypeStruct((2, 8, columns), f32),
        ),
        in_specs=[anywhere] * 3 + [vmem] * 9,
        out_specs=(anywhere, vmem),
        scratch_shapes=[
            pltpu.VMEM((BATCH, PIX), bf16),
            pltpu.VMEM((count, PIX), bf16),
            images,
            images,
            pltpu.VMEM((BATCH, WIRE, LANES), bf16),
            parcels,
            parcels,
            pltpu.VMEM((count, P_SIZE, 4 * LANES), bf16),
            pltpu.VMEM((CAP * tile_count, P_SIZE, 2 * LANES), f32),
            pltpu.VMEM((count, PIX), bf16),
            pltpu.VMEM((CAP * tile_count, LANES), f32),
            pltpu.VMEM((count, LANES), f32),
            pltpu.VMEM((2, 16, columns), bf16),
            pltpu.VMEM((GZ, 16, columns), bf16),
            pltpu.VMEM((2 * REACH + 1, GZ, 16, columns), bf16),
            pltpu.VMEM((8 * tile_count, LANES), i32),
            pltpu.VMEM((8 * tile_count, LANES), i32),
            pltpu.VMEM((tile_count, LANES), i32),
            pltpu.VMEM((8, LANES), i32),
            pltpu.SMEM((tile_count, LANES), i32),
            pltpu.SMEM((8, LANES), i32),
            pltpu.VMEM((8, columns), f32),
            near,
            pltpu.VMEM((GZ, columns), f32),
            pltpu.VMEM((2 * REACH + 1, GZ, columns), f32),
            pltpu.VMEM((2, LANES, LANES), f32),
            pltpu.VMEM((rows, 8, columns), f32),
            pltpu.VMEM((rows, 8, columns), f32),
            pltpu.VMEM((2, rows, 8, columns), f32),
            pltpu.VMEM((rows, 8, columns), f32),
            near,
            near,
            dma(7),
        ]
        + [dma(tile_count)] * 2
        + [dma(GZ - 1)] * 2
        + [dma(2 * REACH)] * 2
        + [dma(tile_count)] * 2
        + [dma(GZ - 1)] * 2
        + [dma(2 * REACH)] * 2
        + [dma(8 * REACH)] * 2
        + [dma(GZ - 1)] * 2,
        compiler_params=pltpu.CompilerParams(
            collective_id=1, has_side_effects=True, vmem_limit_bytes=60 * 1024 * 1024
        ),
        cost_estimate=pl.CostEstimate(flops=30_000_000_000, bytes_accessed=32_000_000, transcendentals=0),
    )(patches, prior, blocks, row, want, flows, valid, stiffness, *fixed)


def on_device(patches, prior_patches, blocks, dest, target, flows, valid, stiffness):
    corr_maps, mesh_nodes = whole(
        lax.axis_size("tile"), patches, prior_patches, blocks, dest[:, :, 0], target, flows, valid, stiffness, *tables()
    )
    return (corr_maps[None], mesh_nodes[None])


def solution(mesh):
    return jax.shard_map(
        on_device,
        mesh=mesh,
        in_specs=(
            P("gz", "tile", None),
            P("tile", None),
            P("gz", "tile", None),
            P("gz", "tile", None),
            P("gz", "tile"),
            P("gz", None, "tile", None),
            P("gz", "tile", None),
            P("gz", "tile", None),
        ),
        out_specs=(P("gz", "tile", None), P("gz", None, "tile", None)),
        check_vma=False,
    )
```

```python
import functools

import jax
import jax.numpy as jnp
import ml_dtypes
import numpy as np
from jax import lax
from jax.experimental import pallas as pl
from jax.experimental.pallas import tpu as pltpu
from jax.sharding import PartitionSpec as P

P_SIZE = 160
PIX = 25600
CAP = 2
ITERS = 64
PHASE = ITERS // 2
UNROLL = 8


LANES = 128
HALF = 64
WIRE = 208
BATCH = 16


def tables():
    size = P_SIZE
    line = np.arange(size)
    angles = (np.outer(line, line) % size).astype(np.float32) * np.float32(2.0 * np.pi / size)
    rounded = lambda x: x.astype(ml_dtypes.bfloat16).astype(np.float32)
    cos_t, sin_t = rounded(np.cos(angles)), rounded(np.sin(angles))
    lane = np.arange(2 * LANES)
    column = HALF * (lane // LANES) + lane % HALF
    used = column <= size // 2
    column = np.where(used, column, 0)
    real = lane % LANES < HALF
    c, s = cos_t[:, column] * used, sin_t[:, column] * used
    first = np.zeros((2 * LANES, 4 * LANES), np.float32)
    first[:size, : 2 * LANES] = np.where(real, c, s)
    first[:size, 2 * LANES :] = np.where(real, -s, c)
    second = np.concatenate([cos_t, sin_t], axis=1)
    third = np.concatenate([cos_t, sin_t], axis=0)
    twice = np.where((column == 0) | (column == size // 2), 1.0, 2.0)
    fourth = np.zeros((4 * LANES, 2 * LANES), np.float32)
    fourth[: 2 * LANES, :size] = (np.where(real, c, -s) * twice).T
    fourth[2 * LANES :, :size] = (np.where(real, -s, -c) * twice).T
    return [jnp.asarray(x, jnp.bfloat16) for x in (first, second, third, fourth)]


def to_images(rows_ref, low_buf, high_buf):
    parts = PIX // 640
    chunk = lambda m: rows_ref[:, pl.ds(pl.multiple_of(640 * m, LANES), 640)].astype(jnp.float32)
    fold = lambda x: sum(x[:, LANES * k : LANES * k + LANES] for k in range(5))
    zero = jnp.zeros((BATCH, LANES), jnp.float32)
    sums = lax.fori_loop(0, parts, lambda m, t: t + fold(chunk(m)), zero)
    mean = jnp.sum(sums, axis=1, keepdims=True) * (1.0 / PIX)

    def square(m, t):
        x = chunk(m) - mean
        return t + fold(x * x)

    sums = lax.fori_loop(0, parts, square, zero)
    scale = lax.rsqrt(jnp.sum(sums, axis=1, keepdims=True) * (1.0 / PIX) + 1e-05)
    lane = lax.broadcasted_iota(jnp.int32, (BATCH, LANES), 1)

    def place(m, carry):
        x = (chunk(m) - mean) * scale
        t = [x[:, LANES * k : LANES * k + LANES] for k in range(5)]
        low = [
            t[0],
            pltpu.roll(jnp.where(lane < 32, t[2], t[1]), 96, 1),
            pltpu.roll(jnp.where(lane < 64, t[3], t[2]), 64, 1),
            pltpu.roll(jnp.where(lane < 96, t[4], t[3]), 32, 1),
        ]
        high = [t[1], pltpu.roll(t[2], 96, 1), pltpu.roll(t[3], 64, 1), pltpu.roll(t[4], 32, 1)]
        for k in range(4):
            at = pl.ds(4 * m + k, BATCH, stride=P_SIZE)
            low_buf[at, :] = low[k]
            high_buf[at, :] = high[k]
        return carry

    lax.fori_loop(0, parts, place, 0)


def image_spectrum(n, low_buf, high_buf, first_ref, second_ref):
    at = pl.ds(pl.multiple_of(P_SIZE * n, 8), P_SIZE)
    image = jnp.concatenate([low_buf[at, :], high_buf[at, :]], axis=1).astype(jnp.bfloat16)
    first = jnp.dot(image, first_ref[...], preferred_element_type=jnp.float32).astype(jnp.bfloat16)
    both = jnp.concatenate([first[:, : 2 * LANES], first[:, 2 * LANES :]], axis=0)
    return jnp.dot(second_ref[...], both, preferred_element_type=jnp.float32)


def block_batch(low_buf, high_buf, first_ref, second_ref, out_ref):
    low_half = lax.broadcasted_iota(jnp.int32, (P_SIZE, LANES), 1) < HALF

    def image(n, carry):
        spec = image_spectrum(n, low_buf, high_buf, first_ref, second_ref)
        for h in range(2):
            x = spec[:, LANES * h : LANES * h + LANES]
            swapped = pltpu.roll(x, HALF, 1)
            out_ref[n, :, LANES * h : LANES * h + LANES] = jnp.where(low_half, x, swapped).astype(jnp.bfloat16)
            at = slice(LANES * (2 + h), LANES * (3 + h))
            out_ref[n, :, at] = jnp.where(low_half, swapped, -x).astype(jnp.bfloat16)
        return carry

    lax.fori_loop(0, BATCH, image, 0, unroll=UNROLL)


def patch_batch(low_buf, high_buf, first_ref, second_ref, wire_buf):
    lane = lax.broadcasted_iota(jnp.int32, (8, LANES), 1) % HALF

    def image(n, carry):
        spec = image_spectrum(n, low_buf, high_buf, first_ref, second_ref)
        rest = [spec[8 * i : 8 * i + 8, LANES:] for i in range(20)]
        pieces = [spec[:, :LANES]]
        for i in range(5):
            pieces.append(sum(pltpu.roll(jnp.where(lane < 16, rest[5 * b + i], 0.0), 16 * b, 1) for b in range(4)))
        pieces.append(sum(pltpu.roll(jnp.where(lane == 16, rest[i], 0.0), (i + 112) % LANES, 1) for i in range(20)))
        wire_buf[n] = jnp.concatenate(pieces, axis=0).astype(jnp.bfloat16)
        return carry

    lax.fori_loop(0, BATCH, image, 0, unroll=UNROLL)


def match_one(wire, block_of, third_ref, fourth_ref):
    lane8 = lax.broadcasted_iota(jnp.int32, (8, LANES), 1) % HALF == 16
    last = wire[200:208]
    rest = []
    for i in range(20):
        part = wire[160 + 8 * (i % 5) : 168 + 8 * (i % 5)]
        part = pltpu.roll(part, (LANES - 16 * (i // 5)) % LANES, 1)
        rest.append(jnp.where(lane8, pltpu.roll(last, (16 - i) % LANES, 1), part))
    cross = []
    for h, a in enumerate((wire[:P_SIZE], jnp.concatenate(rest, axis=0))):
        straight, swapped = block_of(h).astype(jnp.float32), block_of(2 + h).astype(jnp.float32)
        cross.append((a * straight + pltpu.roll(a, HALF, 1) * swapped).astype(jnp.bfloat16))
    back = jnp.dot(third_ref[...], jnp.concatenate(cross, axis=1), preferred_element_type=jnp.float32)
    back = back.astype(jnp.bfloat16)
    back = jnp.concatenate([back[:P_SIZE], back[P_SIZE:]], axis=1)
    return jnp.dot(back, fourth_ref[...], preferred_element_type=jnp.float32) * (1.0 / float(P_SIZE) ** 3)


def to_rows(low_buf, high_buf, map_ref):
    lane = lax.broadcasted_iota(jnp.int32, (BATCH, LANES), 1)

    def place(m, carry):
        load = lambda buf, k: buf[pl.ds(4 * m + k, BATCH, stride=P_SIZE), :]
        low = [load(low_buf, 0)] + [pltpu.roll(load(low_buf, k), 32 * k, 1) for k in range(1, 4)]
        high = [load(high_buf, 0)] + [pltpu.roll(load(high_buf, k), 32 * k, 1) for k in range(1, 4)]
        tiles = [
            low[0],
            jnp.where(lane < 32, high[0], low[1]),
            jnp.where(lane < 32, low[1], jnp.where(lane < 64, high[1], low[2])),
            jnp.where(lane < 64, low[2], jnp.where(lane < 96, high[2], low[3])),
            jnp.where(lane < 96, low[3], high[3]),
        ]
        rows = jnp.concatenate(tiles, axis=1).astype(jnp.bfloat16)
        map_ref[:, pl.ds(pl.multiple_of(640 * m, LANES), 640)] = rows
        return carry

    lax.fori_loop(0, P_SIZE // 4, place, 0, unroll=2)


MESH = pl.DeviceIdType.MESH
GZ = 8
REACH = 4


def group_barrier(peers):
    barrier = pltpu.get_barrier_semaphore()
    for peer in peers:
        pl.semaphore_signal(barrier, inc=1, device_id=peer, device_id_type=MESH)
    pl.semaphore_wait(barrier, len(peers))


def gz_peers():
    gz, tile = lax.axis_index("gz"), lax.axis_index("tile")
    return [(lax.rem(gz + d, GZ), tile) for d in range(1, GZ)]


def tile_peers(tile_count):
    gz, tile = lax.axis_index("gz"), lax.axis_index("tile")
    offsets = [e for k in range(1, REACH + 1) for e in (k, -k)]
    return offsets, [(gz, lax.rem(tile + e + tile_count, tile_count)) for e in offsets]


def exchange_gz(source_of, held, send, recv):
    gz = lax.axis_index("gz")
    copies = []
    for d, peer in enumerate(gz_peers()):
        copies.append(
            pltpu.make_async_remote_copy(
                src_ref=source_of(peer[0]), dst_ref=held.at[gz], send_sem=send.at[d], recv_sem=recv.at[d],
                device_id=peer, device_id_type=MESH,
            )
        )
    for copy in copies:
        copy.start()
    return copies


def exchange_tiles(tile_count, source, window, send, recv):
    offsets, peers = tile_peers(tile_count)
    copies = []
    for n, (e, peer) in enumerate(zip(offsets, peers)):
        copies.append(
            pltpu.make_async_remote_copy(
                src_ref=source, dst_ref=window.at[REACH - e], send_sem=send.at[n], recv_sem=recv.at[n],
                device_id=peer, device_id_type=MESH,
            )
        )
    for copy in copies:
        copy.start()
    return copies


def request_rows(owner_row, wanted_row):
    count = owner_row.shape[1]
    grid = lambda axis: lax.broadcasted_iota(jnp.int32, (count, count), axis)
    column = lambda row: jnp.sum(jnp.where(grid(0) == grid(1), row, 0), axis=1, keepdims=True)
    owner_col = column(owner_row)
    same = owner_col == owner_row
    rank = jnp.sum(jnp.where((grid(0) < grid(1)) & same, 1, 0), axis=0, keepdims=True)
    rank_col = jnp.sum(jnp.where((grid(1) < grid(0)) & same, 1, 0), axis=1, keepdims=True)
    used = owner_col * CAP + rank_col == lax.broadcasted_iota(jnp.int32, (count, LANES), 1)
    total = lambda values: jnp.sum(jnp.where(used, values, 0), axis=0, keepdims=True)
    block = total(lax.broadcasted_iota(jnp.int32, (count, LANES), 0))
    return owner_row * CAP + rank, block, total(column(wanted_row))


SIDE = 4
STEPS = 2
KINDS = ((0, 0), (-1, 0), (1, 0), (-2, 0), (2, 0), (-2, 1), (2, -1), (-2, 2), (2, -2))


FRONT = 32
SPAN = 8 * (2 * REACH + 1)


def whole_kernel(
    tile_count, patch_ref, prior_ref, block_ref, row_ref, want_ref, flow_ref, valid_ref, stiff_ref, first_ref,
    second_ref, third_ref, fourth_ref, map_ref, mesh_ref, rows_buf, block_buf, low_buf, high_buf, wire_buf, send_buf,
    arrived_buf, spec_buf, field_buf, map_buf, slot_peak, peak_buf, own_buf, held, window_buf, near_up, far_up, near_down, far_down, ask_buf, heard_buf,
    list_buf, index_buf, told_smem, index_smem, conf_own, conf_held, conf_pack, conf_window, s_buf, w_buf, f_buf, u_buf,
    mid_buf, mid_wire, mid_own, spread_own, spread_held, local, send_r, recv_r, send_a, recv_a, send_b, recv_b, send_h, recv_h, send_p,
    recv_p, send_c, recv_c, send_d, recv_d, send_m, recv_m, send_s, recv_s,
):
    gz, tile = lax.axis_index("gz"), lax.axis_index("tile")
    component, part = lax.rem(gz, 2), gz // 2
    mid_wire[...] = jnp.zeros_like(mid_wire)
    after, before = lax.rem(gz + 1, GZ), lax.rem(gz + GZ - 1, GZ)
    barrier = pltpu.get_barrier_semaphore()

    def greet(peer):
        pl.semaphore_signal(barrier, inc=1, device_id=peer, device_id_type=MESH)

    plane, spot_in_plane = tile // SIDE, lax.rem(tile, SIDE)
    planes = tile_count // SIDE

    def tile_at(offset, y):
        return lax.rem(plane + offset + planes, planes) * SIDE + y

    def greet_planes(n, carry):
        peer = tile_at(n // SIDE - STEPS, lax.rem(n, SIDE))
        greet((after, peer))
        greet((before, peer))
        return carry

    asks = SIDE * (2 * STEPS + 1)
    heard_buf[8 * asks :, :] = jnp.zeros((heard_buf.shape[0] - 8 * asks, LANES), jnp.int32)
    lax.fori_loop(0, asks, greet_planes, 0)
    for d in range(2, GZ - 1):
        greet((lax.rem(gz + d, GZ), tile))
    for d in (0, 2, 4, 6):
        for e in range(1, REACH + 1):
            for sign in (e, tile_count - e):
                greet((lax.rem(gz + d, GZ), lax.rem(tile + sign, tile_count)))

    from_prior = pltpu.make_async_copy(prior_ref, rows_buf, local.at[0])
    from_patches = pltpu.make_async_copy(patch_ref.at[0], rows_buf, local.at[0])
    load_blocks = pltpu.make_async_copy(block_ref.at[0], block_buf, local.at[1])

    @pl.when(gz == GZ - 1)
    def _():
        from_prior.start()

    @pl.when(gz != GZ - 1)
    def _():
        from_patches.start()

    load_blocks.start()

    slot_row, block_row, asked_row = request_rows(row_ref[...], want_ref[...])
    count = slot_row.shape[1]
    index_buf[0:1, 0:count] = slot_row
    index_buf[1:2, :] = block_row
    index = pltpu.make_async_copy(index_buf, index_smem, local.at[6])
    index.start()
    ask_buf[...] = jnp.broadcast_to(asked_row, ask_buf.shape)
    columns = stiff_ref.shape[2]
    lane = lax.broadcasted_iota(jnp.int32, (columns, columns), 1)
    order = 2 * lax.rem(lane, columns // 2) + lane // (columns // 2)
    pick = jnp.where(lax.broadcasted_iota(jnp.int32, (columns, columns), 0) == order, 1.0, 0.0).astype(jnp.bfloat16)
    spring = stiff_ref[0] * valid_ref[0].astype(jnp.float32)
    for c in range(2):
        nodes = jnp.concatenate([spring, flow_ref[0, c]], axis=0).astype(jnp.bfloat16)
        own_buf[c] = jnp.dot(nodes, pick, preferred_element_type=jnp.float32).astype(jnp.bfloat16)

    @pl.when(gz == GZ - 1)
    def _():
        from_prior.wait()

    @pl.when(gz != GZ - 1)
    def _():
        from_patches.wait()

    to_images(rows_buf, low_buf, high_buf)

    pl.semaphore_wait(barrier, 2 * asks + GZ - 3 + 8 * REACH)

    springs = exchange_gz(lambda peer: own_buf.at[lax.rem(peer, 2)], held, send_a, recv_a)
    mine = pltpu.make_async_copy(own_buf.at[lax.rem(gz, 2)], held.at[gz], local.at[2])
    mine.start()

    def request(n, landing):
        peer = tile_at(n // SIDE - STEPS, lax.rem(n, SIDE))
        return pltpu.make_async_remote_copy(
            src_ref=ask_buf, dst_ref=heard_buf.at[pl.ds(pl.multiple_of(8 * landing, 8), 8)], send_sem=send_r.at[n],
            recv_sem=recv_r.at[landing], device_id=(before, peer), device_id_type=MESH,
        )

    def each(first, last, act):
        def body(d, carry):
            act(d)
            return carry

        lax.fori_loop(first, last, body, 0)

    each(0, asks, lambda n: request(n, n // SIDE * SIDE + spot_in_plane).start())

    mine.wait()
    for copy in springs:
        copy.wait()
    springs = exchange_tiles(tile_count, held, window_buf, send_b, recv_b)
    mine = pltpu.make_async_copy(held, window_buf.at[REACH], local.at[2])
    mine.start()
    each(0, asks, lambda n: request(n, n).wait())
    list_buf[...] = heard_buf[pl.ds(0, list_buf.shape[0], stride=8), :]
    told = pltpu.make_async_copy(list_buf, told_smem, local.at[3])
    told.start()
    patch_batch(low_buf, high_buf, first_ref, second_ref, wire_buf)
    told.wait()

    def hop(up, far, chunk):
        near, end = (near_up, far_up) if up else (near_down, far_down)
        batch = pl.ds(BATCH // 2 * chunk, BATCH // 2)
        number = 4 * int(up) + 2 * int(far) + chunk
        return pltpu.make_async_remote_copy(
            src_ref=(near if far else wire_buf).at[batch], dst_ref=(end if far else near).at[batch],
            send_sem=send_h.at[number], recv_sem=recv_h.at[number],
            device_id=(gz, tile_at(1 if up else -1, spot_in_plane)), device_id_type=MESH,
        )

    def parcel(kind, y_to, source, landing):
        if isinstance(kind, int) and kind >= 7:
            half = pl.ds(WIRE * (kind - 7), WIRE)
            outgoing, incoming = send_buf.at[28 + y_to, half], arrived_buf.at[source, half]
        else:
            outgoing, incoming = send_buf.at[SIDE * kind + y_to], arrived_buf.at[source]
        reach = KINDS[kind][1] if isinstance(kind, int) else 0
        return pltpu.make_async_remote_copy(
            src_ref=outgoing, dst_ref=incoming, send_sem=send_p.at[SIDE * kind + y_to],
            recv_sem=recv_p.at[SIDE * kind + landing], device_id=(after, tile_at(reach, y_to)), device_id_type=MESH,
        )

    def post(kind, held_patches):
        offset, reach = KINDS[kind]
        source = tile_at(offset, spot_in_plane)

        def one(y):
            listed = (STEPS - reach) * SIDE + y
            for c in range(CAP) if kind < 7 else (kind - 7,):
                entry, half = (SIDE * kind + y, c) if kind < 7 else (28 + y, c)
                patch = held_patches[told_smem[listed, CAP * source + c]]
                send_buf[entry, WIRE * half : WIRE * half + WIRE, :] = patch
            parcel(kind, y, source, spot_in_plane).start()

        each(0, SIDE, one)

    for chunk in range(2):
        for up in (True, False):
            hop(up, False, chunk).start()
    post(0, wire_buf)
    for buf in (w_buf, f_buf, u_buf, mid_buf):
        buf[...] = jnp.zeros_like(buf)

    load_blocks.wait()
    for half in range(2):
        batch = pl.ds(BATCH * half, BATCH)
        to_images(block_buf.at[batch], low_buf, high_buf)
        if half == 0:
            for up in (True, False):
                hop(up, False, 0).wait_recv()
                hop(up, True, 0).start()
        block_batch(low_buf, high_buf, first_ref, second_ref, spec_buf.at[batch])
    for up in (True, False):
        hop(up, False, 1).wait_recv()
        hop(up, True, 1).start()
    post(1, near_up)
    post(2, near_down)
    index.wait()
    mine.wait()
    for copy in springs:
        copy.wait()
    inner = lax.broadcasted_iota(jnp.int32, (P_SIZE, LANES), 1) < P_SIZE - LANES

    def match_slot(source, c):
        wire = arrived_buf[source, WIRE * c : WIRE * c + WIRE, :].astype(jnp.float32)
        block = index_smem[1, CAP * source + c]
        quarter = lambda q: spec_buf[block, :, LANES * q : LANES * q + LANES]
        field = match_one(wire, quarter, third_ref, fourth_ref)
        field_buf[CAP * source + c] = field
        top = jnp.maximum(field[:, :LANES], jnp.where(inner, field[:, LANES:], field[:, :LANES]))
        top = jnp.max(jnp.max(top, axis=0, keepdims=True), axis=1, keepdims=True)
        slot_peak[pl.ds(CAP * source + c, 1), :] = jnp.broadcast_to(top, (1, LANES))

    def match(n):
        kind = n // 2
        away = (kind + 1) // 2
        offset = jnp.where(lax.rem(kind, 2) == 1, -away, away)
        pairs = []
        for y in (2 * lax.rem(n, 2), 2 * lax.rem(n, 2) + 1):
            source = tile_at(offset, y)
            parcel(kind, y, source, y).wait_recv()
            pairs.append(source)
        for source in pairs:
            for c in range(CAP):
                match_slot(source, c)

    each(0, 2, match)
    for chunk in range(2):
        for up in (True, False):
            hop(up, True, chunk).wait_recv()
    for kind, held_patches in ((7, far_up), (8, far_down), (5, far_up), (6, far_down), (3, far_up), (4, far_down)):
        post(kind, held_patches)
    each(2, 14, match)

    def match_halfway(n):
        pairs = []
        for y in (2 * n, 2 * n + 1):
            source = tile_at(planes // 2, y)
            for kind in (7, 8):
                parcel(kind, y, source, y).wait_recv()
            pairs.append(source)
        for source in pairs:
            for c in range(CAP):
                match_slot(source, c)

    each(0, SIDE // 2, match_halfway)

    def store_maps(half):
        batch = pl.ds(BATCH * half, BATCH)

        def collect(n):
            field = field_buf[index_smem[0, BATCH * half + n]]
            at = pl.ds(pl.multiple_of(P_SIZE * n, 8), P_SIZE)
            low_buf[at, :] = field[:, :LANES]
            high_buf[at, :] = field[:, LANES:]

        each(0, BATCH, collect)
        to_rows(low_buf, high_buf, map_buf.at[batch])
        store = pltpu.make_async_copy(map_buf.at[batch], map_ref.at[batch], local.at[4 + half])
        store.start()
        return store

    for n in range(count):
        peak_buf[n : n + 1, :] = slot_peak[pl.ds(index_smem[0, n], 1), :]
    peak = peak_buf[...].astype(jnp.bfloat16).astype(jnp.float32)
    peak = jnp.concatenate([peak] * (columns // LANES), axis=1)
    block = lax.rem(lax.broadcasted_iota(jnp.int32, (count, columns), 1), columns // 2) // (columns // 2 // count)
    own = block == lax.broadcasted_iota(jnp.int32, (count, columns), 0)
    confidence = jnp.sum(jnp.where(own, peak / (1.0 + peak), 0.0), axis=0, keepdims=True)
    conf_own[...] = jnp.broadcast_to(confidence, conf_own.shape)
    copies = exchange_gz(lambda peer: conf_own, conf_held, send_c, recv_c)
    conf_held[gz] = conf_own[...]
    stores = [store_maps(0)]
    for copy in copies:
        copy.wait()
    for s in range(GZ):
        conf_pack[s : s + 1, :] = conf_held[s, 0:1, :]
    copies = exchange_tiles(tile_count, conf_pack, conf_window, send_d, recv_d)
    conf_window[REACH] = conf_pack[...]
    stores.append(store_maps(1))
    for copy in copies:
        copy.wait()

    first_slot = jnp.maximum(REACH - tile, 0)
    last_slot = jnp.minimum(REACH + tile_count - tile, 2 * REACH + 1)
    lane = lax.broadcasted_iota(jnp.int32, (1, 8, LANES), 2)
    first_lane, last_lane = lane == 0, lane == LANES - 1
    section = lax.broadcasted_iota(jnp.int32, (8, columns), 0)

    def picked(j):
        return jnp.concatenate([s_buf[h, pl.ds(j, 8, stride=16), :] for h in range(2)], axis=1)

    def prepare(k, carry):
        conf = jnp.where(section == 0, 0.0, 0.15 * conf_window[k])
        nodes = window_buf[k].astype(jnp.float32).reshape(LANES, columns)
        s_buf[0], s_buf[1] = nodes[:, :LANES], nodes[:, LANES:]
        for j in range(8):
            i = FRONT + 8 * k + j
            w = picked(j) * conf
            wf = w * picked(8 + j)
            w_buf[i] = w
            f_buf[i] = wf
            u_buf[0, i] = wf - pltpu.roll(wf, 7, 0)
        return carry

    lax.fori_loop(first_slot, last_slot, prepare, 0)

    def step(source, target, s):
        low = jnp.maximum((2 * part + s) // 8, first_slot)
        high = jnp.minimum((2 * part + 2 * PHASE + 2 - s + 7) // 8, last_slot)
        i = FRONT + 8 * low

        def advance(slots):
            rows = 8 * slots
            even, odd = [source[pl.ds(i - 1, rows + 2), :, LANES * h : LANES * h + LANES] for h in range(2)]
            to_left = jnp.where(first_lane, 0.0, pltpu.roll(odd[1:-1], 1, 2))
            to_right = jnp.where(last_lane, 0.0, pltpu.roll(even[1:-1], LANES - 1, 2))
            for h, (x, beside, other) in enumerate(((even, odd[1:-1], to_left), (odd, even[1:-1], to_right))):
                at = (pl.ds(i, rows), slice(None), slice(LANES * h, LANES * h + LANES))
                mid = x[1:-1]
                around = (x[:-2] + x[2:]) + (beside + other)
                force = w_buf[at] * (pltpu.roll(mid, 1, 1) - mid) + f_buf[at]
                target[at] = (0.4 * mid + 0.15 * around) + (force - pltpu.roll(force, 7, 1))

        for slots in range(1, 2 * REACH + 2):

            @pl.when(high - low == slots)
            def _():
                advance(slots)

    ping, pong = u_buf.at[0], u_buf.at[1]

    def run_step(s, carry):
        step(u_buf.at[lax.rem(s, 2)], u_buf.at[1 - lax.rem(s, 2)], s)
        return carry

    def rest_of_phase():
        lax.fori_loop(2, PHASE + 1, run_step, 0)

    base = FRONT + 8 * REACH + 2 * part
    rest_of_phase()

    place = 4 * tile + part
    places = 4 * tile_count

    def handover(n):
        e = jnp.where(n < 4 * REACH, n + 1, 4 * REACH - 1 - n)
        peer = lax.rem(place + e + places, places)
        row = FRONT + 8 * REACH + 2 * lax.rem(part + e + 4 * REACH, 4) - 2 * e
        copy = pltpu.make_async_remote_copy(
            src_ref=mid_own, dst_ref=mid_wire.at[row // 2], send_sem=send_m.at[n],
            recv_sem=recv_m.at[n], device_id=(2 * lax.rem(peer, 4) + component, peer // 4), device_id_type=MESH,
        )
        sends = (place + e >= 0) & (place + e < places)
        receives = (place - e >= 0) & (place - e < places)
        return copy, sends, receives

    def hand_out(n):
        copy, sends, _ = handover(n)

        @pl.when(sends)
        def _():
            copy.start()

    def take_in(n):
        copy, sends, receives = handover(n)

        @pl.when(sends)
        def _():
            copy.wait_send()

        @pl.when(receives)
        def _():
            copy.wait_recv()

    mid_own[...] = pong[pl.ds(base, 2)].reshape(mid_own.shape).astype(jnp.bfloat16)
    each(0, 8 * REACH, hand_out)
    each(0, 8 * REACH, take_in)

    def widen(p):
        mid_buf[pl.ds(2 * p, 2)] = mid_wire[p].astype(jnp.float32).reshape(2, 8, columns)

    each(FRONT // 2, (FRONT + SPAN) // 2, widen)
    mid_buf[pl.ds(base, 2)] = pong[pl.ds(base, 2)]
    step(mid_buf, ping, 1)
    rest_of_phase()

    for s in range(GZ):
        for r in range(2):
            spread_own[s, r : r + 1, :] = pong[base + r, s : s + 1, :]
    copies = exchange_gz(lambda peer: spread_own.at[peer], spread_held, send_s, recv_s)
    spread_held[gz] = spread_own[gz]
    order = lax.broadcasted_iota(jnp.int32, (columns, columns), 1)
    order = order // 2 + lax.rem(order, 2) * (columns // 2)
    spot = lax.broadcasted_iota(jnp.int32, (columns, columns), 0) == order
    pick = jnp.where(spot, 1.0, 0.0).astype(jnp.bfloat16)
    for copy in copies:
        copy.wait()
    rest = jnp.concatenate([spread_held[2 * h + c, 0:2, :] for c in range(2) for h in range(4)], axis=0)
    total = jnp.zeros_like(rest)
    for _ in range(3):
        piece = rest.astype(jnp.bfloat16)
        rest = rest - piece.astype(jnp.float32)
        total = total + jnp.dot(piece, pick, preferred_element_type=jnp.float32)
    mesh_ref[0] = total[:8]
    mesh_ref[1] = total[8:]
    for copy in stores:
        copy.wait()
    each(0, 7 * SIDE, lambda n: parcel(n // SIDE, lax.rem(n, SIDE), tile, 0).wait_send())
    for kind in (7, 8):
        each(0, SIDE, lambda y: parcel(kind, y, tile, 0).wait_send())
    for up in (True, False):
        for far in (False, True):
            for chunk in range(2):
                hop(up, far, chunk).wait_send()


def whole(tile_count, patches, prior, blocks, row, want, flows, valid, stiffness, *fixed):
    count = blocks.shape[1]
    columns = flows.shape[3]
    rows = SPAN + 2 * FRONT
    dma = lambda number: pltpu.SemaphoreType.DMA((number,))
    vmem, anywhere = pl.BlockSpec(memory_space=pltpu.VMEM), pl.BlockSpec(memory_space=pl.ANY)
    f32, bf16, i32 = jnp.float32, jnp.bfloat16, jnp.int32
    images = pltpu.VMEM((BATCH * P_SIZE, LANES), f32)
    parcels = pltpu.VMEM((tile_count, CAP * WIRE, LANES), bf16)
    near = pltpu.VMEM((GZ, 8, columns), f32)
    patches_held = pltpu.VMEM((BATCH, WIRE, LANES), bf16)
    listed = 24
    return pl.pallas_call(
        functools.partial(whole_kernel, tile_count),
        out_shape=(
            jax.ShapeDtypeStruct((count, PIX), bf16),
            jax.ShapeDtypeStruct((2, 8, columns), f32),
        ),
        in_specs=[anywhere] * 3 + [vmem] * 9,
        out_specs=(anywhere, vmem),
        scratch_shapes=[
            pltpu.VMEM((BATCH, PIX), bf16),
            pltpu.VMEM((count, PIX), bf16),
            images,
            images,
            pltpu.VMEM((BATCH, WIRE, LANES), bf16),
            parcels,
            parcels,
            pltpu.VMEM((count, P_SIZE, 4 * LANES), bf16),
            pltpu.VMEM((CAP * tile_count, P_SIZE, 2 * LANES), f32),
            pltpu.VMEM((count, PIX), bf16),
            pltpu.VMEM((CAP * tile_count, LANES), f32),
            pltpu.VMEM((count, LANES), f32),
            pltpu.VMEM((2, 16, columns), bf16),
            pltpu.VMEM((GZ, 16, columns), bf16),
            pltpu.VMEM((2 * REACH + 1, GZ, 16, columns), bf16),
            patches_held,
            patches_held,
            patches_held,
            patches_held,
            pltpu.VMEM((8, LANES), i32),
            pltpu.VMEM((8 * listed, LANES), i32),
            pltpu.VMEM((listed, LANES), i32),
            pltpu.VMEM((8, LANES), i32),
            pltpu.SMEM((listed, LANES), i32),
            pltpu.SMEM((8, LANES), i32),
            pltpu.VMEM((8, columns), f32),
            near,
            pltpu.VMEM((GZ, columns), f32),
            pltpu.VMEM((2 * REACH + 1, GZ, columns), f32),
            pltpu.VMEM((2, LANES, LANES), f32),
            pltpu.VMEM((rows, 8, columns), f32),
            pltpu.VMEM((rows, 8, columns), f32),
            pltpu.VMEM((2, rows, 8, columns), f32),
            pltpu.VMEM((rows, 8, columns), f32),
            pltpu.VMEM((rows // 2, 16, columns), bf16),
            pltpu.VMEM((16, columns), bf16),
            near,
            near,
            dma(7),
        ]
        + [dma(SIDE * (2 * STEPS + 1))] * 2
        + [dma(GZ - 1)] * 2
        + [dma(2 * REACH)] * 2
        + [dma(8)] * 2
        + [dma(SIDE * len(KINDS))] * 2
        + [dma(GZ - 1)] * 2
        + [dma(2 * REACH)] * 2
        + [dma(8 * REACH)] * 2
        + [dma(GZ - 1)] * 2,
        compiler_params=pltpu.CompilerParams(
            collective_id=1, has_side_effects=True, vmem_limit_bytes=60 * 1024 * 1024
        ),
        cost_estimate=pl.CostEstimate(flops=30_000_000_000, bytes_accessed=32_000_000, transcendentals=0),
    )(patches, prior, blocks, row, want, flows, valid, stiffness, *fixed)


def on_device(patches, prior_patches, blocks, dest, target, flows, valid, stiffness):
    corr_maps, mesh_nodes = whole(
        lax.axis_size("tile"), patches, prior_patches, blocks, dest[:, :, 0], target, flows, valid, stiffness, *tables()
    )
    return (corr_maps[None], mesh_nodes[None])


def solution(mesh):
    return jax.shard_map(
        on_device,
        mesh=mesh,
        in_specs=(
            P("gz", "tile", None),
            P("tile", None),
            P("gz", "tile", None),
            P("gz", "tile", None),
            P("gz", "tile"),
            P("gz", None, "tile", None),
            P("gz", "tile", None),
            P("gz", "tile", None),
        ),
        out_specs=(P("gz", "tile", None), P("gz", None, "tile", None)),
        check_vma=False,
    )
```

```python
import functools

import jax
import jax.numpy as jnp
import ml_dtypes
import numpy as np
from jax import lax
from jax.experimental import pallas as pl
from jax.experimental.pallas import tpu as pltpu
from jax.sharding import PartitionSpec as P

P_SIZE = 160
PIX = 25600
CAP = 2
ITERS = 64
PHASE = ITERS // 2
UNROLL = 8


LANES = 128
HALF = 64
WIRE = 208
BATCH = 16


def tables():
    size = P_SIZE
    line = np.arange(size)
    angles = (np.outer(line, line) % size).astype(np.float32) * np.float32(2.0 * np.pi / size)
    rounded = lambda x: x.astype(ml_dtypes.bfloat16).astype(np.float32)
    cos_t, sin_t = rounded(np.cos(angles)), rounded(np.sin(angles))
    lane = np.arange(2 * LANES)
    column = HALF * (lane // LANES) + lane % HALF
    used = column <= size // 2
    column = np.where(used, column, 0)
    real = lane % LANES < HALF
    c, s = cos_t[:, column] * used, sin_t[:, column] * used
    first = np.zeros((2 * LANES, 4 * LANES), np.float32)
    first[:size, : 2 * LANES] = np.where(real, c, s)
    first[:size, 2 * LANES :] = np.where(real, -s, c)
    second = np.concatenate([cos_t, sin_t], axis=1)
    third = np.concatenate([cos_t, sin_t], axis=0)
    twice = np.where((column == 0) | (column == size // 2), 1.0, 2.0)
    fourth = np.zeros((4 * LANES, 2 * LANES), np.float32)
    fourth[: 2 * LANES, :size] = (np.where(real, c, -s) * twice).T
    fourth[2 * LANES :, :size] = (np.where(real, -s, -c) * twice).T
    return [jnp.asarray(x, jnp.bfloat16) for x in (first, second, third, fourth)]


def to_images(rows_ref, low_buf, high_buf):
    parts = PIX // 640
    chunk = lambda m: rows_ref[:, pl.ds(pl.multiple_of(640 * m, LANES), 640)].astype(jnp.float32)
    fold = lambda x: sum(x[:, LANES * k : LANES * k + LANES] for k in range(5))
    zero = jnp.zeros((BATCH, LANES), jnp.float32)
    sums = lax.fori_loop(0, parts, lambda m, t: t + fold(chunk(m)), zero)
    mean = jnp.sum(sums, axis=1, keepdims=True) * (1.0 / PIX)

    def square(m, t):
        x = chunk(m) - mean
        return t + fold(x * x)

    sums = lax.fori_loop(0, parts, square, zero)
    scale = lax.rsqrt(jnp.sum(sums, axis=1, keepdims=True) * (1.0 / PIX) + 1e-05)
    lane = lax.broadcasted_iota(jnp.int32, (BATCH, LANES), 1)

    def place(m, carry):
        x = (chunk(m) - mean) * scale
        t = [x[:, LANES * k : LANES * k + LANES] for k in range(5)]
        low = [
            t[0],
            pltpu.roll(jnp.where(lane < 32, t[2], t[1]), 96, 1),
            pltpu.roll(jnp.where(lane < 64, t[3], t[2]), 64, 1),
            pltpu.roll(jnp.where(lane < 96, t[4], t[3]), 32, 1),
        ]
        high = [t[1], pltpu.roll(t[2], 96, 1), pltpu.roll(t[3], 64, 1), pltpu.roll(t[4], 32, 1)]
        for k in range(4):
            at = pl.ds(4 * m + k, BATCH, stride=P_SIZE)
            low_buf[at, :] = low[k]
            high_buf[at, :] = high[k]
        return carry

    lax.fori_loop(0, parts, place, 0)


def image_spectrum(n, low_buf, high_buf, first_ref, second_ref):
    at = pl.ds(pl.multiple_of(P_SIZE * n, 8), P_SIZE)
    image = jnp.concatenate([low_buf[at, :], high_buf[at, :]], axis=1).astype(jnp.bfloat16)
    first = jnp.dot(image, first_ref[...], preferred_element_type=jnp.float32).astype(jnp.bfloat16)
    both = jnp.concatenate([first[:, : 2 * LANES], first[:, 2 * LANES :]], axis=0)
    return jnp.dot(second_ref[...], both, preferred_element_type=jnp.float32)


def block_batch(low_buf, high_buf, first_ref, second_ref, out_ref):
    low_half = lax.broadcasted_iota(jnp.int32, (P_SIZE, LANES), 1) < HALF

    def image(n, carry):
        spec = image_spectrum(n, low_buf, high_buf, first_ref, second_ref)
        for h in range(2):
            x = spec[:, LANES * h : LANES * h + LANES]
            swapped = pltpu.roll(x, HALF, 1)
            out_ref[n, :, LANES * h : LANES * h + LANES] = jnp.where(low_half, x, swapped).astype(jnp.bfloat16)
            at = slice(LANES * (2 + h), LANES * (3 + h))
            out_ref[n, :, at] = jnp.where(low_half, swapped, -x).astype(jnp.bfloat16)
        return carry

    lax.fori_loop(0, BATCH, image, 0, unroll=UNROLL)


def patch_batch(low_buf, high_buf, first_ref, second_ref, wire_buf):
    lane = lax.broadcasted_iota(jnp.int32, (8, LANES), 1) % HALF

    def image(n, carry):
        spec = image_spectrum(n, low_buf, high_buf, first_ref, second_ref)
        rest = [spec[8 * i : 8 * i + 8, LANES:] for i in range(20)]
        pieces = [spec[:, :LANES]]
        for i in range(5):
            pieces.append(sum(pltpu.roll(jnp.where(lane < 16, rest[5 * b + i], 0.0), 16 * b, 1) for b in range(4)))
        pieces.append(sum(pltpu.roll(jnp.where(lane == 16, rest[i], 0.0), (i + 112) % LANES, 1) for i in range(20)))
        wire_buf[n] = jnp.concatenate(pieces, axis=0).astype(jnp.bfloat16)
        return carry

    lax.fori_loop(0, BATCH, image, 0, unroll=UNROLL)


def match_one(wire, block_of, third_ref, fourth_ref):
    lane8 = lax.broadcasted_iota(jnp.int32, (8, LANES), 1) % HALF == 16
    last = wire[200:208]
    rest = []
    for i in range(20):
        part = wire[160 + 8 * (i % 5) : 168 + 8 * (i % 5)]
        part = pltpu.roll(part, (LANES - 16 * (i // 5)) % LANES, 1)
        rest.append(jnp.where(lane8, pltpu.roll(last, (16 - i) % LANES, 1), part))
    cross = []
    for h, a in enumerate((wire[:P_SIZE], jnp.concatenate(rest, axis=0))):
        straight, swapped = block_of(h).astype(jnp.float32), block_of(2 + h).astype(jnp.float32)
        cross.append((a * straight + pltpu.roll(a, HALF, 1) * swapped).astype(jnp.bfloat16))
    back = jnp.dot(third_ref[...], jnp.concatenate(cross, axis=1), preferred_element_type=jnp.float32)
    back = back.astype(jnp.bfloat16)
    back = jnp.concatenate([back[:P_SIZE], back[P_SIZE:]], axis=1)
    return jnp.dot(back, fourth_ref[...], preferred_element_type=jnp.float32) * (1.0 / float(P_SIZE) ** 3)


def to_rows(low_buf, high_buf, map_ref):
    lane = lax.broadcasted_iota(jnp.int32, (BATCH, LANES), 1)

    def place(m, carry):
        load = lambda buf, k: buf[pl.ds(4 * m + k, BATCH, stride=P_SIZE), :]
        low = [load(low_buf, 0)] + [pltpu.roll(load(low_buf, k), 32 * k, 1) for k in range(1, 4)]
        high = [load(high_buf, 0)] + [pltpu.roll(load(high_buf, k), 32 * k, 1) for k in range(1, 4)]
        tiles = [
            low[0],
            jnp.where(lane < 32, high[0], low[1]),
            jnp.where(lane < 32, low[1], jnp.where(lane < 64, high[1], low[2])),
            jnp.where(lane < 64, low[2], jnp.where(lane < 96, high[2], low[3])),
            jnp.where(lane < 96, low[3], high[3]),
        ]
        rows = jnp.concatenate(tiles, axis=1).astype(jnp.bfloat16)
        map_ref[:, pl.ds(pl.multiple_of(640 * m, LANES), 640)] = rows
        return carry

    lax.fori_loop(0, P_SIZE // 4, place, 0, unroll=2)


MESH = pl.DeviceIdType.MESH
GZ = 8
REACH = 4


def group_barrier(peers):
    barrier = pltpu.get_barrier_semaphore()
    for peer in peers:
        pl.semaphore_signal(barrier, inc=1, device_id=peer, device_id_type=MESH)
    pl.semaphore_wait(barrier, len(peers))


def gz_peers():
    gz, tile = lax.axis_index("gz"), lax.axis_index("tile")
    return [(lax.rem(gz + d, GZ), tile) for d in range(1, GZ)]


def tile_peers(tile_count):
    gz, tile = lax.axis_index("gz"), lax.axis_index("tile")
    offsets = [e for k in range(1, REACH + 1) for e in (k, -k)]
    return offsets, [(gz, lax.rem(tile + e + tile_count, tile_count)) for e in offsets]


def exchange_gz(source_of, held, send, recv):
    gz = lax.axis_index("gz")
    copies = []
    for d, peer in enumerate(gz_peers()):
        copies.append(
            pltpu.make_async_remote_copy(
                src_ref=source_of(peer[0]), dst_ref=held.at[gz], send_sem=send.at[d], recv_sem=recv.at[d],
                device_id=peer, device_id_type=MESH,
            )
        )
    for copy in copies:
        copy.start()
    return copies


def exchange_tiles(tile_count, source, window, send, recv):
    offsets, peers = tile_peers(tile_count)
    copies = []
    for n, (e, peer) in enumerate(zip(offsets, peers)):
        copies.append(
            pltpu.make_async_remote_copy(
                src_ref=source, dst_ref=window.at[REACH - e], send_sem=send.at[n], recv_sem=recv.at[n],
                device_id=peer, device_id_type=MESH,
            )
        )
    for copy in copies:
        copy.start()
    return copies


def request_rows(owner_row, wanted_row):
    count = owner_row.shape[1]
    grid = lambda axis: lax.broadcasted_iota(jnp.int32, (count, count), axis)
    column = lambda row: jnp.sum(jnp.where(grid(0) == grid(1), row, 0), axis=1, keepdims=True)
    owner_col = column(owner_row)
    same = owner_col == owner_row
    rank = jnp.sum(jnp.where((grid(0) < grid(1)) & same, 1, 0), axis=0, keepdims=True)
    rank_col = jnp.sum(jnp.where((grid(1) < grid(0)) & same, 1, 0), axis=1, keepdims=True)
    used = owner_col * CAP + rank_col == lax.broadcasted_iota(jnp.int32, (count, LANES), 1)
    total = lambda values: jnp.sum(jnp.where(used, values, 0), axis=0, keepdims=True)
    block = total(lax.broadcasted_iota(jnp.int32, (count, LANES), 0))
    return owner_row * CAP + rank, block, total(column(wanted_row))


SIDE = 4
STEPS = 3
KINDS = ((0, 0), (-1, 0), (1, 0), (-1, 1), (1, -1), (-1, 2), (1, -2), (-1, 3), (1, -3))


FRONT = 32
SPAN = 8 * (2 * REACH + 1)


def whole_kernel(
    tile_count, patch_ref, prior_ref, block_ref, row_ref, want_ref, flow_ref, valid_ref, stiff_ref, first_ref,
    second_ref, third_ref, fourth_ref, map_ref, mesh_ref, rows_buf, block_buf, low_buf, high_buf, wire_buf, send_buf,
    arrived_buf, spec_buf, field_buf, map_buf, slot_peak, peak_buf, own_buf, held, window_buf, near_up, near_down, ask_buf, heard_buf,
    list_buf, index_buf, told_smem, index_smem, conf_own, conf_held, conf_pack, conf_window, s_buf, w_buf, f_buf, u_buf,
    mid_buf, mid_wire, mid_own, spread_own, spread_held, local, send_r, recv_r, send_a, recv_a, send_b, recv_b, send_h, recv_h, send_p,
    recv_p, send_c, recv_c, send_d, recv_d, send_m, recv_m, send_s, recv_s,
):
    gz, tile = lax.axis_index("gz"), lax.axis_index("tile")
    component, part = lax.rem(gz, 2), gz // 2
    mid_wire[...] = jnp.zeros_like(mid_wire)
    after, before = lax.rem(gz + 1, GZ), lax.rem(gz + GZ - 1, GZ)
    barrier = pltpu.get_barrier_semaphore()

    def greet(peer):
        pl.semaphore_signal(barrier, inc=1, device_id=peer, device_id_type=MESH)

    plane, spot_in_plane = tile // SIDE, lax.rem(tile, SIDE)
    planes = tile_count // SIDE

    def tile_at(offset, y):
        return lax.rem(plane + offset + planes, planes) * SIDE + y

    def greet_planes(n, carry):
        peer = tile_at(n // SIDE - STEPS, lax.rem(n, SIDE))
        greet((after, peer))
        greet((before, peer))
        return carry

    asks = SIDE * (2 * STEPS + 1)
    heard_buf[8 * asks :, :] = jnp.zeros((heard_buf.shape[0] - 8 * asks, LANES), jnp.int32)
    lax.fori_loop(0, asks, greet_planes, 0)
    for d in range(2, GZ - 1):
        greet((lax.rem(gz + d, GZ), tile))
    for d in (0, 2, 4, 6):
        for e in range(1, REACH + 1):
            for sign in (e, tile_count - e):
                greet((lax.rem(gz + d, GZ), lax.rem(tile + sign, tile_count)))

    from_prior = pltpu.make_async_copy(prior_ref, rows_buf, local.at[0])
    from_patches = pltpu.make_async_copy(patch_ref.at[0], rows_buf, local.at[0])
    load_blocks = pltpu.make_async_copy(block_ref.at[0], block_buf, local.at[1])

    @pl.when(gz == GZ - 1)
    def _():
        from_prior.start()

    @pl.when(gz != GZ - 1)
    def _():
        from_patches.start()

    load_blocks.start()

    slot_row, block_row, asked_row = request_rows(row_ref[...], want_ref[...])
    count = slot_row.shape[1]
    index_buf[0:1, 0:count] = slot_row
    index_buf[1:2, :] = block_row
    index = pltpu.make_async_copy(index_buf, index_smem, local.at[6])
    index.start()
    ask_buf[...] = jnp.broadcast_to(asked_row, ask_buf.shape)
    columns = stiff_ref.shape[2]
    lane = lax.broadcasted_iota(jnp.int32, (columns, columns), 1)
    order = 2 * lax.rem(lane, columns // 2) + lane // (columns // 2)
    pick = jnp.where(lax.broadcasted_iota(jnp.int32, (columns, columns), 0) == order, 1.0, 0.0).astype(jnp.bfloat16)
    spring = stiff_ref[0] * valid_ref[0].astype(jnp.float32)
    for c in range(2):
        nodes = jnp.concatenate([spring, flow_ref[0, c]], axis=0).astype(jnp.bfloat16)
        own_buf[c] = jnp.dot(nodes, pick, preferred_element_type=jnp.float32).astype(jnp.bfloat16)

    @pl.when(gz == GZ - 1)
    def _():
        from_prior.wait()

    @pl.when(gz != GZ - 1)
    def _():
        from_patches.wait()

    to_images(rows_buf, low_buf, high_buf)

    pl.semaphore_wait(barrier, 2 * asks + GZ - 3 + 8 * REACH)

    springs = exchange_gz(lambda peer: own_buf.at[lax.rem(peer, 2)], held, send_a, recv_a)
    mine = pltpu.make_async_copy(own_buf.at[lax.rem(gz, 2)], held.at[gz], local.at[2])
    mine.start()

    def request(n, landing):
        peer = tile_at(n // SIDE - STEPS, lax.rem(n, SIDE))
        return pltpu.make_async_remote_copy(
            src_ref=ask_buf, dst_ref=heard_buf.at[pl.ds(pl.multiple_of(8 * landing, 8), 8)], send_sem=send_r.at[n],
            recv_sem=recv_r.at[landing], device_id=(before, peer), device_id_type=MESH,
        )

    def each(first, last, act):
        def body(d, carry):
            act(d)
            return carry

        lax.fori_loop(first, last, body, 0)

    each(0, asks, lambda n: request(n, n // SIDE * SIDE + spot_in_plane).start())

    mine.wait()
    for copy in springs:
        copy.wait()
    springs = exchange_tiles(tile_count, held, window_buf, send_b, recv_b)
    mine = pltpu.make_async_copy(held, window_buf.at[REACH], local.at[2])
    mine.start()
    each(0, asks, lambda n: request(n, n).wait())
    list_buf[...] = heard_buf[pl.ds(0, list_buf.shape[0], stride=8), :]
    told = pltpu.make_async_copy(list_buf, told_smem, local.at[3])
    told.start()
    patch_batch(low_buf, high_buf, first_ref, second_ref, wire_buf)
    told.wait()

    def hop(up):
        return pltpu.make_async_remote_copy(
            src_ref=wire_buf, dst_ref=near_up if up else near_down, send_sem=send_h.at[int(up)],
            recv_sem=recv_h.at[int(up)], device_id=(gz, tile_at(1 if up else -1, spot_in_plane)), device_id_type=MESH,
        )

    def parcel(kind, y_to, source, landing):
        if isinstance(kind, int) and kind >= 7:
            half = pl.ds(WIRE * (kind - 7), WIRE)
            outgoing, incoming = send_buf.at[28 + y_to, half], arrived_buf.at[source, half]
        else:
            outgoing, incoming = send_buf.at[SIDE * kind + y_to], arrived_buf.at[source]
        reach = KINDS[kind][1] if isinstance(kind, int) else 0
        return pltpu.make_async_remote_copy(
            src_ref=outgoing, dst_ref=incoming, send_sem=send_p.at[SIDE * kind + y_to],
            recv_sem=recv_p.at[SIDE * kind + landing], device_id=(after, tile_at(reach, y_to)), device_id_type=MESH,
        )

    def post(kind, held_patches):
        offset, reach = KINDS[kind]
        source = tile_at(offset, spot_in_plane)

        def one(y):
            listed = (STEPS - reach) * SIDE + y
            for c in range(CAP) if kind < 7 else (kind - 7,):
                entry, half = (SIDE * kind + y, c) if kind < 7 else (28 + y, c)
                patch = held_patches[told_smem[listed, CAP * source + c]]
                send_buf[entry, WIRE * half : WIRE * half + WIRE, :] = patch
            parcel(kind, y, source, spot_in_plane).start()

        each(0, SIDE, one)

    for up in (True, False):
        hop(up).start()
    post(0, wire_buf)
    for buf in (w_buf, f_buf, u_buf, mid_buf):
        buf[...] = jnp.zeros_like(buf)

    load_blocks.wait()
    for half in range(2):
        batch = pl.ds(BATCH * half, BATCH)
        to_images(block_buf.at[batch], low_buf, high_buf)
        block_batch(low_buf, high_buf, first_ref, second_ref, spec_buf.at[batch])
    for up in (True, False):
        hop(up).wait_recv()
    for kind in (1, 2, 3, 4, 5, 6, 7, 8):
        post(kind, near_up if kind % 2 else near_down)
    index.wait()
    mine.wait()
    for copy in springs:
        copy.wait()
    inner = lax.broadcasted_iota(jnp.int32, (P_SIZE, LANES), 1) < P_SIZE - LANES

    def match_slot(source, c):
        wire = arrived_buf[source, WIRE * c : WIRE * c + WIRE, :].astype(jnp.float32)
        block = index_smem[1, CAP * source + c]
        quarter = lambda q: spec_buf[block, :, LANES * q : LANES * q + LANES]
        field = match_one(wire, quarter, third_ref, fourth_ref)
        field_buf[CAP * source + c] = field
        top = jnp.maximum(field[:, :LANES], jnp.where(inner, field[:, LANES:], field[:, :LANES]))
        top = jnp.max(jnp.max(top, axis=0, keepdims=True), axis=1, keepdims=True)
        slot_peak[pl.ds(CAP * source + c, 1), :] = jnp.broadcast_to(top, (1, LANES))

    def match(n):
        kind = n // 2
        away = (kind + 1) // 2
        offset = jnp.where(lax.rem(kind, 2) == 1, -away, away)
        pairs = []
        for y in (2 * lax.rem(n, 2), 2 * lax.rem(n, 2) + 1):
            source = tile_at(offset, y)
            parcel(kind, y, source, y).wait_recv()
            pairs.append(source)
        for source in pairs:
            for c in range(CAP):
                match_slot(source, c)

    each(0, 14, match)

    def match_halfway(n):
        pairs = []
        for y in (2 * n, 2 * n + 1):
            source = tile_at(planes // 2, y)
            for kind in (7, 8):
                parcel(kind, y, source, y).wait_recv()
            pairs.append(source)
        for source in pairs:
            for c in range(CAP):
                match_slot(source, c)

    each(0, SIDE // 2, match_halfway)

    def store_maps(half):
        batch = pl.ds(BATCH * half, BATCH)

        def collect(n):
            field = field_buf[index_smem[0, BATCH * half + n]]
            at = pl.ds(pl.multiple_of(P_SIZE * n, 8), P_SIZE)
            low_buf[at, :] = field[:, :LANES]
            high_buf[at, :] = field[:, LANES:]

        each(0, BATCH, collect)
        to_rows(low_buf, high_buf, map_buf.at[batch])
        store = pltpu.make_async_copy(map_buf.at[batch], map_ref.at[batch], local.at[4 + half])
        store.start()
        return store

    for n in range(count):
        peak_buf[n : n + 1, :] = slot_peak[pl.ds(index_smem[0, n], 1), :]
    peak = peak_buf[...].astype(jnp.bfloat16).astype(jnp.float32)
    peak = jnp.concatenate([peak] * (columns // LANES), axis=1)
    block = lax.rem(lax.broadcasted_iota(jnp.int32, (count, columns), 1), columns // 2) // (columns // 2 // count)
    own = block == lax.broadcasted_iota(jnp.int32, (count, columns), 0)
    confidence = jnp.sum(jnp.where(own, peak / (1.0 + peak), 0.0), axis=0, keepdims=True)
    conf_own[...] = jnp.broadcast_to(confidence, conf_own.shape)
    copies = exchange_gz(lambda peer: conf_own, conf_held, send_c, recv_c)
    conf_held[gz] = conf_own[...]
    stores = [store_maps(0)]
    for copy in copies:
        copy.wait()
    for s in range(GZ):
        conf_pack[s : s + 1, :] = conf_held[s, 0:1, :]
    copies = exchange_tiles(tile_count, conf_pack, conf_window, send_d, recv_d)
    conf_window[REACH] = conf_pack[...]
    stores.append(store_maps(1))
    for copy in copies:
        copy.wait()

    first_slot = jnp.maximum(REACH - tile, 0)
    last_slot = jnp.minimum(REACH + tile_count - tile, 2 * REACH + 1)
    lane = lax.broadcasted_iota(jnp.int32, (1, 8, LANES), 2)
    first_lane, last_lane = lane == 0, lane == LANES - 1
    section = lax.broadcasted_iota(jnp.int32, (8, columns), 0)

    def picked(j):
        return jnp.concatenate([s_buf[h, pl.ds(j, 8, stride=16), :] for h in range(2)], axis=1)

    def prepare(k, carry):
        conf = jnp.where(section == 0, 0.0, 0.15 * conf_window[k])
        nodes = window_buf[k].astype(jnp.float32).reshape(LANES, columns)
        s_buf[0], s_buf[1] = nodes[:, :LANES], nodes[:, LANES:]
        for j in range(8):
            i = FRONT + 8 * k + j
            w = picked(j) * conf
            wf = w * picked(8 + j)
            w_buf[i] = w
            f_buf[i] = wf
            u_buf[0, i] = wf - pltpu.roll(wf, 7, 0)
        return carry

    lax.fori_loop(first_slot, last_slot, prepare, 0)

    def step(source, target, s):
        low = jnp.maximum((2 * part + s) // 8, first_slot)
        high = jnp.minimum((2 * part + 2 * PHASE + 2 - s + 7) // 8, last_slot)
        i = FRONT + 8 * low

        def advance(slots):
            rows = 8 * slots
            even, odd = [source[pl.ds(i - 1, rows + 2), :, LANES * h : LANES * h + LANES] for h in range(2)]
            to_left = jnp.where(first_lane, 0.0, pltpu.roll(odd[1:-1], 1, 2))
            to_right = jnp.where(last_lane, 0.0, pltpu.roll(even[1:-1], LANES - 1, 2))
            for h, (x, beside, other) in enumerate(((even, odd[1:-1], to_left), (odd, even[1:-1], to_right))):
                at = (pl.ds(i, rows), slice(None), slice(LANES * h, LANES * h + LANES))
                mid = x[1:-1]
                around = (x[:-2] + x[2:]) + (beside + other)
                force = w_buf[at] * (pltpu.roll(mid, 1, 1) - mid) + f_buf[at]
                target[at] = (0.4 * mid + 0.15 * around) + (force - pltpu.roll(force, 7, 1))

        for slots in range(1, 2 * REACH + 2):

            @pl.when(high - low == slots)
            def _():
                advance(slots)

    ping, pong = u_buf.at[0], u_buf.at[1]

    def run_step(s, carry):
        step(u_buf.at[lax.rem(s, 2)], u_buf.at[1 - lax.rem(s, 2)], s)
        return carry

    def rest_of_phase():
        lax.fori_loop(2, PHASE + 1, run_step, 0)

    base = FRONT + 8 * REACH + 2 * part
    rest_of_phase()

    place = 4 * tile + part
    places = 4 * tile_count

    def handover(n):
        e = jnp.where(n < 4 * REACH, n + 1, 4 * REACH - 1 - n)
        peer = lax.rem(place + e + places, places)
        row = FRONT + 8 * REACH + 2 * lax.rem(part + e + 4 * REACH, 4) - 2 * e
        copy = pltpu.make_async_remote_copy(
            src_ref=mid_own, dst_ref=mid_wire.at[row // 2], send_sem=send_m.at[n],
            recv_sem=recv_m.at[n], device_id=(2 * lax.rem(peer, 4) + component, peer // 4), device_id_type=MESH,
        )
        sends = (place + e >= 0) & (place + e < places)
        receives = (place - e >= 0) & (place - e < places)
        return copy, sends, receives

    def hand_out(n):
        copy, sends, _ = handover(n)

        @pl.when(sends)
        def _():
            copy.start()

    def take_in(n):
        copy, sends, receives = handover(n)

        @pl.when(sends)
        def _():
            copy.wait_send()

        @pl.when(receives)
        def _():
            copy.wait_recv()

    mid_own[...] = pong[pl.ds(base, 2)].reshape(mid_own.shape).astype(jnp.bfloat16)
    each(0, 8 * REACH, hand_out)
    each(0, 8 * REACH, take_in)

    def widen(p):
        mid_buf[pl.ds(2 * p, 2)] = mid_wire[p].astype(jnp.float32).reshape(2, 8, columns)

    each(FRONT // 2, (FRONT + SPAN) // 2, widen)
    mid_buf[pl.ds(base, 2)] = pong[pl.ds(base, 2)]
    step(mid_buf, ping, 1)
    rest_of_phase()

    for s in range(GZ):
        for r in range(2):
            spread_own[s, r : r + 1, :] = pong[base + r, s : s + 1, :]
    copies = exchange_gz(lambda peer: spread_own.at[peer], spread_held, send_s, recv_s)
    spread_held[gz] = spread_own[gz]
    order = lax.broadcasted_iota(jnp.int32, (columns, columns), 1)
    order = order // 2 + lax.rem(order, 2) * (columns // 2)
    spot = lax.broadcasted_iota(jnp.int32, (columns, columns), 0) == order
    pick = jnp.where(spot, 1.0, 0.0).astype(jnp.bfloat16)
    for copy in copies:
        copy.wait()
    rest = jnp.concatenate([spread_held[2 * h + c, 0:2, :] for c in range(2) for h in range(4)], axis=0)
    total = jnp.zeros_like(rest)
    for _ in range(3):
        piece = rest.astype(jnp.bfloat16)
        rest = rest - piece.astype(jnp.float32)
        total = total + jnp.dot(piece, pick, preferred_element_type=jnp.float32)
    mesh_ref[0] = total[:8]
    mesh_ref[1] = total[8:]
    for copy in stores:
        copy.wait()
    each(0, 7 * SIDE, lambda n: parcel(n // SIDE, lax.rem(n, SIDE), tile, 0).wait_send())
    for kind in (7, 8):
        each(0, SIDE, lambda y: parcel(kind, y, tile, 0).wait_send())
    for up in (True, False):
        hop(up).wait_send()


def whole(tile_count, patches, prior, blocks, row, want, flows, valid, stiffness, *fixed):
    count = blocks.shape[1]
    columns = flows.shape[3]
    rows = SPAN + 2 * FRONT
    dma = lambda number: pltpu.SemaphoreType.DMA((number,))
    vmem, anywhere = pl.BlockSpec(memory_space=pltpu.VMEM), pl.BlockSpec(memory_space=pl.ANY)
    f32, bf16, i32 = jnp.float32, jnp.bfloat16, jnp.int32
    images = pltpu.VMEM((BATCH * P_SIZE, LANES), f32)
    parcels = pltpu.VMEM((tile_count, CAP * WIRE, LANES), bf16)
    near = pltpu.VMEM((GZ, 8, columns), f32)
    patches_held = pltpu.VMEM((BATCH, WIRE, LANES), bf16)
    listed = 32
    return pl.pallas_call(
        functools.partial(whole_kernel, tile_count),
        out_shape=(
            jax.ShapeDtypeStruct((count, PIX), bf16),
            jax.ShapeDtypeStruct((2, 8, columns), f32),
        ),
        in_specs=[anywhere] * 3 + [vmem] * 9,
        out_specs=(anywhere, vmem),
        scratch_shapes=[
            pltpu.VMEM((BATCH, PIX), bf16),
            pltpu.VMEM((count, PIX), bf16),
            images,
            images,
            pltpu.VMEM((BATCH, WIRE, LANES), bf16),
            parcels,
            parcels,
            pltpu.VMEM((count, P_SIZE, 4 * LANES), bf16),
            pltpu.VMEM((CAP * tile_count, P_SIZE, 2 * LANES), f32),
            pltpu.VMEM((count, PIX), bf16),
            pltpu.VMEM((CAP * tile_count, LANES), f32),
            pltpu.VMEM((count, LANES), f32),
            pltpu.VMEM((2, 16, columns), bf16),
            pltpu.VMEM((GZ, 16, columns), bf16),
            pltpu.VMEM((2 * REACH + 1, GZ, 16, columns), bf16),
            patches_held,
            patches_held,
            pltpu.VMEM((8, LANES), i32),
            pltpu.VMEM((8 * listed, LANES), i32),
            pltpu.VMEM((listed, LANES), i32),
            pltpu.VMEM((8, LANES), i32),
            pltpu.SMEM((listed, LANES), i32),
            pltpu.SMEM((8, LANES), i32),
            pltpu.VMEM((8, columns), f32),
            near,
            pltpu.VMEM((GZ, columns), f32),
            pltpu.VMEM((2 * REACH + 1, GZ, columns), f32),
            pltpu.VMEM((2, LANES, LANES), f32),
            pltpu.VMEM((rows, 8, columns), f32),
            pltpu.VMEM((rows, 8, columns), f32),
            pltpu.VMEM((2, rows, 8, columns), f32),
            pltpu.VMEM((rows, 8, columns), f32),
            pltpu.VMEM((rows // 2, 16, columns), bf16),
            pltpu.VMEM((16, columns), bf16),
            near,
            near,
            dma(7),
        ]
        + [dma(SIDE * (2 * STEPS + 1))] * 2
        + [dma(GZ - 1)] * 2
        + [dma(2 * REACH)] * 2
        + [dma(2)] * 2
        + [dma(SIDE * len(KINDS))] * 2
        + [dma(GZ - 1)] * 2
        + [dma(2 * REACH)] * 2
        + [dma(8 * REACH)] * 2
        + [dma(GZ - 1)] * 2,
        compiler_params=pltpu.CompilerParams(
            collective_id=1, has_side_effects=True, vmem_limit_bytes=60 * 1024 * 1024
        ),
        cost_estimate=pl.CostEstimate(flops=30_000_000_000, bytes_accessed=32_000_000, transcendentals=0),
    )(patches, prior, blocks, row, want, flows, valid, stiffness, *fixed)


def on_device(patches, prior_patches, blocks, dest, target, flows, valid, stiffness):
    corr_maps, mesh_nodes = whole(
        lax.axis_size("tile"), patches, prior_patches, blocks, dest[:, :, 0], target, flows, valid, stiffness, *tables()
    )
    return (corr_maps[None], mesh_nodes[None])


def solution(mesh):
    return jax.shard_map(
        on_device,
        mesh=mesh,
        in_specs=(
            P("gz", "tile", None),
            P("tile", None),
            P("gz", "tile", None),
            P("gz", "tile", None),
            P("gz", "tile"),
            P("gz", None, "tile", None),
            P("gz", "tile", None),
            P("gz", "tile", None),
        ),
        out_specs=(P("gz", "tile", None), P("gz", None, "tile", None)),
        check_vma=False,
    )
```
